512 devices in a mesh: seq: 128 (over z, y, core), chan: 4 (over x).
Axes of the slice: x: 4, y: 8, z: 8, core: 2. Of those that a mesh axis runs over, the one named last changes fastest.
Arguments:
- tokens: bfloat16 [32768, 8192], P('seq', 'chan'), may hold values from -6 to 6
- in_weight: bfloat16 [8192, 3, 256], P('chan'), may hold values from -0.0625 to 0.0625
- short_weight: float32 [3, 3, 256], P(None, None, 'chan'), may hold values from -3 to 3
- residue: float32 [256, 16], P('chan'), may hold values from -2 to 2
- rates: float32 [256, 16], P('chan'), may hold values from 7.6293945e-06 to 0.05
- skip: float32 [256], P('chan'), may hold values from -4 to 4
Outputs:
- mixed: bfloat16 [32768, 256], P('seq', 'chan')
The draws below stay inside these ranges and needn't reach their ends.
All inputs are finite; a program needn't handle non-finite values.
Results may differ from the reference program's by a relative error of at most 0.005.
Values sent between devices are 32-bit elements; how exact they have to be, the bound alone decides.
No kernel may reach another device: no remote copies, remote signals or barrier semaphores. Data moves between devices by JAX's collectives and lax.ppermute only.
A program may use at most 64 MiB of HBM per device.

```python
import math
import jax
import jax.numpy as jnp
from jax import lax

D = 8192
CH = 256
TOKENS = 32768
POLES = 16


def steps_of(own_key, shape, cuts, low, top_value):
    loudness, own = 1.0, jax.random.fold_in(own_key, 6)
    for dim, parts in cuts:
        steps = jnp.exp(jax.random.uniform(jax.random.fold_in(own, dim), (parts,), jnp.float32, low / len(cuts), top_value / len(cuts)))
        loudness = loudness * jnp.repeat(steps, shape[dim] // parts).reshape([-1 if axis == dim else 1 for axis in range(len(shape))])
    return loudness


def noise(key, extent, spread, bound, cuts=(), kind=jnp.bfloat16):
    array = spread * jax.random.normal(key, extent, jnp.float32)
    if cuts:
        array = array * steps_of(key, extent, cuts, -0.22, 0.18)
    return jnp.clip(array, -bound, bound).astype(kind)


def setup_inputs(seed: int = 0) -> dict:
    key_of = jax.random.split(jax.random.key(seed), 7)
    tokens = noise(key_of[0], (TOKENS, D), 1.0, 6.0, ((0, 128), (1, 4)))
    in_weight = noise(key_of[1], (D, 3, CH), D ** -0.5, 0.0625, ((0, 4),))
    short_weight = noise(key_of[2], (3, 3, CH), 0.6, 3.0, ((2, 4),), jnp.float32)
    residue = noise(key_of[3], (CH, POLES), 0.35, 2.0, ((0, 4),), jnp.float32)
    rates = jnp.clip(jnp.exp(math.log(0.05) - 8.78777 * jax.random.uniform(key_of[4], (CH, POLES), jnp.float32) ** steps_of(key_of[4], (CH, POLES), ((0, 4),), -0.2, 0.2)), 7.62939453125e-06, 0.05)
    skip = noise(key_of[5], (CH,), 1.0, 4.0, ((0, 4),), jnp.float32)
    return dict(tokens=tokens, in_weight=in_weight, short_weight=short_weight, residue=residue, rates=rates, skip=skip)


def reference(tokens, in_weight, short_weight, residue, rates, skip):
    projected = jnp.einsum('td,djc->tjc', tokens.astype(jnp.float32), in_weight.astype(jnp.float32), precision=lax.Precision.HIGHEST)
    padded = jnp.concatenate([jnp.zeros((2, 3, CH), jnp.float32), projected], axis=0)
    features = short_weight[0] * projected + short_weight[1] * padded[1:-1] + short_weight[2] * padded[:-2]
    queries = features[:, 0, :]
    mixed_in = features[:, 1, :] * features[:, 2, :]
    positions = jnp.arange(TOKENS).astype(jnp.float32)
    impulse = jnp.zeros((TOKENS, CH), jnp.float32)
    for pole in range(POLES):
        weight_pole = residue[:, pole] * jnp.sqrt(2.0 * rates[:, pole])
        impulse = impulse + weight_pole[None, :] * jnp.exp(-rates[:, pole][None, :] * positions[:, None])
    length_fft = 2 * TOKENS
    spectrum = jnp.fft.rfft(mixed_in, n=length_fft, axis=0) * jnp.fft.rfft(impulse, n=length_fft, axis=0)
    convolved = jnp.fft.irfft(spectrum, n=length_fft, axis=0)[:TOKENS]
    return (queries * (convolved + skip[None, :] * mixed_in)).astype(jnp.bfloat16)
```

```python
import functools

import jax
import jax.numpy as jnp
from jax import lax
from jax.experimental import pallas as pl
from jax.experimental.pallas import tpu as pltpu
from jax.sharding import Mesh, PartitionSpec as P

NEAR = 16
STEP = 8
F32 = jnp.float32


def lanes_of(shape):
    return lax.broadcasted_iota(jnp.int32, shape, 1)


def rows_of(shape):
    return lax.broadcasted_iota(jnp.int32, shape, 0)


def swap(tile):
    return pltpu.roll(tile, tile.shape[1] // 2, 1)


def twice(row):
    return jnp.concatenate([row, row], axis=1)


def folded(poles):
    half = poles.shape[0] // 2
    return jnp.concatenate([poles[:half], poles[half:]], axis=1)


def project_kernel(tok_ref, w_ref, out_ref):
    acc = jnp.dot(tok_ref[...], w_ref[0], preferred_element_type=F32)
    rows = acc.shape[0] // 2
    for pair in range(acc.shape[1] // 128):
        early = acc[:rows, 128 * pair : 128 * (pair + 1)]
        late = acc[rows:, 128 * pair : 128 * (pair + 1)]
        left = lanes_of(early.shape) < 64
        out_ref[2 * pair, 0] = jnp.where(left, early, swap(late))
        out_ref[2 * pair + 1, 0] = jnp.where(left, swap(early), late)


def project(tokens, weight):
    rows, depth = tokens.shape
    streams, _, width = weight.shape
    chan = width // 64
    return pl.pallas_call(
        project_kernel,
        grid=(streams,),
        in_specs=[
            pl.BlockSpec((rows, depth), lambda s: (0, 0)),
            pl.BlockSpec((1, depth, width), lambda s: (s, 0, 0)),
        ],
        out_specs=pl.BlockSpec((chan, 1, rows // 2, 128), lambda s: (0, s, 0, 0)),
        out_shape=jax.ShapeDtypeStruct((chan, streams, rows // 2, 128), F32),
        compiler_params=pltpu.CompilerParams(vmem_limit_bytes=32 * 2**20),
        name="project",
    )(tokens, weight)


def local_kernel(part_ref, short_ref, residue_ref, rates_ref, send_ref, q_ref, x_ref, y_ref, half_ref, own_ref):
    count = part_ref.shape[0]
    rows, width = q_ref.shape
    lane = lanes_of((1, width))
    right = lane >= width // 2
    row = rows_of((rows, width))
    feats, edges = [], []
    for s in range(3):
        p = part_ref[0, s]
        for i in range(1, count):
            p = p + part_ref[i, s]
        tap = [twice(short_ref[k, s : s + 1, :]) for k in range(3)]
        before = jnp.where(right, swap(p[rows - 8 :]), 0.0)
        one = jnp.where(row < 1, before[7:8], pltpu.roll(p, 1, 0))
        two = pltpu.roll(p, 2, 0)
        two = jnp.where(row == 0, before[6:7], jnp.where(row == 1, before[7:8], two))
        feats.append(tap[0] * p + tap[1] * one + tap[2] * two)
        edges.append((tap[1] * p[rows - 1 :] + tap[2] * p[rows - 2 : rows - 1], tap[2] * p[rows - 1 :]))
    q, a, b = feats
    q_ref[...] = q
    x = jnp.where(jnp.logical_and(row < 2, jnp.logical_not(right)), 0.0, a * b)
    x_ref[...] = x
    tile = [
        jnp.where(right, swap(b[0:1]), a[0:1]),
        jnp.where(right, swap(b[1:2]), a[1:2]),
        jnp.where(right, edges[2][0], swap(edges[1][0])),
        jnp.where(right, edges[2][1], swap(edges[1][1])),
        jnp.where(right, edges[0][1], swap(edges[0][0])),
    ]
    own = jnp.concatenate(tile + [jnp.zeros((3, width), F32)], axis=0)
    own_ref[...] = own

    rates = twice(rates_ref[...])
    weight = twice(residue_ref[...]) * jnp.sqrt(2.0 * rates)
    poles = rates.shape[0]
    inner = rows_of((STEP, width))
    step_pos = inner.astype(F32)
    impulse = [jnp.sum(weight * jnp.exp(-rates * float(u)), axis=0, keepdims=True) for u in range(STEP)]
    near = [jnp.where(inner >= u, impulse[u], 0.0) for u in range(STEP)]
    decay = jnp.exp(-float(STEP) * rates)
    into, outof, fade = [], [], []
    for r in range(poles):
        rate = rates[r : r + 1]
        into.append(jnp.exp(-rate * (STEP - 1.0 - step_pos)))
        outof.append(weight[r : r + 1] * jnp.exp(-rate * (step_pos + 1.0)))
        fade.append(decay[r : r + 1])
    state = [None] * poles
    for k in range(rows // STEP):
        xk = x[k * STEP : (k + 1) * STEP]
        yk = near[0] * xk
        for u in range(1, STEP):
            yk = yk + near[u] * pltpu.roll(xk, u, 0)
        for r in range(poles):
            gain = jnp.sum(into[r] * xk, axis=0, keepdims=True)
            if k > 0:
                yk = yk + outof[r] * state[r]
                gain = gain + fade[r] * state[r]
            state[r] = gain
        y_ref[k * STEP : (k + 1) * STEP, :] = yk
    half = jnp.concatenate(state, axis=0)
    half_ref[...] = half
    total = half + jnp.exp(-float(rows) * rates) * swap(half)
    h = poles // 2
    packed = jnp.where(right, total[h:], swap(total[:h]))
    for i in range(send_ref.shape[0]):
        send_ref[i, 0:8, :] = packed
        send_ref[i, 8:16, :] = own


def local(parts, short_weight, residue, rates):
    _, _, rows, width = parts.shape
    tile = jax.ShapeDtypeStruct((rows, width), F32)
    return pl.pallas_call(
        local_kernel,
        out_shape=(
            jax.ShapeDtypeStruct((NEAR, 16, width), F32),
            tile,
            tile,
            tile,
            jax.ShapeDtypeStruct((rates.shape[0], width), F32),
            jax.ShapeDtypeStruct((8, width), F32),
        ),
        compiler_params=pltpu.CompilerParams(vmem_limit_bytes=32 * 2**20),
        name="local",
    )(parts, short_weight, residue, rates)


def gate_of(tile, before):
    a = tile[0:2]
    if before is not None:
        a = a + before[2:4]
    return a * swap(a)


def near_kernel(shard_rows, place_ref, got_ref, rates_ref, send_ref, prefix_ref, before_ref):
    near = place_ref[0]
    rates = folded(rates_ref[...])
    fade = jnp.exp(-float(shard_rows) * rates)
    first = jnp.exp(-(shard_rows - 1.0) * rates)
    second = jnp.exp(-(shard_rows - 2.0) * rates)
    total = got_ref[0, 0:8, :]
    prefix = jnp.where(near > 0, total, 0.0)
    before = jnp.zeros_like(total)
    for i in range(1, NEAR):
        edge = got_ref[i - 1, 8:16, :]
        gate = gate_of(got_ref[i, 8:16, :], edge)
        grown = total * fade + (got_ref[i, 0:8, :] + first * gate[0:1] + second * gate[1:2])
        before = jnp.where(near == i, edge, before)
        total = grown
        prefix = jnp.where(near > i, grown, prefix)
    prefix_ref[...] = prefix
    before_ref[...] = before
    head = got_ref[0, 8:16, :]
    tail = got_ref[NEAR - 1, 8:16, :]
    ends = jnp.where(rows_of(head.shape) < 2, head, tail)
    for i in range(send_ref.shape[0]):
        send_ref[i, 0:8, :] = total
        send_ref[i, 8:16, :] = ends


def near_sums(place, got, rates, shard_rows, far_count):
    width = got.shape[2]
    tile = jax.ShapeDtypeStruct((8, width), F32)
    vmem = pl.BlockSpec(memory_space=pltpu.VMEM)
    return pl.pallas_call(
        functools.partial(near_kernel, shard_rows),
        in_specs=[pl.BlockSpec(memory_space=pltpu.SMEM), vmem, vmem],
        out_shape=(jax.ShapeDtypeStruct((far_count, 16, width), F32), tile, tile),
        name="near_sums",
    )(place, got, rates)


def finish_kernel(
    shard_rows, place_ref, got_ref, prefix_ref, before_ref, own_ref, half_ref, q_ref, x_ref, y_ref,
    residue_ref, rates_ref, skip_ref, out_ref,
):
    near, far = place_ref[0], place_ref[1]
    rows, width = q_ref.shape
    rates = folded(rates_ref[...])
    first = jnp.exp(-(shard_rows - 1.0) * rates)
    second = jnp.exp(-(shard_rows - 2.0) * rates)
    last = jnp.exp(-float((NEAR - 1) * shard_rows) * rates)
    row_fade = jnp.exp(-float(NEAR * shard_rows) * rates)
    before = before_ref[...]
    carry = jnp.zeros_like(rates)
    opening = jnp.zeros_like(rates)
    edge = None
    for z in range(got_ref.shape[0]):
        gate = gate_of(got_ref[z, 8:16, :], edge)
        start = first * gate[0:1] + second * gate[1:2]
        opening = jnp.where(far == z, start, opening)
        if edge is not None:
            before = jnp.where(jnp.logical_and(near == 0, far == z), edge, before)
        grown = carry * row_fade + (got_ref[z, 0:8, :] + last * start)
        carry = jnp.where(far > z, grown, carry)
        edge = got_ref[z, 8:16, :]
    place = near.astype(F32) * float(shard_rows)
    state = prefix_ref[...] + jnp.exp(-place * rates) * carry
    beyond = jnp.exp(-jnp.maximum(place - shard_rows, 0.0) * rates) * opening
    state = state + jnp.where(near > 0, beyond, 0.0)
    gate = gate_of(own_ref[...], before)
    state = state + jnp.exp(rates) * gate[0:1] + jnp.exp(2.0 * rates) * gate[1:2]

    rates = twice(rates_ref[...])
    weight = twice(residue_ref[...]) * jnp.sqrt(2.0 * rates)
    poles = rates.shape[0]
    left = lanes_of((1, width)) < width // 2
    other = swap(state)
    whole = jnp.concatenate([jnp.where(left, state, other), jnp.where(left, other, state)], axis=0)
    whole = jnp.where(left, whole, swap(half_ref[...]) + jnp.exp(-float(rows) * rates) * whole)
    skip = twice(skip_ref[...])
    step_pos = rows_of((STEP, width)).astype(F32)
    decay = jnp.exp(-float(STEP) * rates)
    states, outof, fade = [], [], []
    for r in range(poles):
        states.append(jnp.broadcast_to(whole[r : r + 1], (STEP, width)))
        outof.append(weight[r : r + 1] * jnp.exp(-rates[r : r + 1] * (step_pos + 1.0)))
        fade.append(jnp.broadcast_to(decay[r : r + 1], (STEP, width)))
    states = [s * o for s, o in zip(states, outof)]
    for k in range(rows // STEP):
        at = slice(k * STEP, (k + 1) * STEP)
        xk, qk, yk = x_ref[at, :], q_ref[at, :], y_ref[at, :]
        if k == 0:
            inner = rows_of((STEP, width))
            ahead = jnp.sum(weight * jnp.exp(rates), axis=0, keepdims=True)
            top = jnp.logical_and(left, inner == 0)
            next_ = jnp.logical_and(left, inner == 1)
            xk = jnp.where(top, gate[0:1], jnp.where(next_, gate[1:2], xk))
            yk = yk - jnp.where(top, ahead * gate[1:2], 0.0)
            q_edge = before[4:5]
            qk = qk + jnp.where(top, q_edge, jnp.where(next_, swap(q_edge), 0.0))
        for r in range(poles):
            yk = yk + states[r]
            states[r] = states[r] * fade[r]
        mixed = qk * (yk + skip * xk)
        out_ref[at, :] = mixed[:, : width // 2].astype(out_ref.dtype)
        out_ref[rows + k * STEP : rows + (k + 1) * STEP, :] = mixed[:, width // 2 :].astype(out_ref.dtype)


def finish(shard_rows, place, got, prefix, before, own, half, q, x, y, residue, rates, skip):
    rows, width = q.shape
    vmem = pl.BlockSpec(memory_space=pltpu.VMEM)
    return pl.pallas_call(
        functools.partial(finish_kernel, shard_rows),
        in_specs=[pl.BlockSpec(memory_space=pltpu.SMEM)] + [vmem] * 11,
        out_shape=jax.ShapeDtypeStruct((2 * rows, width // 2), jnp.bfloat16),
        name="finish",
    )(place, got, prefix, before, own, half, q, x, y, residue, rates, skip)


def per_device(tokens, in_weight, short_weight, residue, rates, skip):
    shard_rows = tokens.shape[0]
    place = jnp.stack([lax.axis_index("near"), lax.axis_index("far")]).astype(jnp.int32)
    residue, rates = residue.T, rates.T
    partials = project(tokens, in_weight.transpose(1, 0, 2))
    parts = lax.all_to_all(partials, "chan", 0, 0, tiled=True)
    send, q, x, y, half, own = local(parts, short_weight, residue, rates)
    got = lax.all_to_all(send, "near", 0, 0, tiled=True)
    send, prefix, before = near_sums(place, got, rates, shard_rows, lax.axis_size("far"))
    got = lax.all_to_all(send, "far", 0, 0, tiled=True)
    return finish(shard_rows, place, got, prefix, before, own, half, q, x, y, residue, rates, skip[None, :])


def solution(mesh):
    seq, chan = mesh.devices.shape
    mesh = Mesh(mesh.devices.reshape(seq // NEAR, NEAR, chan), ("far", "near", "chan"))
    whole = ("far", "near")
    in_specs = (
        P(whole, "chan"),
        P("chan", None, None),
        P(None, None, "chan"),
        P("chan", None),
        P("chan", None),
        P("chan"),
    )
    return jax.shard_map(
        per_device, mesh=mesh, in_specs=in_specs, out_specs=P(whole, "chan"), check_vma=False
    )
```

```python
import functools

import jax
import jax.numpy as jnp
from jax import lax
from jax.experimental import pallas as pl
from jax.experimental.pallas import tpu as pltpu
from jax.sharding import Mesh, PartitionSpec as P

NEAR = 16
STEP = 8
F32 = jnp.float32
HBM = pl.BlockSpec(memory_space=pl.ANY)
VMEM = pl.BlockSpec(memory_space=pltpu.VMEM)
ROOMY = pltpu.CompilerParams(vmem_limit_bytes=56 * 2**20)


def lanes_of(shape):
    return lax.broadcasted_iota(jnp.int32, shape, 1)


def rows_of(shape):
    return lax.broadcasted_iota(jnp.int32, shape, 0)


def swap(tile):
    return pltpu.roll(tile, tile.shape[1] // 2, 1)


def twice(row):
    return jnp.concatenate([row, row], axis=1)


def folded(poles):
    half = poles.shape[0] // 2
    return jnp.concatenate([poles[:half], poles[half:]], axis=1)


def project_kernel(tok_hbm, w_hbm, out_ref, tok_ref, w_ref, tok_sem, w_sem):
    streams = w_ref.shape[0]
    tok_copy = pltpu.make_async_copy(tok_hbm, tok_ref, tok_sem)
    tok_copy.start()
    w_copies = [pltpu.make_async_copy(w_hbm.at[s], w_ref.at[s], w_sem.at[s]) for s in range(streams)]
    for copy in w_copies:
        copy.start()
    tok_copy.wait()
    for s in range(streams):
        w_copies[s].wait()
        acc = jnp.dot(tok_ref[...], w_ref[s], preferred_element_type=F32)
        rows = acc.shape[0] // 2
        for pair in range(acc.shape[1] // 128):
            early = acc[:rows, 128 * pair : 128 * (pair + 1)]
            late = acc[rows:, 128 * pair : 128 * (pair + 1)]
            left = lanes_of(early.shape) < 64
            out_ref[2 * pair, s] = jnp.where(left, early, swap(late))
            out_ref[2 * pair + 1, s] = jnp.where(left, swap(early), late)


def project(tokens, weight):
    rows, depth = tokens.shape
    streams, _, width = weight.shape
    chan = width // 64
    return pl.pallas_call(
        project_kernel,
        in_specs=[HBM, HBM],
        out_shape=jax.ShapeDtypeStruct((chan, streams, rows // 2, 128), F32),
        scratch_shapes=[
            pltpu.VMEM(tokens.shape, tokens.dtype),
            pltpu.VMEM(weight.shape, weight.dtype),
            pltpu.SemaphoreType.DMA(()),
            pltpu.SemaphoreType.DMA((streams,)),
        ],
        compiler_params=ROOMY,
        name="project",
    )(tokens, weight)


def local_kernel(part_ref, short_ref, residue_ref, rates_ref, send_ref, keep_ref):
    count = part_ref.shape[0]
    rows, width = part_ref.shape[2:]
    right = lanes_of((1, width)) >= width // 2
    row = rows_of((rows, width))
    feats, edges = [], []
    for s in range(3):
        p = part_ref[0, s]
        for i in range(1, count):
            p = p + part_ref[i, s]
        tap = [twice(short_ref[k, s : s + 1, :]) for k in range(3)]
        before = jnp.where(right, swap(p[rows - 8 :]), 0.0)
        one = jnp.where(row < 1, before[7:8], pltpu.roll(p, 1, 0))
        two = pltpu.roll(p, 2, 0)
        two = jnp.where(row == 0, before[6:7], jnp.where(row == 1, before[7:8], two))
        feats.append(tap[0] * p + tap[1] * one + tap[2] * two)
        edges.append((tap[1] * p[rows - 1 :] + tap[2] * p[rows - 2 : rows - 1], tap[2] * p[rows - 1 :]))
    q, a, b = feats
    keep_ref[0:rows, :] = q
    x = jnp.where(jnp.logical_and(row < 2, jnp.logical_not(right)), 0.0, a * b)
    keep_ref[rows : 2 * rows, :] = x
    tile = [
        jnp.where(right, swap(b[0:1]), a[0:1]),
        jnp.where(right, swap(b[1:2]), a[1:2]),
        jnp.where(right, edges[2][0], swap(edges[1][0])),
        jnp.where(right, edges[2][1], swap(edges[1][1])),
        jnp.where(right, edges[0][1], swap(edges[0][0])),
    ]
    own = jnp.concatenate(tile + [jnp.zeros((3, width), F32)], axis=0)
    keep_ref[3 * rows : 3 * rows + 8, :] = own

    rates = twice(rates_ref[...])
    weight = twice(residue_ref[...]) * jnp.sqrt(2.0 * rates)
    poles = rates.shape[0]
    inner = rows_of((STEP, width))
    step_pos = inner.astype(F32)
    impulse = [jnp.sum(weight * jnp.exp(-rates * float(u)), axis=0, keepdims=True) for u in range(STEP)]
    near = [jnp.where(inner >= u, impulse[u], 0.0) for u in range(STEP)]
    decay = jnp.exp(-float(STEP) * rates)
    into, outof, fade = [], [], []
    for r in range(poles):
        rate = rates[r : r + 1]
        into.append(jnp.exp(-rate * (STEP - 1.0 - step_pos)))
        outof.append(weight[r : r + 1] * jnp.exp(-rate * (step_pos + 1.0)))
        fade.append(decay[r : r + 1])
    state = [None] * poles
    for k in range(rows // STEP):
        xk = x[k * STEP : (k + 1) * STEP]
        yk = near[0] * xk
        for u in range(1, STEP):
            yk = yk + near[u] * pltpu.roll(xk, u, 0)
        for r in range(poles):
            gain = jnp.sum(into[r] * xk, axis=0, keepdims=True)
            if k > 0:
                yk = yk + outof[r] * state[r]
                gain = gain + fade[r] * state[r]
            state[r] = gain
        keep_ref[2 * rows + k * STEP : 2 * rows + (k + 1) * STEP, :] = yk
    half = jnp.concatenate(state, axis=0)
    keep_ref[3 * rows + 8 :, :] = half
    total = half + jnp.exp(-float(rows) * rates) * swap(half)
    h = poles // 2
    packed = jnp.where(right, total[h:], swap(total[:h]))
    for i in range(send_ref.shape[0]):
        send_ref[i, 0:8, :] = packed
        send_ref[i, 8:16, :] = own


def local(parts, short_weight, residue, rates):
    _, _, rows, width = parts.shape
    return pl.pallas_call(
        local_kernel,
        out_shape=(
            jax.ShapeDtypeStruct((NEAR, 16, width), F32),
            jax.ShapeDtypeStruct((3 * rows + 8 + rates.shape[0], width), F32),
        ),
        compiler_params=ROOMY,
        name="local",
    )(parts, short_weight, residue, rates)


def gate_of(tile, before):
    a = tile[0:2]
    if before is not None:
        a = a + before[2:4]
    return a * swap(a)


def near_kernel(shard_rows, got_hbm, rates_ref, send_ref, keep_ref, got_ref, sem):
    copy = pltpu.make_async_copy(got_hbm, got_ref, sem)
    copy.start()
    near = lax.axis_index("near")
    rates = folded(rates_ref[...])
    fade = jnp.exp(-float(shard_rows) * rates)
    first = jnp.exp(-(shard_rows - 1.0) * rates)
    second = jnp.exp(-(shard_rows - 2.0) * rates)
    copy.wait()
    total = got_ref[0, 0:8, :]
    prefix = jnp.where(near > 0, total, 0.0)
    before = jnp.zeros_like(total)
    for i in range(1, NEAR):
        edge = got_ref[i - 1, 8:16, :]
        gate = gate_of(got_ref[i, 8:16, :], edge)
        grown = total * fade + (got_ref[i, 0:8, :] + first * gate[0:1] + second * gate[1:2])
        before = jnp.where(near == i, edge, before)
        total = grown
        prefix = jnp.where(near > i, grown, prefix)
    keep_ref[0:8, :] = prefix
    keep_ref[8:16, :] = before
    head = got_ref[0, 8:16, :]
    tail = got_ref[NEAR - 1, 8:16, :]
    ends = jnp.where(rows_of(head.shape) < 2, head, tail)
    for i in range(send_ref.shape[0]):
        send_ref[i, 0:8, :] = total
        send_ref[i, 8:16, :] = ends


def near_sums(got, rates, shard_rows, far_count):
    width = got.shape[2]
    return pl.pallas_call(
        functools.partial(near_kernel, shard_rows),
        in_specs=[HBM, VMEM],
        out_shape=(jax.ShapeDtypeStruct((far_count, 16, width), F32), jax.ShapeDtypeStruct((16, width), F32)),
        scratch_shapes=[pltpu.VMEM(got.shape, F32), pltpu.SemaphoreType.DMA(())],
        compiler_params=ROOMY,
        name="near_sums",
    )(got, rates)


def finish_kernel(
    shard_rows, got_hbm, near_hbm, keep_hbm, residue_ref, rates_ref, skip_ref, out_ref, got_ref, near_ref, keep_ref, sems
):
    copies = [
        pltpu.make_async_copy(source, target, sems.at[i])
        for i, (source, target) in enumerate([(got_hbm, got_ref), (near_hbm, near_ref), (keep_hbm, keep_ref)])
    ]
    for copy in copies:
        copy.start()
    near, far = lax.axis_index("near"), lax.axis_index("far")
    rows, width = out_ref.shape[1] // 2, keep_ref.shape[1]
    rates = twice(rates_ref[...])
    weight = twice(residue_ref[...]) * jnp.sqrt(2.0 * rates)
    poles = rates.shape[0]
    skip = twice(skip_ref[...])
    step_pos = rows_of((STEP, width)).astype(F32)
    decay = jnp.exp(-float(STEP) * rates)
    half_decay = jnp.exp(-float(rows) * rates)
    ahead = jnp.sum(weight * jnp.exp(rates), axis=0, keepdims=True)
    outof, fade = [], []
    for r in range(poles):
        outof.append(weight[r : r + 1] * jnp.exp(-rates[r : r + 1] * (step_pos + 1.0)))
        fade.append(jnp.broadcast_to(decay[r : r + 1], (STEP, width)))

    rates = folded(rates_ref[...])
    first = jnp.exp(-(shard_rows - 1.0) * rates)
    second = jnp.exp(-(shard_rows - 2.0) * rates)
    last = jnp.exp(-float((NEAR - 1) * shard_rows) * rates)
    row_fade = jnp.exp(-float(NEAR * shard_rows) * rates)
    place = near.astype(F32) * float(shard_rows)
    place_fade = jnp.exp(-place * rates)
    beyond_fade = jnp.where(near > 0, jnp.exp(-jnp.maximum(place - shard_rows, 0.0) * rates), 0.0)
    ahead_one, ahead_two = jnp.exp(rates), jnp.exp(2.0 * rates)
    for copy in copies:
        copy.wait()
    before = near_ref[8:16, :]
    carry = jnp.zeros_like(rates)
    opening = jnp.zeros_like(rates)
    edge = None
    for z in range(got_ref.shape[0]):
        gate = gate_of(got_ref[z, 8:16, :], edge)
        start = first * gate[0:1] + second * gate[1:2]
        opening = jnp.where(far == z, start, opening)
        if edge is not None:
            before = jnp.where(jnp.logical_and(near == 0, far == z), edge, before)
        grown = carry * row_fade + (got_ref[z, 0:8, :] + last * start)
        carry = jnp.where(far > z, grown, carry)
        edge = got_ref[z, 8:16, :]
    state = near_ref[0:8, :] + place_fade * carry + beyond_fade * opening
    gate = gate_of(keep_ref[3 * rows : 3 * rows + 8, :], before)
    state = state + ahead_one * gate[0:1] + ahead_two * gate[1:2]

    left = lanes_of((1, width)) < width // 2
    other = swap(state)
    whole = jnp.concatenate([jnp.where(left, state, other), jnp.where(left, other, state)], axis=0)
    whole = jnp.where(left, whole, swap(keep_ref[3 * rows + 8 :, :]) + half_decay * whole)
    states = [jnp.broadcast_to(whole[r : r + 1], (STEP, width)) * outof[r] for r in range(poles)]
    steps = []
    for k in range(rows // STEP):
        at = k * STEP
        qk = keep_ref[at : at + STEP, :]
        xk = keep_ref[rows + at : rows + at + STEP, :]
        yk = keep_ref[2 * rows + at : 2 * rows + at + STEP, :]
        if k == 0:
            inner = rows_of((STEP, width))
            top = jnp.logical_and(left, inner == 0)
            next_ = jnp.logical_and(left, inner == 1)
            xk = jnp.where(top, gate[0:1], jnp.where(next_, gate[1:2], xk))
            yk = yk - jnp.where(top, ahead * gate[1:2], 0.0)
            q_edge = before[4:5]
            qk = qk + jnp.where(top, q_edge, jnp.where(next_, swap(q_edge), 0.0))
        for r in range(poles):
            yk = yk + states[r]
            states[r] = states[r] * fade[r]
        steps.append(qk * (yk + skip * xk))
    mixed = jnp.concatenate(steps, axis=0).T
    out_ref[:, :rows] = mixed[: width // 2].astype(out_ref.dtype)
    out_ref[:, rows:] = mixed[width // 2 :].astype(out_ref.dtype)


def finish(shard_rows, got, near, keep, residue, rates, skip):
    width = keep.shape[1]
    return pl.pallas_call(
        functools.partial(finish_kernel, shard_rows),
        in_specs=[HBM] * 3 + [VMEM] * 3,
        out_shape=jax.ShapeDtypeStruct((width // 2, shard_rows), jnp.bfloat16),
        scratch_shapes=[pltpu.VMEM(a.shape, F32) for a in (got, near, keep)] + [pltpu.SemaphoreType.DMA((3,))],
        compiler_params=ROOMY,
        name="finish",
    )(got, near, keep, residue, rates, skip)


def per_device(tokens, in_weight, short_weight, residue, rates, skip):
    shard_rows = tokens.shape[0]
    residue, rates = residue.T, rates.T
    partials = project(tokens, in_weight.transpose(1, 0, 2))
    parts = lax.all_to_all(partials, "chan", 0, 0, tiled=True)
    send, keep = local(parts, short_weight, residue, rates)
    got = lax.all_to_all(send, "near", 0, 0, tiled=True)
    send, near = near_sums(got, rates, shard_rows, lax.axis_size("far"))
    got = lax.all_to_all(send, "far", 0, 0, tiled=True)
    return finish(shard_rows, got, near, keep, residue, rates, skip[None, :]).T


def solution(mesh):
    seq, chan = mesh.devices.shape
    mesh = Mesh(mesh.devices.reshape(seq // NEAR, NEAR, chan), ("far", "near", "chan"))
    whole = ("far", "near")
    in_specs = (
        P(whole, "chan"),
        P("chan", None, None),
        P(None, None, "chan"),
        P("chan", None),
        P("chan", None),
        P("chan"),
    )
    return jax.shard_map(
        per_device, mesh=mesh, in_specs=in_specs, out_specs=P(whole, "chan"), check_vma=False
    )
```

```python
import functools

import jax
import jax.numpy as jnp
from jax import lax
from jax.experimental import pallas as pl
from jax.experimental.pallas import tpu as pltpu
from jax.sharding import Mesh, PartitionSpec as P

NEAR = 16
STEP = 8
F32 = jnp.float32
HBM = pl.BlockSpec(memory_space=pl.ANY)
ROOMY = pltpu.CompilerParams(vmem_limit_bytes=24 * 2**20)


def in_vmem(array):
    return pltpu.with_memory_space_constraint(array, pltpu.VMEM)


def in_hbm(array):
    return pltpu.with_memory_space_constraint(array, pltpu.HBM)


def lanes_of(shape):
    return lax.broadcasted_iota(jnp.int32, shape, 1)


def rows_of(shape):
    return lax.broadcasted_iota(jnp.int32, shape, 0)


def swap(tile):
    return pltpu.roll(tile, tile.shape[1] // 2, 1)


def twice(row):
    return jnp.concatenate([row, row], axis=1)


def folded(poles):
    half = poles.shape[0] // 2
    return jnp.concatenate([poles[:half], poles[half:]], axis=1)


def project_kernel(tok_hbm, w_hbm, out_ref, tok_ref, w_ref, acc_ref, tok_sems, w_sems):
    streams, depth, _ = w_ref.shape
    pieces = tok_sems.shape[0]
    deep = depth // pieces
    parts = [pl.ds(i * deep, deep) for i in range(pieces)]
    tok_copies = [
        pltpu.make_async_copy(tok_hbm.at[:, part], tok_ref.at[:, part], tok_sems.at[i]) for i, part in enumerate(parts)
    ]
    w_copies = [
        [pltpu.make_async_copy(w_hbm.at[s, part], w_ref.at[s, part], w_sems.at[s, i]) for i, part in enumerate(parts)]
        for s in range(streams)
    ]
    for i in range(pieces):
        tok_copies[i].start()
        w_copies[0][i].start()
    for s in range(1, streams):
        for copy in w_copies[s]:
            copy.start()
    for s in range(streams):
        for i, part in enumerate(parts):
            if s == 0:
                tok_copies[i].wait()
            w_copies[s][i].wait()
            term = jnp.dot(tok_ref[:, part], w_ref[s, part, :], preferred_element_type=F32)
            acc_ref[...] = term if i == 0 else acc_ref[...] + term
        rows = acc_ref.shape[0] // 2
        for pair in range(acc_ref.shape[1] // 128):
            early = acc_ref[:rows, 128 * pair : 128 * (pair + 1)]
            late = acc_ref[rows:, 128 * pair : 128 * (pair + 1)]
            left = lanes_of(early.shape) < 64
            out_ref[2 * pair, s] = jnp.where(left, early, swap(late))
            out_ref[2 * pair + 1, s] = jnp.where(left, swap(early), late)


def project(tokens, weight):
    rows, depth = tokens.shape
    streams, _, width = weight.shape
    chan = width // 64
    pieces = 4
    return pl.pallas_call(
        project_kernel,
        in_specs=[HBM, HBM],
        out_shape=pltpu.VMEM((chan, streams, rows // 2, 128), F32),
        scratch_shapes=[
            pltpu.VMEM(tokens.shape, tokens.dtype),
            pltpu.VMEM(weight.shape, weight.dtype),
            pltpu.VMEM((rows, width), F32),
            pltpu.SemaphoreType.DMA((pieces,)),
            pltpu.SemaphoreType.DMA((streams, pieces)),
        ],
        compiler_params=ROOMY,
        name="project",
    )(in_hbm(tokens), in_hbm(weight))


def local_kernel(part_ref, short_ref, residue_ref, rates_ref, send_ref, keep_ref):
    count = part_ref.shape[0]
    rows, width = part_ref.shape[2:]
    right = lanes_of((1, width)) >= width // 2
    row = rows_of((rows, width))
    feats, edges = [], []
    for s in range(3):
        p = part_ref[0, s]
        for i in range(1, count):
            p = p + part_ref[i, s]
        tap = [twice(short_ref[k, s : s + 1, :]) for k in range(3)]
        before = jnp.where(right, swap(p[rows - 8 :]), 0.0)
        one = jnp.where(row < 1, before[7:8], pltpu.roll(p, 1, 0))
        two = pltpu.roll(p, 2, 0)
        two = jnp.where(row == 0, before[6:7], jnp.where(row == 1, before[7:8], two))
        feats.append(tap[0] * p + tap[1] * one + tap[2] * two)
        edges.append((tap[1] * p[rows - 1 :] + tap[2] * p[rows - 2 : rows - 1], tap[2] * p[rows - 1 :]))
    q, a, b = feats
    keep_ref[0:rows, :] = q
    x = jnp.where(jnp.logical_and(row < 2, jnp.logical_not(right)), 0.0, a * b)
    keep_ref[rows : 2 * rows, :] = x
    tile = [
        jnp.where(right, swap(b[0:1]), a[0:1]),
        jnp.where(right, swap(b[1:2]), a[1:2]),
        jnp.where(right, edges[2][0], swap(edges[1][0])),
        jnp.where(right, edges[2][1], swap(edges[1][1])),
        jnp.where(right, edges[0][1], swap(edges[0][0])),
    ]
    own = jnp.concatenate(tile + [jnp.zeros((3, width), F32)], axis=0)
    keep_ref[3 * rows : 3 * rows + 8, :] = own

    rates = twice(rates_ref[...])
    weight = twice(residue_ref[...]) * jnp.sqrt(2.0 * rates)
    poles = rates.shape[0]
    inner = rows_of((STEP, width))
    step_pos = inner.astype(F32)
    impulse = [jnp.sum(weight * jnp.exp(-rates * float(u)), axis=0, keepdims=True) for u in range(STEP)]
    near = [jnp.where(inner >= u, impulse[u], 0.0) for u in range(STEP)]
    decay = jnp.exp(-float(STEP) * rates)
    into, outof, fade = [], [], []
    for r in range(poles):
        rate = rates[r : r + 1]
        into.append(jnp.exp(-rate * (STEP - 1.0 - step_pos)))
        outof.append(weight[r : r + 1] * jnp.exp(-rate * (step_pos + 1.0)))
        fade.append(decay[r : r + 1])
    state = [None] * poles
    for k in range(rows // STEP):
        xk = x[k * STEP : (k + 1) * STEP]
        yk = near[0] * xk
        for u in range(1, STEP):
            yk = yk + near[u] * pltpu.roll(xk, u, 0)
        for r in range(poles):
            gain = jnp.sum(into[r] * xk, axis=0, keepdims=True)
            if k > 0:
                yk = yk + outof[r] * state[r]
                gain = gain + fade[r] * state[r]
            state[r] = gain
        keep_ref[2 * rows + k * STEP : 2 * rows + (k + 1) * STEP, :] = yk
    half = jnp.concatenate(state, axis=0)
    keep_ref[3 * rows + 8 :, :] = half
    total = half + jnp.exp(-float(rows) * rates) * swap(half)
    h = poles // 2
    packed = jnp.where(right, total[h:], swap(total[:h]))
    for i in range(send_ref.shape[0]):
        send_ref[i, 0:8, :] = packed
        send_ref[i, 8:16, :] = own


def local(parts, short_weight, residue, rates):
    _, _, rows, width = parts.shape
    return pl.pallas_call(
        local_kernel,
        out_shape=(
            pltpu.VMEM((NEAR, 16, width), F32),
            pltpu.VMEM((3 * rows + 8 + rates.shape[0], width), F32),
        ),
        compiler_params=ROOMY,
        name="local",
    )(in_vmem(parts), short_weight, residue, rates)


def gate_of(tile, before):
    a = tile[0:2]
    if before is not None:
        a = a + before[2:4]
    return a * swap(a)


def near_kernel(shard_rows, got_ref, rates_ref, send_ref, keep_ref):
    near = lax.axis_index("near")
    rates = folded(rates_ref[...])
    fade = jnp.exp(-float(shard_rows) * rates)
    first = jnp.exp(-(shard_rows - 1.0) * rates)
    second = jnp.exp(-(shard_rows - 2.0) * rates)
    total = got_ref[0, 0:8, :]
    prefix = jnp.where(near > 0, total, 0.0)
    before = jnp.zeros_like(total)
    for i in range(1, NEAR):
        edge = got_ref[i - 1, 8:16, :]
        gate = gate_of(got_ref[i, 8:16, :], edge)
        grown = total * fade + (got_ref[i, 0:8, :] + first * gate[0:1] + second * gate[1:2])
        before = jnp.where(near == i, edge, before)
        total = grown
        prefix = jnp.where(near > i, grown, prefix)
    keep_ref[0:8, :] = prefix
    keep_ref[8:16, :] = before
    head = got_ref[0, 8:16, :]
    tail = got_ref[NEAR - 1, 8:16, :]
    ends = jnp.where(rows_of(head.shape) < 2, head, tail)
    for i in range(send_ref.shape[0]):
        send_ref[i, 0:8, :] = total
        send_ref[i, 8:16, :] = ends


def near_sums(got, rates, shard_rows, far_count):
    width = got.shape[2]
    return pl.pallas_call(
        functools.partial(near_kernel, shard_rows),
        out_shape=(pltpu.VMEM((far_count, 16, width), F32), pltpu.VMEM((16, width), F32)),
        name="near_sums",
    )(in_vmem(got), rates)


def finish_kernel(shard_rows, got_ref, near_ref, keep_ref, residue_ref, rates_ref, skip_ref, out_ref):
    near, far = lax.axis_index("near"), lax.axis_index("far")
    rows, width = out_ref.shape[1] // 2, keep_ref.shape[1]
    rates = twice(rates_ref[...])
    weight = twice(residue_ref[...]) * jnp.sqrt(2.0 * rates)
    poles = rates.shape[0]
    skip = twice(skip_ref[...])
    step_pos = rows_of((STEP, width)).astype(F32)
    decay = jnp.exp(-float(STEP) * rates)
    half_decay = jnp.exp(-float(rows) * rates)
    ahead = jnp.sum(weight * jnp.exp(rates), axis=0, keepdims=True)
    outof, fade = [], []
    for r in range(poles):
        outof.append(weight[r : r + 1] * jnp.exp(-rates[r : r + 1] * (step_pos + 1.0)))
        fade.append(jnp.broadcast_to(decay[r : r + 1], (STEP, width)))

    rates = folded(rates_ref[...])
    first = jnp.exp(-(shard_rows - 1.0) * rates)
    second = jnp.exp(-(shard_rows - 2.0) * rates)
    last = jnp.exp(-float((NEAR - 1) * shard_rows) * rates)
    row_fade = jnp.exp(-float(NEAR * shard_rows) * rates)
    place = near.astype(F32) * float(shard_rows)
    place_fade = jnp.exp(-place * rates)
    beyond_fade = jnp.where(near > 0, jnp.exp(-jnp.maximum(place - shard_rows, 0.0) * rates), 0.0)
    ahead_one, ahead_two = jnp.exp(rates), jnp.exp(2.0 * rates)
    before = near_ref[8:16, :]
    carry = jnp.zeros_like(rates)
    opening = jnp.zeros_like(rates)
    edge = None
    for z in range(got_ref.shape[0]):
        gate = gate_of(got_ref[z, 8:16, :], edge)
        start = first * gate[0:1] + second * gate[1:2]
        opening = jnp.where(far == z, start, opening)
        if edge is not None:
            before = jnp.where(jnp.logical_and(near == 0, far == z), edge, before)
        grown = carry * row_fade + (got_ref[z, 0:8, :] + last * start)
        carry = jnp.where(far > z, grown, carry)
        edge = got_ref[z, 8:16, :]
    state = near_ref[0:8, :] + place_fade * carry + beyond_fade * opening
    gate = gate_of(keep_ref[3 * rows : 3 * rows + 8, :], before)
    state = state + ahead_one * gate[0:1] + ahead_two * gate[1:2]

    left = lanes_of((1, width)) < width // 2
    other = swap(state)
    whole = jnp.concatenate([jnp.where(left, state, other), jnp.where(left, other, state)], axis=0)
    whole = jnp.where(left, whole, swap(keep_ref[3 * rows + 8 :, :]) + half_decay * whole)
    states = [jnp.broadcast_to(whole[r : r + 1], (STEP, width)) * outof[r] for r in range(poles)]
    steps = []
    for k in range(rows // STEP):
        at = k * STEP
        qk = keep_ref[at : at + STEP, :]
        xk = keep_ref[rows + at : rows + at + STEP, :]
        yk = keep_ref[2 * rows + at : 2 * rows + at + STEP, :]
        if k == 0:
            inner = rows_of((STEP, width))
            top = jnp.logical_and(left, inner == 0)
            next_ = jnp.logical_and(left, inner == 1)
            xk = jnp.where(top, gate[0:1], jnp.where(next_, gate[1:2], xk))
            yk = yk - jnp.where(top, ahead * gate[1:2], 0.0)
            q_edge = before[4:5]
            qk = qk + jnp.where(top, q_edge, jnp.where(next_, swap(q_edge), 0.0))
        for r in range(poles):
            yk = yk + states[r]
            states[r] = states[r] * fade[r]
        steps.append(qk * (yk + skip * xk))
    mixed = jnp.concatenate(steps, axis=0).T
    out_ref[:, :rows] = mixed[: width // 2].astype(out_ref.dtype)
    out_ref[:, rows:] = mixed[width // 2 :].astype(out_ref.dtype)


def finish(shard_rows, got, near, keep, residue, rates, skip):
    width = keep.shape[1]
    return pl.pallas_call(
        functools.partial(finish_kernel, shard_rows),
        out_shape=jax.ShapeDtypeStruct((width // 2, shard_rows), jnp.bfloat16),
        name="finish",
    )(in_vmem(got), in_vmem(near), in_vmem(keep), residue, rates, skip)


def per_device(tokens, in_weight, short_weight, residue, rates, skip):
    shard_rows = tokens.shape[0]
    residue, rates = residue.T, rates.T
    partials = project(tokens, in_weight.transpose(1, 0, 2))
    parts = lax.all_to_all(partials, "chan", 0, 0, tiled=True)
    send, keep = local(parts, short_weight, residue, rates)
    got = lax.all_to_all(send, "near", 0, 0, tiled=True)
    send, near = near_sums(got, rates, shard_rows, lax.axis_size("far"))
    got = lax.all_to_all(send, "far", 0, 0, tiled=True)
    return finish(shard_rows, got, near, keep, residue, rates, skip[None, :]).T


def solution(mesh):
    seq, chan = mesh.devices.shape
    mesh = Mesh(mesh.devices.reshape(seq // NEAR, NEAR, chan), ("far", "near", "chan"))
    whole = ("far", "near")
    in_specs = (
        P(whole, "chan"),
        P("chan", None, None),
        P(None, None, "chan"),
        P("chan", None),
        P("chan", None),
        P("chan"),
    )
    return jax.shard_map(
        per_device, mesh=mesh, in_specs=in_specs, out_specs=P(whole, "chan"), check_vma=False
    )
```

```python
import functools

import jax
import jax.numpy as jnp
from jax import lax
from jax.experimental import pallas as pl
from jax.experimental.pallas import tpu as pltpu
from jax.sharding import Mesh, PartitionSpec as P

NEAR = 16
STEP = 8
F32 = jnp.float32
HBM = pl.BlockSpec(memory_space=pl.ANY)
ROOMY = pltpu.CompilerParams(vmem_limit_bytes=24 * 2**20)


def in_vmem(array):
    return pltpu.with_memory_space_constraint(array, pltpu.VMEM)


def in_hbm(array):
    return pltpu.with_memory_space_constraint(array, pltpu.HBM)


def lanes_of(shape):
    return lax.broadcasted_iota(jnp.int32, shape, 1)


def rows_of(shape):
    return lax.broadcasted_iota(jnp.int32, shape, 0)


def swap(tile):
    return pltpu.roll(tile, tile.shape[1] // 2, 1)


def twice(row):
    return jnp.concatenate([row, row], axis=1)


def folded(poles):
    half = poles.shape[0] // 2
    return jnp.concatenate([poles[:half], poles[half:]], axis=1)


def project_kernel(tok_hbm, w_hbm, out_ref, tok_ref, w_ref, acc_ref, tok_sems, w_sems):
    streams, depth, _ = w_ref.shape
    pieces = tok_sems.shape[0]
    deep = depth // pieces
    parts = [pl.ds(i * deep, deep) for i in range(pieces)]
    copies = []
    for i, part in enumerate(parts):
        copies.append([pltpu.make_async_copy(tok_hbm.at[:, part], tok_ref.at[:, part], tok_sems.at[i])])
        for s in range(streams):
            copies[i].append(pltpu.make_async_copy(w_hbm.at[s, part], w_ref.at[s, part], w_sems.at[s, i]))
    for piece in copies:
        for copy in piece:
            copy.start()
    for i, part in enumerate(parts):
        for copy in copies[i]:
            copy.wait()
        for s in range(streams):
            term = jnp.dot(tok_ref[:, part], w_ref[s, part, :], preferred_element_type=F32)
            acc_ref[s] = term if i == 0 else acc_ref[s] + term
    rows = acc_ref.shape[1] // 2
    for s in range(streams):
        for pair in range(acc_ref.shape[2] // 128):
            early = acc_ref[s, :rows, 128 * pair : 128 * (pair + 1)]
            late = acc_ref[s, rows:, 128 * pair : 128 * (pair + 1)]
            left = lanes_of(early.shape) < 64
            out_ref[2 * pair, s] = jnp.where(left, early, swap(late))
            out_ref[2 * pair + 1, s] = jnp.where(left, swap(early), late)


def project(tokens, weight):
    rows, depth = tokens.shape
    streams, _, width = weight.shape
    chan = width // 64
    pieces = 4
    return pl.pallas_call(
        project_kernel,
        in_specs=[HBM, HBM],
        out_shape=pltpu.VMEM((chan, streams, rows // 2, 128), F32),
        scratch_shapes=[
            pltpu.VMEM(tokens.shape, tokens.dtype),
            pltpu.VMEM(weight.shape, weight.dtype),
            pltpu.VMEM((streams, rows, width), F32),
            pltpu.SemaphoreType.DMA((pieces,)),
            pltpu.SemaphoreType.DMA((streams, pieces)),
        ],
        compiler_params=ROOMY,
        name="project",
    )(in_hbm(tokens), in_hbm(weight))


def local_kernel(part_ref, short_ref, residue_ref, rates_ref, send_ref, keep_ref):
    count = part_ref.shape[0]
    rows, width = part_ref.shape[2:]
    right = lanes_of((1, width)) >= width // 2
    row = rows_of((rows, width))
    feats, edges = [], []
    for s in range(3):
        p = part_ref[0, s]
        for i in range(1, count):
            p = p + part_ref[i, s]
        tap = [twice(short_ref[k, s : s + 1, :]) for k in range(3)]
        before = jnp.where(right, swap(p[rows - 8 :]), 0.0)
        one = jnp.where(row < 1, before[7:8], pltpu.roll(p, 1, 0))
        two = pltpu.roll(p, 2, 0)
        two = jnp.where(row == 0, before[6:7], jnp.where(row == 1, before[7:8], two))
        feats.append(tap[0] * p + tap[1] * one + tap[2] * two)
        edges.append((tap[1] * p[rows - 1 :] + tap[2] * p[rows - 2 : rows - 1], tap[2] * p[rows - 1 :]))
    q, a, b = feats
    keep_ref[0:rows, :] = q
    x = jnp.where(jnp.logical_and(row < 2, jnp.logical_not(right)), 0.0, a * b)
    keep_ref[rows : 2 * rows, :] = x
    tile = [
        jnp.where(right, swap(b[0:1]), a[0:1]),
        jnp.where(right, swap(b[1:2]), a[1:2]),
        jnp.where(right, edges[2][0], swap(edges[1][0])),
        jnp.where(right, edges[2][1], swap(edges[1][1])),
        jnp.where(right, edges[0][1], swap(edges[0][0])),
    ]
    own = jnp.concatenate(tile + [jnp.zeros((3, width), F32)], axis=0)
    keep_ref[3 * rows : 3 * rows + 8, :] = own

    rates = twice(rates_ref[...])
    weight = twice(residue_ref[...]) * jnp.sqrt(2.0 * rates)
    poles = rates.shape[0]
    inner = rows_of((STEP, width))
    step_pos = inner.astype(F32)
    impulse = [jnp.sum(weight * jnp.exp(-rates * float(u)), axis=0, keepdims=True) for u in range(STEP)]
    near = [jnp.where(inner >= u, impulse[u], 0.0) for u in range(STEP)]
    decay = jnp.exp(-float(STEP) * rates)
    into, outof, fade = [], [], []
    for r in range(poles):
        rate = rates[r : r + 1]
        into.append(jnp.exp(-rate * (STEP - 1.0 - step_pos)))
        outof.append(weight[r : r + 1] * jnp.exp(-rate * (step_pos + 1.0)))
        fade.append(decay[r : r + 1])
    state = [None] * poles
    for k in range(rows // STEP):
        xk = x[k * STEP : (k + 1) * STEP]
        yk = near[0] * xk
        for u in range(1, STEP):
            yk = yk + near[u] * pltpu.roll(xk, u, 0)
        for r in range(poles):
            gain = jnp.sum(into[r] * xk, axis=0, keepdims=True)
            if k > 0:
                yk = yk + outof[r] * state[r]
                gain = gain + fade[r] * state[r]
            state[r] = gain
        keep_ref[2 * rows + k * STEP : 2 * rows + (k + 1) * STEP, :] = yk
    half = jnp.concatenate(state, axis=0)
    keep_ref[3 * rows + 8 :, :] = half
    total = half + jnp.exp(-float(rows) * rates) * swap(half)
    h = poles // 2
    packed = jnp.where(right, total[h:], swap(total[:h]))
    for i in range(send_ref.shape[0]):
        send_ref[i, 0:8, :] = packed
        send_ref[i, 8:16, :] = own


def local(parts, short_weight, residue, rates):
    _, _, rows, width = parts.shape
    return pl.pallas_call(
        local_kernel,
        out_shape=(
            pltpu.VMEM((NEAR, 16, width), F32),
            pltpu.VMEM((3 * rows + 8 + rates.shape[0], width), F32),
        ),
        compiler_params=ROOMY,
        name="local",
    )(in_vmem(parts), short_weight, residue, rates)


def gate_of(tile, before):
    a = tile[0:2]
    if before is not None:
        a = a + before[2:4]
    return a * swap(a)


def near_kernel(shard_rows, got_ref, rates_ref, send_ref, keep_ref):
    near = lax.axis_index("near")
    rates = folded(rates_ref[...])
    fade = jnp.exp(-float(shard_rows) * rates)
    first = jnp.exp(-(shard_rows - 1.0) * rates)
    second = jnp.exp(-(shard_rows - 2.0) * rates)
    total = got_ref[0, 0:8, :]
    prefix = jnp.where(near > 0, total, 0.0)
    before = jnp.zeros_like(total)
    for i in range(1, NEAR):
        edge = got_ref[i - 1, 8:16, :]
        gate = gate_of(got_ref[i, 8:16, :], edge)
        grown = total * fade + (got_ref[i, 0:8, :] + first * gate[0:1] + second * gate[1:2])
        before = jnp.where(near == i, edge, before)
        total = grown
        prefix = jnp.where(near > i, grown, prefix)
    keep_ref[0:8, :] = prefix
    keep_ref[8:16, :] = before
    head = got_ref[0, 8:16, :]
    tail = got_ref[NEAR - 1, 8:16, :]
    ends = jnp.where(rows_of(head.shape) < 2, head, tail)
    for i in range(send_ref.shape[0]):
        send_ref[i, 0:8, :] = total
        send_ref[i, 8:16, :] = ends


def near_sums(got, rates, shard_rows, far_count):
    width = got.shape[2]
    return pl.pallas_call(
        functools.partial(near_kernel, shard_rows),
        out_shape=(pltpu.VMEM((far_count, 16, width), F32), pltpu.VMEM((16, width), F32)),
        name="near_sums",
    )(in_vmem(got), rates)


def finish_kernel(shard_rows, got_ref, near_ref, keep_ref, residue_ref, rates_ref, skip_ref, out_ref):
    near, far = lax.axis_index("near"), lax.axis_index("far")
    rows, width = out_ref.shape[1] // 2, keep_ref.shape[1]
    rates = twice(rates_ref[...])
    weight = twice(residue_ref[...]) * jnp.sqrt(2.0 * rates)
    poles = rates.shape[0]
    skip = twice(skip_ref[...])
    step_pos = rows_of((STEP, width)).astype(F32)
    decay = jnp.exp(-float(STEP) * rates)
    half_decay = jnp.exp(-float(rows) * rates)
    ahead = jnp.sum(weight * jnp.exp(rates), axis=0, keepdims=True)
    outof, fade = [], []
    for r in range(poles):
        outof.append(weight[r : r + 1] * jnp.exp(-rates[r : r + 1] * (step_pos + 1.0)))
        fade.append(jnp.broadcast_to(decay[r : r + 1], (STEP, width)))

    rates = folded(rates_ref[...])
    first = jnp.exp(-(shard_rows - 1.0) * rates)
    second = jnp.exp(-(shard_rows - 2.0) * rates)
    last = jnp.exp(-float((NEAR - 1) * shard_rows) * rates)
    row_fade = jnp.exp(-float(NEAR * shard_rows) * rates)
    place = near.astype(F32) * float(shard_rows)
    place_fade = jnp.exp(-place * rates)
    beyond_fade = jnp.where(near > 0, jnp.exp(-jnp.maximum(place - shard_rows, 0.0) * rates), 0.0)
    ahead_one, ahead_two = jnp.exp(rates), jnp.exp(2.0 * rates)
    before = near_ref[8:16, :]
    carry = jnp.zeros_like(rates)
    opening = jnp.zeros_like(rates)
    edge = None
    for z in range(got_ref.shape[0]):
        gate = gate_of(got_ref[z, 8:16, :], edge)
        start = first * gate[0:1] + second * gate[1:2]
        opening = jnp.where(far == z, start, opening)
        if edge is not None:
            before = jnp.where(jnp.logical_and(near == 0, far == z), edge, before)
        grown = carry * row_fade + (got_ref[z, 0:8, :] + last * start)
        carry = jnp.where(far > z, grown, carry)
        edge = got_ref[z, 8:16, :]
    state = near_ref[0:8, :] + place_fade * carry + beyond_fade * opening
    gate = gate_of(keep_ref[3 * rows : 3 * rows + 8, :], before)
    state = state + ahead_one * gate[0:1] + ahead_two * gate[1:2]

    left = lanes_of((1, width)) < width // 2
    other = swap(state)
    whole = jnp.concatenate([jnp.where(left, state, other), jnp.where(left, other, state)], axis=0)
    whole = jnp.where(left, whole, swap(keep_ref[3 * rows + 8 :, :]) + half_decay * whole)
    states = [jnp.broadcast_to(whole[r : r + 1], (STEP, width)) * outof[r] for r in range(poles)]
    steps = []
    for k in range(rows // STEP):
        at = k * STEP
        qk = keep_ref[at : at + STEP, :]
        xk = keep_ref[rows + at : rows + at + STEP, :]
        yk = keep_ref[2 * rows + at : 2 * rows + at + STEP, :]
        if k == 0:
            inner = rows_of((STEP, width))
            top = jnp.logical_and(left, inner == 0)
            next_ = jnp.logical_and(left, inner == 1)
            xk = jnp.where(top, gate[0:1], jnp.where(next_, gate[1:2], xk))
            yk = yk - jnp.where(top, ahead * gate[1:2], 0.0)
            q_edge = before[4:5]
            qk = qk + jnp.where(top, q_edge, jnp.where(next_, swap(q_edge), 0.0))
        for r in range(poles):
            yk = yk + states[r]
            states[r] = states[r] * fade[r]
        steps.append(qk * (yk + skip * xk))
    mixed = jnp.concatenate(steps, axis=0).T
    out_ref[:, :rows] = mixed[: width // 2].astype(out_ref.dtype)
    out_ref[:, rows:] = mixed[width // 2 :].astype(out_ref.dtype)


def finish(shard_rows, got, near, keep, residue, rates, skip):
    width = keep.shape[1]
    return pl.pallas_call(
        functools.partial(finish_kernel, shard_rows),
        out_shape=jax.ShapeDtypeStruct((width // 2, shard_rows), jnp.bfloat16),
        name="finish",
    )(in_vmem(got), in_vmem(near), in_vmem(keep), residue, rates, skip)


def per_device(tokens, in_weight, short_weight, residue, rates, skip):
    shard_rows = tokens.shape[0]
    residue, rates = residue.T, rates.T
    partials = project(tokens, in_weight.transpose(1, 0, 2))
    parts = lax.all_to_all(partials, "chan", 0, 0, tiled=True)
    send, keep = local(parts, short_weight, residue, rates)
    got = lax.all_to_all(send, "near", 0, 0, tiled=True)
    send, near = near_sums(got, rates, shard_rows, lax.axis_size("far"))
    got = lax.all_to_all(send, "far", 0, 0, tiled=True)
    return finish(shard_rows, got, near, keep, residue, rates, skip[None, :]).T


def solution(mesh):
    seq, chan = mesh.devices.shape
    mesh = Mesh(mesh.devices.reshape(seq // NEAR, NEAR, chan), ("far", "near", "chan"))
    whole = ("far", "near")
    in_specs = (
        P(whole, "chan"),
        P("chan", None, None),
        P(None, None, "chan"),
        P("chan", None),
        P("chan", None),
        P("chan"),
    )
    return jax.shard_map(
        per_device, mesh=mesh, in_specs=in_specs, out_specs=P(whole, "chan"), check_vma=False
    )
```

```python
import functools

import jax
import jax.numpy as jnp
from jax import lax
from jax.experimental import pallas as pl
from jax.experimental.pallas import tpu as pltpu
from jax.sharding import Mesh, PartitionSpec as P

NEAR = 16
STEP = 8
F32 = jnp.float32
HBM = pl.BlockSpec(memory_space=pl.ANY)
ROOMY = pltpu.CompilerParams(vmem_limit_bytes=24 * 2**20)


def in_vmem(array):
    return pltpu.with_memory_space_constraint(array, pltpu.VMEM)


def in_hbm(array):
    return pltpu.with_memory_space_constraint(array, pltpu.HBM)


def lanes_of(shape):
    return lax.broadcasted_iota(jnp.int32, shape, 1)


def rows_of(shape):
    return lax.broadcasted_iota(jnp.int32, shape, 0)


def swap(tile):
    return pltpu.roll(tile, tile.shape[1] // 2, 1)


def twice(row):
    return jnp.concatenate([row, row], axis=1)


def folded(poles):
    half = poles.shape[0] // 2
    return jnp.concatenate([poles[:half], poles[half:]], axis=1)


def project_kernel(tok_hbm, w_hbm, out_ref, tok_ref, w_ref, acc_ref, sems):
    streams, depth, _ = w_ref.shape
    pieces = sems.shape[0]
    deep = depth // pieces
    parts = [pl.ds(i * deep, deep) for i in range(pieces)]
    copies = []
    for i, part in enumerate(parts):
        copies.append([pltpu.make_async_copy(tok_hbm.at[:, part], tok_ref.at[:, part], sems.at[i, streams])])
        for s in range(streams):
            copies[i].append(pltpu.make_async_copy(w_hbm.at[s, part], w_ref.at[s, part], sems.at[i, s]))
    for piece in copies:
        for copy in piece:
            copy.start()
    for i, part in enumerate(parts):
        for copy in copies[i]:
            copy.wait()
        for s in range(streams):
            term = jnp.dot(tok_ref[:, part], w_ref[s, part, :], preferred_element_type=F32)
            acc_ref[s] = term if i == 0 else acc_ref[s] + term
    rows = acc_ref.shape[1] // 2
    for s in range(streams):
        for pair in range(acc_ref.shape[2] // 128):
            early = acc_ref[s, :rows, 128 * pair : 128 * (pair + 1)]
            late = acc_ref[s, rows:, 128 * pair : 128 * (pair + 1)]
            left = lanes_of(early.shape) < 64
            out_ref[2 * pair, s] = jnp.where(left, early, swap(late))
            out_ref[2 * pair + 1, s] = jnp.where(left, swap(early), late)


def project(tokens, weight):
    rows, depth = tokens.shape
    streams, _, width = weight.shape
    chan = width // 64
    pieces = 4
    return pl.pallas_call(
        project_kernel,
        in_specs=[HBM, HBM],
        out_shape=pltpu.VMEM((chan, streams, rows // 2, 128), F32),
        scratch_shapes=[
            pltpu.VMEM(tokens.shape, tokens.dtype),
            pltpu.VMEM(weight.shape, weight.dtype),
            pltpu.VMEM((streams, rows, width), F32),
            pltpu.SemaphoreType.DMA((pieces, streams + 1)),
        ],
        compiler_params=ROOMY,
        name="project",
    )(in_hbm(tokens), in_hbm(weight))


def local_kernel(part_ref, short_ref, residue_ref, rates_ref, send_ref, keep_ref):
    count = part_ref.shape[0]
    rows, width = part_ref.shape[2:]
    right = lanes_of((1, width)) >= width // 2
    row = rows_of((rows, width))
    feats, edges = [], []
    for s in range(3):
        p = part_ref[0, s]
        for i in range(1, count):
            p = p + part_ref[i, s]
        tap = [twice(short_ref[k, s : s + 1, :]) for k in range(3)]
        before = jnp.where(right, swap(p[rows - 8 :]), 0.0)
        one = jnp.where(row < 1, before[7:8], pltpu.roll(p, 1, 0))
        two = pltpu.roll(p, 2, 0)
        two = jnp.where(row == 0, before[6:7], jnp.where(row == 1, before[7:8], two))
        feats.append(tap[0] * p + tap[1] * one + tap[2] * two)
        edges.append((tap[1] * p[rows - 1 :] + tap[2] * p[rows - 2 : rows - 1], tap[2] * p[rows - 1 :]))
    q, a, b = feats
    keep_ref[0:rows, :] = q
    x = jnp.where(jnp.logical_and(row < 2, jnp.logical_not(right)), 0.0, a * b)
    keep_ref[rows : 2 * rows, :] = x
    tile = [
        jnp.where(right, swap(b[0:1]), a[0:1]),
        jnp.where(right, swap(b[1:2]), a[1:2]),
        jnp.where(right, edges[2][0], swap(edges[1][0])),
        jnp.where(right, edges[2][1], swap(edges[1][1])),
        jnp.where(right, edges[0][1], swap(edges[0][0])),
    ]
    own = jnp.concatenate(tile + [jnp.zeros((3, width), F32)], axis=0)
    keep_ref[3 * rows : 3 * rows + 8, :] = own

    rates = twice(rates_ref[...])
    weight = twice(residue_ref[...]) * jnp.sqrt(2.0 * rates)
    poles = rates.shape[0]
    inner = rows_of((STEP, width))
    step_pos = inner.astype(F32)
    impulse = [jnp.sum(weight * jnp.exp(-rates * float(u)), axis=0, keepdims=True) for u in range(STEP)]
    near = [jnp.where(inner >= u, impulse[u], 0.0) for u in range(STEP)]
    decay = jnp.exp(-float(STEP) * rates)
    into, outof, fade = [], [], []
    for r in range(poles):
        rate = rates[r : r + 1]
        into.append(jnp.exp(-rate * (STEP - 1.0 - step_pos)))
        outof.append(weight[r : r + 1] * jnp.exp(-rate * (step_pos + 1.0)))
        fade.append(decay[r : r + 1])
    state = [None] * poles
    for k in range(rows // STEP):
        xk = x[k * STEP : (k + 1) * STEP]
        yk = near[0] * xk
        for u in range(1, STEP):
            yk = yk + near[u] * pltpu.roll(xk, u, 0)
        for r in range(poles):
            gain = jnp.sum(into[r] * xk, axis=0, keepdims=True)
            if k > 0:
                yk = yk + outof[r] * state[r]
                gain = gain + fade[r] * state[r]
            state[r] = gain
        keep_ref[2 * rows + k * STEP : 2 * rows + (k + 1) * STEP, :] = yk
    half = jnp.concatenate(state, axis=0)
    keep_ref[3 * rows + 8 :, :] = half
    total = half + jnp.exp(-float(rows) * rates) * swap(half)
    h = poles // 2
    packed = jnp.where(right, total[h:], swap(total[:h]))
    for i in range(send_ref.shape[0]):
        send_ref[i, 0:8, :] = packed
        send_ref[i, 8:16, :] = own


def local(parts, short_weight, residue, rates):
    _, _, rows, width = parts.shape
    return pl.pallas_call(
        local_kernel,
        out_shape=(
            pltpu.VMEM((NEAR, 16, width), F32),
            pltpu.VMEM((3 * rows + 8 + rates.shape[0], width), F32),
        ),
        compiler_params=ROOMY,
        name="local",
    )(in_vmem(parts), in_vmem(short_weight), in_vmem(residue), in_vmem(rates))


def gate_of(tile, before):
    a = tile[0:2]
    if before is not None:
        a = a + before[2:4]
    return a * swap(a)


def near_kernel(shard_rows, got_ref, rates_ref, send_ref, keep_ref):
    near = lax.axis_index("near")
    rates = folded(rates_ref[...])
    fade = jnp.exp(-float(shard_rows) * rates)
    first = jnp.exp(-(shard_rows - 1.0) * rates)
    second = jnp.exp(-(shard_rows - 2.0) * rates)
    total = got_ref[0, 0:8, :]
    prefix = jnp.where(near > 0, total, 0.0)
    before = jnp.zeros_like(total)
    for i in range(1, NEAR):
        edge = got_ref[i - 1, 8:16, :]
        gate = gate_of(got_ref[i, 8:16, :], edge)
        grown = total * fade + (got_ref[i, 0:8, :] + first * gate[0:1] + second * gate[1:2])
        before = jnp.where(near == i, edge, before)
        total = grown
        prefix = jnp.where(near > i, grown, prefix)
    keep_ref[0:8, :] = prefix
    keep_ref[8:16, :] = before
    head = got_ref[0, 8:16, :]
    tail = got_ref[NEAR - 1, 8:16, :]
    ends = jnp.where(rows_of(head.shape) < 2, head, tail)
    for i in range(send_ref.shape[0]):
        send_ref[i, 0:8, :] = total
        send_ref[i, 8:16, :] = ends


def near_sums(got, rates, shard_rows, far_count):
    width = got.shape[2]
    return pl.pallas_call(
        functools.partial(near_kernel, shard_rows),
        out_shape=(pltpu.VMEM((far_count, 16, width), F32), pltpu.VMEM((16, width), F32)),
        compiler_params=ROOMY,
        name="near_sums",
    )(in_vmem(got), in_vmem(rates))


def finish_kernel(shard_rows, got_ref, near_ref, keep_ref, residue_ref, rates_ref, skip_ref, out_ref):
    near, far = lax.axis_index("near"), lax.axis_index("far")
    rows, width = out_ref.shape[1] // 2, keep_ref.shape[1]
    rates = twice(rates_ref[...])
    weight = twice(residue_ref[...]) * jnp.sqrt(2.0 * rates)
    poles = rates.shape[0]
    skip = twice(skip_ref[...])
    step_pos = rows_of((STEP, width)).astype(F32)
    decay = jnp.exp(-float(STEP) * rates)
    half_decay = jnp.exp(-float(rows) * rates)
    ahead = jnp.sum(weight * jnp.exp(rates), axis=0, keepdims=True)
    outof, fade = [], []
    for r in range(poles):
        outof.append(weight[r : r + 1] * jnp.exp(-rates[r : r + 1] * (step_pos + 1.0)))
        fade.append(jnp.broadcast_to(decay[r : r + 1], (STEP, width)))

    rates = folded(rates_ref[...])
    first = jnp.exp(-(shard_rows - 1.0) * rates)
    second = jnp.exp(-(shard_rows - 2.0) * rates)
    last = jnp.exp(-float((NEAR - 1) * shard_rows) * rates)
    row_fade = jnp.exp(-float(NEAR * shard_rows) * rates)
    place = near.astype(F32) * float(shard_rows)
    place_fade = jnp.exp(-place * rates)
    beyond_fade = jnp.where(near > 0, jnp.exp(-jnp.maximum(place - shard_rows, 0.0) * rates), 0.0)
    ahead_one, ahead_two = jnp.exp(rates), jnp.exp(2.0 * rates)
    before = near_ref[8:16, :]
    carry = jnp.zeros_like(rates)
    opening = jnp.zeros_like(rates)
    edge = None
    for z in range(got_ref.shape[0]):
        gate = gate_of(got_ref[z, 8:16, :], edge)
        start = first * gate[0:1] + second * gate[1:2]
        opening = jnp.where(far == z, start, opening)
        if edge is not None:
            before = jnp.where(jnp.logical_and(near == 0, far == z), edge, before)
        grown = carry * row_fade + (got_ref[z, 0:8, :] + last * start)
        carry = jnp.where(far > z, grown, carry)
        edge = got_ref[z, 8:16, :]
    state = near_ref[0:8, :] + place_fade * carry + beyond_fade * opening
    gate = gate_of(keep_ref[3 * rows : 3 * rows + 8, :], before)
    state = state + ahead_one * gate[0:1] + ahead_two * gate[1:2]

    left = lanes_of((1, width)) < width // 2
    other = swap(state)
    whole = jnp.concatenate([jnp.where(left, state, other), jnp.where(left, other, state)], axis=0)
    whole = jnp.where(left, whole, swap(keep_ref[3 * rows + 8 :, :]) + half_decay * whole)
    states = [jnp.broadcast_to(whole[r : r + 1], (STEP, width)) * outof[r] for r in range(poles)]
    steps = []
    for k in range(rows // STEP):
        at = k * STEP
        qk = keep_ref[at : at + STEP, :]
        xk = keep_ref[rows + at : rows + at + STEP, :]
        yk = keep_ref[2 * rows + at : 2 * rows + at + STEP, :]
        if k == 0:
            inner = rows_of((STEP, width))
            top = jnp.logical_and(left, inner == 0)
            next_ = jnp.logical_and(left, inner == 1)
            xk = jnp.where(top, gate[0:1], jnp.where(next_, gate[1:2], xk))
            yk = yk - jnp.where(top, ahead * gate[1:2], 0.0)
            q_edge = before[4:5]
            qk = qk + jnp.where(top, q_edge, jnp.where(next_, swap(q_edge), 0.0))
        for r in range(poles):
            yk = yk + states[r]
            states[r] = states[r] * fade[r]
        steps.append(qk * (yk + skip * xk))
    mixed = jnp.concatenate(steps, axis=0).T
    out_ref[:, :rows] = mixed[: width // 2].astype(out_ref.dtype)
    out_ref[:, rows:] = mixed[width // 2 :].astype(out_ref.dtype)


def finish(shard_rows, got, near, keep, residue, rates, skip):
    width = keep.shape[1]
    return pl.pallas_call(
        functools.partial(finish_kernel, shard_rows),
        out_shape=jax.ShapeDtypeStruct((width // 2, shard_rows), jnp.bfloat16),
        compiler_params=ROOMY,
        name="finish",
    )(in_vmem(got), in_vmem(near), in_vmem(keep), in_vmem(residue), in_vmem(rates), in_vmem(skip))


def per_device(tokens, in_weight, short_weight, residue, rates, skip):
    shard_rows = tokens.shape[0]
    residue, rates = residue.T, rates.T
    partials = project(tokens, in_weight.transpose(1, 0, 2))
    parts = lax.all_to_all(partials, "chan", 0, 0, tiled=True)
    send, keep = local(parts, short_weight, residue, rates)
    got = lax.all_to_all(send, "near", 0, 0, tiled=True)
    send, near = near_sums(got, rates, shard_rows, lax.axis_size("far"))
    got = lax.all_to_all(send, "far", 0, 0, tiled=True)
    return finish(shard_rows, got, near, keep, residue, rates, skip[None, :]).T


def solution(mesh):
    seq, chan = mesh.devices.shape
    mesh = Mesh(mesh.devices.reshape(seq // NEAR, NEAR, chan), ("far", "near", "chan"))
    whole = ("far", "near")
    in_specs = (
        P(whole, "chan"),
        P("chan", None, None),
        P(None, None, "chan"),
        P("chan", None),
        P("chan", None),
        P("chan"),
    )
    return jax.shard_map(
        per_device, mesh=mesh, in_specs=in_specs, out_specs=P(whole, "chan"), check_vma=False
    )
```

```python
import functools

import jax
import jax.numpy as jnp
from jax import lax
from jax.experimental import pallas as pl
from jax.experimental.pallas import tpu as pltpu
from jax.sharding import Mesh, PartitionSpec as P

NEAR = 16
STEP = 8
F32 = jnp.float32
HBM = pl.BlockSpec(memory_space=pl.ANY)
ROOMY = pltpu.CompilerParams(vmem_limit_bytes=24 * 2**20)


def in_vmem(array):
    return pltpu.with_memory_space_constraint(array, pltpu.VMEM)


def in_hbm(array):
    return pltpu.with_memory_space_constraint(array, pltpu.HBM)


def lanes_of(shape):
    return lax.broadcasted_iota(jnp.int32, shape, 1)


def rows_of(shape):
    return lax.broadcasted_iota(jnp.int32, shape, 0)


def swap(tile):
    return pltpu.roll(tile, tile.shape[1] // 2, 1)


def twice(row):
    return jnp.concatenate([row, row], axis=1)


def folded(poles):
    half = poles.shape[0] // 2
    return jnp.concatenate([poles[:half], poles[half:]], axis=1)


def project_kernel(tok_hbm, w_hbm, out_ref, tok_ref, w_ref, acc_ref, sems):
    streams, depth, _ = w_ref.shape
    pieces = sems.shape[0]
    deep = depth // pieces
    parts = [pl.ds(i * deep, deep) for i in range(pieces)]
    copies = []
    for i, part in enumerate(parts):
        copies.append([pltpu.make_async_copy(tok_hbm.at[:, part], tok_ref.at[:, part], sems.at[i, streams])])
        for s in range(streams):
            copies[i].append(pltpu.make_async_copy(w_hbm.at[s, part], w_ref.at[s, part], sems.at[i, s]))
    for piece in copies:
        for copy in piece:
            copy.start()
    for i, part in enumerate(parts):
        for copy in copies[i]:
            copy.wait()
        for s in range(streams):
            term = jnp.dot(tok_ref[:, part], w_ref[s, part, :], preferred_element_type=F32)
            acc_ref[s] = term if i == 0 else acc_ref[s] + term
    rows = acc_ref.shape[1] // 2
    for s in range(streams):
        for pair in range(acc_ref.shape[2] // 128):
            early = acc_ref[s, :rows, 128 * pair : 128 * (pair + 1)]
            late = acc_ref[s, rows:, 128 * pair : 128 * (pair + 1)]
            left = lanes_of(early.shape) < 64
            out_ref[2 * pair, s] = jnp.where(left, early, swap(late))
            out_ref[2 * pair + 1, s] = jnp.where(left, swap(early), late)


def project(tokens, weight):
    rows, depth = tokens.shape
    streams, _, width = weight.shape
    chan = width // 64
    pieces = 4
    return pl.pallas_call(
        project_kernel,
        in_specs=[HBM, HBM],
        out_shape=pltpu.VMEM((chan, streams, rows // 2, 128), F32),
        scratch_shapes=[
            pltpu.VMEM(tokens.shape, tokens.dtype),
            pltpu.VMEM(weight.shape, weight.dtype),
            pltpu.VMEM((streams, rows, width), F32),
            pltpu.SemaphoreType.DMA((pieces, streams + 1)),
        ],
        compiler_params=ROOMY,
        name="project",
    )(in_hbm(tokens), in_hbm(weight))


def local_kernel(part_ref, short_ref, residue_ref, rates_ref, skip_ref, send_ref, keep_ref):
    count = part_ref.shape[0]
    rows, width = part_ref.shape[2:]
    right = lanes_of((1, width)) >= width // 2
    row = rows_of((rows, width))
    feats, edges = [], []
    for s in range(3):
        p = part_ref[0, s]
        for i in range(1, count):
            p = p + part_ref[i, s]
        tap = [twice(short_ref[k, s : s + 1, :]) for k in range(3)]
        before = jnp.where(right, swap(p[rows - 8 :]), 0.0)
        one = jnp.where(row < 1, before[7:8], pltpu.roll(p, 1, 0))
        two = pltpu.roll(p, 2, 0)
        two = jnp.where(row == 0, before[6:7], jnp.where(row == 1, before[7:8], two))
        feats.append(tap[0] * p + tap[1] * one + tap[2] * two)
        edges.append((tap[1] * p[rows - 1 :] + tap[2] * p[rows - 2 : rows - 1], tap[2] * p[rows - 1 :]))
    q, a, b = feats
    keep_ref[0:rows, :] = q
    x = jnp.where(jnp.logical_and(row < 2, jnp.logical_not(right)), 0.0, a * b)
    keep_ref[rows : 2 * rows, :] = x
    tile = [
        jnp.where(right, swap(b[0:1]), a[0:1]),
        jnp.where(right, swap(b[1:2]), a[1:2]),
        jnp.where(right, edges[2][0], swap(edges[1][0])),
        jnp.where(right, edges[2][1], swap(edges[1][1])),
        jnp.where(right, edges[0][1], swap(edges[0][0])),
    ]
    own = jnp.concatenate(tile + [jnp.zeros((3, width), F32)], axis=0)
    keep_ref[3 * rows : 3 * rows + 8, :] = own

    rates = twice(rates_ref[...])
    weight = twice(residue_ref[...]) * jnp.sqrt(2.0 * rates)
    poles = rates.shape[0]
    at = 3 * rows + 8 + poles
    keep_ref[at : at + poles, :] = rates
    keep_ref[at + poles : at + 2 * poles, :] = weight
    keep_ref[at + 2 * poles :, :] = jnp.broadcast_to(twice(skip_ref[...]), (8, width))
    inner = rows_of((STEP, width))
    step_pos = inner.astype(F32)
    impulse = [jnp.sum(weight * jnp.exp(-rates * float(u)), axis=0, keepdims=True) for u in range(STEP)]
    near = [jnp.where(inner >= u, impulse[u], 0.0) for u in range(STEP)]
    decay = jnp.exp(-float(STEP) * rates)
    into, outof, fade = [], [], []
    for r in range(poles):
        rate = rates[r : r + 1]
        into.append(jnp.exp(-rate * (STEP - 1.0 - step_pos)))
        outof.append(weight[r : r + 1] * jnp.exp(-rate * (step_pos + 1.0)))
        fade.append(decay[r : r + 1])
    state = [None] * poles
    for k in range(rows // STEP):
        xk = x[k * STEP : (k + 1) * STEP]
        yk = near[0] * xk
        for u in range(1, STEP):
            yk = yk + near[u] * pltpu.roll(xk, u, 0)
        for r in range(poles):
            gain = jnp.sum(into[r] * xk, axis=0, keepdims=True)
            if k > 0:
                yk = yk + outof[r] * state[r]
                gain = gain + fade[r] * state[r]
            state[r] = gain
        keep_ref[2 * rows + k * STEP : 2 * rows + (k + 1) * STEP, :] = yk
    half = jnp.concatenate(state, axis=0)
    keep_ref[3 * rows + 8 : at, :] = half
    total = half + jnp.exp(-float(rows) * rates) * swap(half)
    h = poles // 2
    packed = jnp.where(right, total[h:], swap(total[:h]))
    for i in range(send_ref.shape[0]):
        send_ref[i, 0:8, :] = packed
        send_ref[i, 8:16, :] = own


def local(parts, short_weight, residue, rates, skip):
    _, _, rows, width = parts.shape
    return pl.pallas_call(
        local_kernel,
        out_shape=(
            pltpu.VMEM((NEAR, 16, width), F32),
            pltpu.VMEM((3 * rows + 16 + 3 * rates.shape[0], width), F32),
        ),
        compiler_params=ROOMY,
        name="local",
    )(in_vmem(parts), in_vmem(short_weight), in_vmem(residue), in_vmem(rates), in_vmem(skip))


def gate_of(tile, before):
    a = tile[0:2]
    if before is not None:
        a = a + before[2:4]
    return a * swap(a)


def near_kernel(shard_rows, got_ref, rates_ref, send_ref, keep_ref):
    near = lax.axis_index("near")
    rates = folded(rates_ref[...])
    fade = jnp.exp(-float(shard_rows) * rates)
    first = jnp.exp(-(shard_rows - 1.0) * rates)
    second = jnp.exp(-(shard_rows - 2.0) * rates)
    total = got_ref[0, 0:8, :]
    prefix = jnp.where(near > 0, total, 0.0)
    before = jnp.zeros_like(total)
    for i in range(1, NEAR):
        edge = got_ref[i - 1, 8:16, :]
        gate = gate_of(got_ref[i, 8:16, :], edge)
        grown = total * fade + (got_ref[i, 0:8, :] + first * gate[0:1] + second * gate[1:2])
        before = jnp.where(near == i, edge, before)
        total = grown
        prefix = jnp.where(near > i, grown, prefix)
    keep_ref[0:8, :] = prefix
    keep_ref[8:16, :] = before
    keep_ref[16:24, :] = rates
    head = got_ref[0, 8:16, :]
    tail = got_ref[NEAR - 1, 8:16, :]
    ends = jnp.where(rows_of(head.shape) < 2, head, tail)
    send_ref[0:8, :] = total
    send_ref[8:16, :] = ends


def near_sums(got, rates, shard_rows):
    width = got.shape[2]
    return pl.pallas_call(
        functools.partial(near_kernel, shard_rows),
        out_shape=(pltpu.VMEM((16, width), F32), pltpu.VMEM((24, width), F32)),
        compiler_params=ROOMY,
        name="near_sums",
    )(in_vmem(got), in_vmem(rates))


def with_row(shard_rows, row, got, rates):
    gate = gate_of(row[8:16], got[8:16])
    start = jnp.exp(-(shard_rows - 1.0) * rates) * gate[0:1] + jnp.exp(-(shard_rows - 2.0) * rates) * gate[1:2]
    state = row[0:8] + jnp.exp(-float((NEAR - 1) * shard_rows) * rates) * start
    state = state + jnp.exp(-float(NEAR * shard_rows) * rates) * got[0:8]
    return jnp.concatenate([state, row[8:16]], axis=0)


def first_kernel(shard_rows, row_ref, near_ref, total_ref):
    total_ref[...] = with_row(shard_rows, row_ref[...], jnp.zeros(row_ref.shape, F32), near_ref[16:24, :])


def first_sum(shard_rows, row, near):
    return pl.pallas_call(
        functools.partial(first_kernel, shard_rows),
        out_shape=pltpu.VMEM(row.shape, F32),
        compiler_params=ROOMY,
        name="first_sum",
    )(in_vmem(row), in_vmem(near))


def hop_kernel(shard_rows, sums, sources, *refs):
    rows_before, (row_ref, near_ref, keep_ref), refs = refs[:sources], refs[sources : sources + 3], refs[sources + 3 :]
    sum_refs, (before_ref, row_out, near_out, keep_out) = refs[:sums], refs[sums:]
    rates = near_ref[16:24, :]
    before = rows_before[0][...]
    if sources > 1:
        before = with_row(shard_rows, rows_before[1][...], before, rates)
    before_ref[...] = before
    if sums:
        total = with_row(shard_rows, row_ref[...], before, rates)
    for ref in sum_refs:
        ref[...] = total
    row_out[...] = row_ref[...]
    near_out[...] = near_ref[...]
    keep_out[...] = keep_ref[...]


def hop(shard_rows, sums, sources, row, near, keep):
    operands = [in_vmem(a) for a in (*sources, row, near, keep)]
    outs = (row,) * (sums + 2) + (near, keep)
    return pl.pallas_call(
        functools.partial(hop_kernel, shard_rows, sums, len(sources)),
        out_shape=tuple(pltpu.VMEM(a.shape, F32) for a in outs),
        compiler_params=ROOMY,
        name="hop",
    )(*operands)


def finish_kernel(shard_rows, row_ref, got_ref, near_ref, keep_ref, out_ref):
    near = lax.axis_index("near")
    rows, width = out_ref.shape[1] // 2, keep_ref.shape[1]
    poles = 2 * near_ref[16:24, :].shape[0]
    at = 3 * rows + 8 + poles
    rates = keep_ref[at : at + poles, :]
    weight = keep_ref[at + poles : at + 2 * poles, :]
    skip = keep_ref[at + 2 * poles : at + 2 * poles + 1, :]
    step_pos = rows_of((STEP, width)).astype(F32)
    decay = jnp.exp(-float(STEP) * rates)
    half_decay = jnp.exp(-float(rows) * rates)
    ahead = jnp.sum(weight * jnp.exp(rates), axis=0, keepdims=True)
    outof, fade = [], []
    for r in range(poles):
        outof.append(weight[r : r + 1] * jnp.exp(-rates[r : r + 1] * (step_pos + 1.0)))
        fade.append(jnp.broadcast_to(decay[r : r + 1], (STEP, width)))

    rates = near_ref[16:24, :]
    first = jnp.exp(-(shard_rows - 1.0) * rates)
    second = jnp.exp(-(shard_rows - 2.0) * rates)
    place = near.astype(F32) * float(shard_rows)
    place_fade = jnp.exp(-place * rates)
    beyond_fade = jnp.where(near > 0, jnp.exp(-jnp.maximum(place - shard_rows, 0.0) * rates), 0.0)
    ahead_one, ahead_two = jnp.exp(rates), jnp.exp(2.0 * rates)
    edge = got_ref[8:16, :]
    before = jnp.where(near == 0, edge, near_ref[8:16, :])
    gate = gate_of(row_ref[8:16, :], edge)
    opening = first * gate[0:1] + second * gate[1:2]
    carry = got_ref[0:8, :]
    state = near_ref[0:8, :] + place_fade * carry + beyond_fade * opening
    gate = gate_of(keep_ref[3 * rows : 3 * rows + 8, :], before)
    state = state + ahead_one * gate[0:1] + ahead_two * gate[1:2]

    left = lanes_of((1, width)) < width // 2
    other = swap(state)
    whole = jnp.concatenate([jnp.where(left, state, other), jnp.where(left, other, state)], axis=0)
    whole = jnp.where(left, whole, swap(keep_ref[3 * rows + 8 : 3 * rows + 8 + poles, :]) + half_decay * whole)
    states = [jnp.broadcast_to(whole[r : r + 1], (STEP, width)) * outof[r] for r in range(poles)]
    steps = []
    for k in range(rows // STEP):
        at = k * STEP
        qk = keep_ref[at : at + STEP, :]
        xk = keep_ref[rows + at : rows + at + STEP, :]
        yk = keep_ref[2 * rows + at : 2 * rows + at + STEP, :]
        if k == 0:
            inner = rows_of((STEP, width))
            top = jnp.logical_and(left, inner == 0)
            next_ = jnp.logical_and(left, inner == 1)
            xk = jnp.where(top, gate[0:1], jnp.where(next_, gate[1:2], xk))
            yk = yk - jnp.where(top, ahead * gate[1:2], 0.0)
            q_edge = before[4:5]
            qk = qk + jnp.where(top, q_edge, jnp.where(next_, swap(q_edge), 0.0))
        for r in range(poles):
            yk = yk + states[r]
            states[r] = states[r] * fade[r]
        steps.append(qk * (yk + skip * xk))
    mixed = jnp.concatenate(steps, axis=0).T
    out_ref[:, :rows] = mixed[: width // 2].astype(out_ref.dtype)
    out_ref[:, rows:] = mixed[width // 2 :].astype(out_ref.dtype)


def finish(shard_rows, row, got, near, keep):
    width = keep.shape[1]
    return pl.pallas_call(
        functools.partial(finish_kernel, shard_rows),
        out_shape=jax.ShapeDtypeStruct((width // 2, shard_rows), jnp.bfloat16),
        compiler_params=ROOMY,
        name="finish",
    )(in_vmem(row), in_vmem(got), in_vmem(near), in_vmem(keep))


def moved_kernel(source_ref, target_ref):
    target_ref[...] = source_ref[...]


def moved(array):
    return pl.pallas_call(
        moved_kernel, out_shape=pltpu.VMEM(array.shape, F32), compiler_params=ROOMY, name="moved"
    )(in_vmem(array))


def nothing(*shapes):
    return pl.pallas_call(
        lambda *refs: None,
        out_shape=tuple(pltpu.VMEM(shape, F32) for shape in shapes),
        name="nothing",
    )()


def per_device(tokens, in_weight, short_weight, residue, rates, skip):
    shard_rows = tokens.shape[0]
    residue, rates, skip = residue.T, rates.T, skip[None, :]
    weight = in_weight.transpose(1, 0, 2)
    far, far_count = lax.axis_index("far"), lax.axis_size("far")

    def row_of_shards():
        parts = lax.all_to_all(project(tokens, weight), "chan", 0, 0, tiled=True)
        send, keep = local(parts, short_weight, residue, rates, skip)
        row, near = near_sums(lax.all_to_all(send, "near", 0, 0, tiled=True), rates, shard_rows)
        return row, near, keep

    shapes = [a.shape for a in jax.eval_shape(row_of_shards)]

    def work_of(mine):
        return lax.cond(mine, row_of_shards, lambda: nothing(*shapes))

    row, near, keep = even = work_of(far % 2 == 0)
    none = jnp.zeros(shapes[0], F32)

    def hand_on(after, total, k):
        here = jnp.logical_or(far == k, far == k + 1)
        return lax.cond(here, lambda: moved(lax.ppermute(total, "far", [(k, k + 1)])), lambda: moved(after))

    total = first_sum(shard_rows, row, near)
    results = [(row, none, near, keep)]
    after = none
    for k in range(1, far_count, 2):
        sums = 2 if k + 1 < far_count else 0

        def odd_row(k=k, total=total, sums=sums):
            sources = [lax.ppermute(total, "far", [(max(k - 2, 0), k)])]
            if k > 1:
                sources.append(lax.ppermute(even[0], "far", [(k - 1, k)]))
            return hop(shard_rows, sums, sources, *work_of(far == k))

        here = jnp.logical_and(far <= k, far >= k - 2)
        out = lax.cond(here, odd_row, lambda sums=sums: nothing(*shapes[:1] * (sums + 1), *shapes))
        before, *rest = out[sums:]
        results.append((rest[0], before, *rest[1:]))
        if k > 1:
            again, *out = lax.optimization_barrier((again, *out))
            after = hand_on(after, again, k - 2)
        total, again = out[:2]
    results[0] = (row, after, near, keep)
    branches = [lambda r=r: finish(shard_rows, *r) for r in results]
    return lax.switch(jnp.where(far % 2 == 0, 0, (far + 1) // 2), branches).T


def solution(mesh):
    seq, chan = mesh.devices.shape
    mesh = Mesh(mesh.devices.reshape(seq // NEAR, NEAR, chan), ("far", "near", "chan"))
    whole = ("far", "near")
    in_specs = (
        P(whole, "chan"),
        P("chan", None, None),
        P(None, None, "chan"),
        P("chan", None),
        P("chan", None),
        P("chan"),
    )
    return jax.shard_map(
        per_device, mesh=mesh, in_specs=in_specs, out_specs=P(whole, "chan"), check_vma=False
    )
```

```python
import functools

import jax
import jax.numpy as jnp
from jax import lax
from jax.experimental import pallas as pl
from jax.experimental.pallas import tpu as pltpu
from jax.sharding import Mesh, PartitionSpec as P

NEAR = 16
STEP = 8
F32 = jnp.float32
HBM = pl.BlockSpec(memory_space=pl.ANY)
ROOMY = pltpu.CompilerParams(vmem_limit_bytes=24 * 2**20)


def in_vmem(array):
    return pltpu.with_memory_space_constraint(array, pltpu.VMEM)


def in_hbm(array):
    return pltpu.with_memory_space_constraint(array, pltpu.HBM)


def lanes_of(shape):
    return lax.broadcasted_iota(jnp.int32, shape, 1)


def rows_of(shape):
    return lax.broadcasted_iota(jnp.int32, shape, 0)


def swap(tile):
    return pltpu.roll(tile, tile.shape[1] // 2, 1)


def twice(row):
    return jnp.concatenate([row, row], axis=1)


def folded(poles):
    half = poles.shape[0] // 2
    return jnp.concatenate([poles[:half], poles[half:]], axis=1)


def project_kernel(tok_hbm, w_hbm, out_ref, tok_ref, w_ref, acc_ref, sems):
    streams, depth, _ = w_ref.shape
    pieces = sems.shape[0]
    deep = depth // pieces
    parts = [pl.ds(i * deep, deep) for i in range(pieces)]
    copies = []
    for i, part in enumerate(parts):
        copies.append([pltpu.make_async_copy(tok_hbm.at[:, part], tok_ref.at[:, part], sems.at[i, streams])])
        for s in range(streams):
            copies[i].append(pltpu.make_async_copy(w_hbm.at[s, part], w_ref.at[s, part], sems.at[i, s]))
    for piece in copies:
        for copy in piece:
            copy.start()
    for i, part in enumerate(parts):
        for copy in copies[i]:
            copy.wait()
        for s in range(streams):
            term = jnp.dot(tok_ref[:, part], w_ref[s, part, :], preferred_element_type=F32)
            acc_ref[s] = term if i == 0 else acc_ref[s] + term
    rows = acc_ref.shape[1] // 2
    for s in range(streams):
        for pair in range(acc_ref.shape[2] // 128):
            early = acc_ref[s, :rows, 128 * pair : 128 * (pair + 1)]
            late = acc_ref[s, rows:, 128 * pair : 128 * (pair + 1)]
            left = lanes_of(early.shape) < 64
            out_ref[2 * pair, s] = jnp.where(left, early, swap(late))
            out_ref[2 * pair + 1, s] = jnp.where(left, swap(early), late)


def project(tokens, weight):
    rows, depth = tokens.shape
    streams, _, width = weight.shape
    chan = width // 64
    pieces = 4
    return pl.pallas_call(
        project_kernel,
        in_specs=[HBM, HBM],
        out_shape=pltpu.VMEM((chan, streams, rows // 2, 128), F32),
        scratch_shapes=[
            pltpu.VMEM(tokens.shape, tokens.dtype),
            pltpu.VMEM(weight.shape, weight.dtype),
            pltpu.VMEM((streams, rows, width), F32),
            pltpu.SemaphoreType.DMA((pieces, streams + 1)),
        ],
        compiler_params=ROOMY,
        name="project",
    )(in_hbm(tokens), in_hbm(weight))


def local_kernel(part_ref, short_ref, residue_ref, rates_ref, skip_ref, send_ref, keep_ref):
    count = part_ref.shape[0]
    rows, width = part_ref.shape[2:]
    right = lanes_of((1, width)) >= width // 2
    row = rows_of((rows, width))
    feats, edges = [], []
    for s in range(3):
        p = part_ref[0, s]
        for i in range(1, count):
            p = p + part_ref[i, s]
        tap = [twice(short_ref[k, s : s + 1, :]) for k in range(3)]
        before = jnp.where(right, swap(p[rows - 8 :]), 0.0)
        one = jnp.where(row < 1, before[7:8], pltpu.roll(p, 1, 0))
        two = pltpu.roll(p, 2, 0)
        two = jnp.where(row == 0, before[6:7], jnp.where(row == 1, before[7:8], two))
        feats.append(tap[0] * p + tap[1] * one + tap[2] * two)
        edges.append((tap[1] * p[rows - 1 :] + tap[2] * p[rows - 2 : rows - 1], tap[2] * p[rows - 1 :]))
    q, a, b = feats
    keep_ref[0:rows, :] = q
    x = jnp.where(jnp.logical_and(row < 2, jnp.logical_not(right)), 0.0, a * b)
    keep_ref[rows : 2 * rows, :] = x
    tile = [
        jnp.where(right, swap(b[0:1]), a[0:1]),
        jnp.where(right, swap(b[1:2]), a[1:2]),
        jnp.where(right, edges[2][0], swap(edges[1][0])),
        jnp.where(right, edges[2][1], swap(edges[1][1])),
        jnp.where(right, edges[0][1], swap(edges[0][0])),
    ]
    own = jnp.concatenate(tile + [jnp.zeros((3, width), F32)], axis=0)
    keep_ref[3 * rows : 3 * rows + 8, :] = own

    rates = twice(rates_ref[...])
    weight = twice(residue_ref[...]) * jnp.sqrt(2.0 * rates)
    poles = rates.shape[0]
    at = 3 * rows + 8 + poles
    keep_ref[at : at + poles, :] = rates
    keep_ref[at + poles : at + 2 * poles, :] = weight
    keep_ref[at + 2 * poles :, :] = jnp.broadcast_to(twice(skip_ref[...]), (8, width))
    inner = rows_of((STEP, width))
    step_pos = inner.astype(F32)
    impulse = [jnp.sum(weight * jnp.exp(-rates * float(u)), axis=0, keepdims=True) for u in range(STEP)]
    near = [jnp.where(inner >= u, impulse[u], 0.0) for u in range(STEP)]
    decay = jnp.exp(-float(STEP) * rates)
    into, outof, fade = [], [], []
    for r in range(poles):
        rate = rates[r : r + 1]
        into.append(jnp.exp(-rate * (STEP - 1.0 - step_pos)))
        outof.append(weight[r : r + 1] * jnp.exp(-rate * (step_pos + 1.0)))
        fade.append(decay[r : r + 1])
    state = [None] * poles
    for k in range(rows // STEP):
        xk = x[k * STEP : (k + 1) * STEP]
        yk = near[0] * xk
        for u in range(1, STEP):
            yk = yk + near[u] * pltpu.roll(xk, u, 0)
        for r in range(poles):
            gain = jnp.sum(into[r] * xk, axis=0, keepdims=True)
            if k > 0:
                yk = yk + outof[r] * state[r]
                gain = gain + fade[r] * state[r]
            state[r] = gain
        keep_ref[2 * rows + k * STEP : 2 * rows + (k + 1) * STEP, :] = yk
    half = jnp.concatenate(state, axis=0)
    keep_ref[3 * rows + 8 : at, :] = half
    total = half + jnp.exp(-float(rows) * rates) * swap(half)
    h = poles // 2
    packed = jnp.where(right, total[h:], swap(total[:h]))
    for i in range(send_ref.shape[0]):
        send_ref[i, 0:8, :] = packed
        send_ref[i, 8:16, :] = own


def local(parts, short_weight, residue, rates, skip):
    _, _, rows, width = parts.shape
    return pl.pallas_call(
        local_kernel,
        out_shape=(
            pltpu.VMEM((NEAR, 16, width), F32),
            pltpu.VMEM((3 * rows + 16 + 3 * rates.shape[0], width), F32),
        ),
        compiler_params=ROOMY,
        name="local",
    )(in_vmem(parts), in_vmem(short_weight), in_vmem(residue), in_vmem(rates), in_vmem(skip))


def gate_of(tile, before):
    a = tile[0:2]
    if before is not None:
        a = a + before[2:4]
    return a * swap(a)


def near_kernel(shard_rows, got_ref, rates_ref, send_ref, keep_ref):
    near = lax.axis_index("near")
    rates = folded(rates_ref[...])
    fade = jnp.exp(-float(shard_rows) * rates)
    first = jnp.exp(-(shard_rows - 1.0) * rates)
    second = jnp.exp(-(shard_rows - 2.0) * rates)
    total = got_ref[0, 0:8, :]
    prefix = jnp.where(near > 0, total, 0.0)
    before = jnp.zeros_like(total)
    for i in range(1, NEAR):
        edge = got_ref[i - 1, 8:16, :]
        gate = gate_of(got_ref[i, 8:16, :], edge)
        grown = total * fade + (got_ref[i, 0:8, :] + first * gate[0:1] + second * gate[1:2])
        before = jnp.where(near == i, edge, before)
        total = grown
        prefix = jnp.where(near > i, grown, prefix)
    keep_ref[0:8, :] = prefix
    keep_ref[8:16, :] = before
    keep_ref[16:24, :] = rates
    head = got_ref[0, 8:16, :]
    tail = got_ref[NEAR - 1, 8:16, :]
    ends = jnp.where(rows_of(head.shape) < 2, head, tail)
    send_ref[0:8, :] = total
    send_ref[8:16, :] = ends


def near_sums(got, rates, shard_rows):
    width = got.shape[2]
    return pl.pallas_call(
        functools.partial(near_kernel, shard_rows),
        out_shape=(pltpu.VMEM((16, width), F32), pltpu.VMEM((24, width), F32)),
        compiler_params=ROOMY,
        name="near_sums",
    )(in_vmem(got), in_vmem(rates))


def with_row(shard_rows, row, got, rates):
    gate = gate_of(row[8:16], got[8:16])
    start = jnp.exp(-(shard_rows - 1.0) * rates) * gate[0:1] + jnp.exp(-(shard_rows - 2.0) * rates) * gate[1:2]
    state = row[0:8] + jnp.exp(-float((NEAR - 1) * shard_rows) * rates) * start
    state = state + jnp.exp(-float(NEAR * shard_rows) * rates) * got[0:8]
    return jnp.concatenate([state, row[8:16]], axis=0)


def first_kernel(shard_rows, row_ref, near_ref, total_ref):
    total_ref[...] = with_row(shard_rows, row_ref[...], jnp.zeros(row_ref.shape, F32), near_ref[16:24, :])


def first_sum(shard_rows, row, near):
    return pl.pallas_call(
        functools.partial(first_kernel, shard_rows),
        out_shape=pltpu.VMEM(row.shape, F32),
        compiler_params=ROOMY,
        name="first_sum",
    )(in_vmem(row), in_vmem(near))


def hop_kernel(shard_rows, sums, sources, *refs):
    rows_before, (row_ref, near_ref, keep_ref), refs = refs[:sources], refs[sources : sources + 3], refs[sources + 3 :]
    sum_refs, (before_ref, row_out, near_out, keep_out) = refs[:sums], refs[sums:]
    rates = near_ref[16:24, :]
    before = rows_before[0][...]
    if sources > 1:
        before = with_row(shard_rows, rows_before[1][...], before, rates)
    before_ref[...] = before
    if sums:
        total = with_row(shard_rows, row_ref[...], before, rates)
    for ref in sum_refs:
        ref[...] = total
    row_out[...] = row_ref[...]
    near_out[...] = near_ref[...]
    keep_out[...] = keep_ref[...]


def hop(shard_rows, sums, sources, row, near, keep):
    operands = [in_vmem(a) for a in (*sources, row, near, keep)]
    outs = (row,) * (sums + 2) + (near, keep)
    return pl.pallas_call(
        functools.partial(hop_kernel, shard_rows, sums, len(sources)),
        out_shape=tuple(pltpu.VMEM(a.shape, F32) for a in outs),
        compiler_params=ROOMY,
        name="hop",
    )(*operands)


def finish_kernel(shard_rows, row_ref, got_ref, near_ref, keep_ref, out_ref):
    near = lax.axis_index("near")
    rows, width = out_ref.shape[1] // 2, keep_ref.shape[1]
    poles = 2 * near_ref[16:24, :].shape[0]
    at = 3 * rows + 8 + poles
    rates = keep_ref[at : at + poles, :]
    weight = keep_ref[at + poles : at + 2 * poles, :]
    skip = keep_ref[at + 2 * poles : at + 2 * poles + 1, :]
    step_pos = rows_of((STEP, width)).astype(F32)
    decay = jnp.exp(-float(STEP) * rates)
    half_decay = jnp.exp(-float(rows) * rates)
    ahead = jnp.sum(weight * jnp.exp(rates), axis=0, keepdims=True)
    outof, fade = [], []
    for r in range(poles):
        outof.append(weight[r : r + 1] * jnp.exp(-rates[r : r + 1] * (step_pos + 1.0)))
        fade.append(jnp.broadcast_to(decay[r : r + 1], (STEP, width)))

    rates = near_ref[16:24, :]
    first = jnp.exp(-(shard_rows - 1.0) * rates)
    second = jnp.exp(-(shard_rows - 2.0) * rates)
    place = near.astype(F32) * float(shard_rows)
    place_fade = jnp.exp(-place * rates)
    beyond_fade = jnp.where(near > 0, jnp.exp(-jnp.maximum(place - shard_rows, 0.0) * rates), 0.0)
    ahead_one, ahead_two = jnp.exp(rates), jnp.exp(2.0 * rates)
    edge = got_ref[8:16, :]
    before = jnp.where(near == 0, edge, near_ref[8:16, :])
    gate = gate_of(row_ref[8:16, :], edge)
    opening = first * gate[0:1] + second * gate[1:2]
    carry = got_ref[0:8, :]
    state = near_ref[0:8, :] + place_fade * carry + beyond_fade * opening
    gate = gate_of(keep_ref[3 * rows : 3 * rows + 8, :], before)
    state = state + ahead_one * gate[0:1] + ahead_two * gate[1:2]

    left = lanes_of((1, width)) < width // 2
    other = swap(state)
    whole = jnp.concatenate([jnp.where(left, state, other), jnp.where(left, other, state)], axis=0)
    whole = jnp.where(left, whole, swap(keep_ref[3 * rows + 8 : 3 * rows + 8 + poles, :]) + half_decay * whole)
    states = [jnp.broadcast_to(whole[r : r + 1], (STEP, width)) * outof[r] for r in range(poles)]
    steps = []
    for k in range(rows // STEP):
        at = k * STEP
        qk = keep_ref[at : at + STEP, :]
        xk = keep_ref[rows + at : rows + at + STEP, :]
        yk = keep_ref[2 * rows + at : 2 * rows + at + STEP, :]
        if k == 0:
            inner = rows_of((STEP, width))
            top = jnp.logical_and(left, inner == 0)
            next_ = jnp.logical_and(left, inner == 1)
            xk = jnp.where(top, gate[0:1], jnp.where(next_, gate[1:2], xk))
            yk = yk - jnp.where(top, ahead * gate[1:2], 0.0)
            q_edge = before[4:5]
            qk = qk + jnp.where(top, q_edge, jnp.where(next_, swap(q_edge), 0.0))
        for r in range(poles):
            yk = yk + states[r]
            states[r] = states[r] * fade[r]
        steps.append(qk * (yk + skip * xk))
    mixed = jnp.concatenate(steps, axis=0).T
    out_ref[:, :rows] = mixed[: width // 2].astype(out_ref.dtype)
    out_ref[:, rows:] = mixed[width // 2 :].astype(out_ref.dtype)


def finish(shard_rows, row, got, near, keep):
    width = keep.shape[1]
    return pl.pallas_call(
        functools.partial(finish_kernel, shard_rows),
        out_shape=jax.ShapeDtypeStruct((width // 2, shard_rows), jnp.bfloat16),
        compiler_params=ROOMY,
        name="finish",
    )(in_vmem(row), in_vmem(got), in_vmem(near), in_vmem(keep))


def moved_kernel(source_ref, target_ref):
    target_ref[...] = source_ref[...]


def moved(array):
    return pl.pallas_call(
        moved_kernel, out_shape=pltpu.VMEM(array.shape, F32), compiler_params=ROOMY, name="moved"
    )(in_vmem(array))


def nothing(*shapes):
    return pl.pallas_call(
        lambda *refs: None,
        out_shape=tuple(pltpu.VMEM(shape, F32) for shape in shapes),
        name="nothing",
    )()


def per_device(tokens, in_weight, short_weight, residue, rates, skip):
    shard_rows = tokens.shape[0]
    residue, rates, skip = residue.T, rates.T, skip[None, :]
    weight = in_weight.transpose(1, 0, 2)
    far, far_count = lax.axis_index("far"), lax.axis_size("far")

    def row_of_shards():
        parts = lax.all_to_all(project(tokens, weight), "chan", 0, 0, tiled=True)
        send, keep = local(parts, short_weight, residue, rates, skip)
        row, near = near_sums(lax.all_to_all(send, "near", 0, 0, tiled=True), rates, shard_rows)
        return row, near, keep

    shapes = [a.shape for a in jax.eval_shape(row_of_shards)]

    def work_of(mine):
        return lax.cond(mine, row_of_shards, lambda: nothing(*shapes))

    none = jnp.zeros(shapes[0], F32)
    chained = jnp.logical_and(far > 0, far % 2 == 0)
    row, near, keep = work_of(jnp.logical_not(chained))
    total = first_sum(shard_rows, row, near)
    again = total
    after = none
    results = [None]

    def hand_on(after, total, k):
        here = jnp.logical_or(far == k, far == k + 1)
        return lax.cond(here, lambda: moved(lax.ppermute(total, "far", [(k, k + 1)])), lambda: moved(after))

    for k in range(2, far_count, 2):

        sums = 2 if k + 2 < far_count else 1

        def even_row(k=k, total=total, sums=sums):
            sources = [lax.ppermute(total, "far", [(k - 2, k)]), lax.ppermute(row, "far", [(k - 1, k)])]
            return hop(shard_rows, sums, sources, *work_of(far == k))

        here = jnp.logical_and(far <= k, far >= k - 2)
        out = lax.cond(here, even_row, lambda sums=sums: nothing(*shapes[:1] * (sums + 1), *shapes))
        results.append((out[sums + 1], out[sums], *out[sums + 2 :]))
        again, *out = lax.optimization_barrier((again, *out))
        after = hand_on(after, again, k - 2)
        total, again = out[0], out[sums - 1]
    after = hand_on(after, again, far_count - 2)
    results[0] = (row, jnp.where(far == 0, none, after), near, keep)
    branches = [lambda r=r: finish(shard_rows, *r) for r in results]
    return lax.switch(jnp.where(chained, far // 2, 0), branches).T


def solution(mesh):
    seq, chan = mesh.devices.shape
    mesh = Mesh(mesh.devices.reshape(seq // NEAR, NEAR, chan), ("far", "near", "chan"))
    whole = ("far", "near")
    in_specs = (
        P(whole, "chan"),
        P("chan", None, None),
        P(None, None, "chan"),
        P("chan", None),
        P("chan", None),
        P("chan"),
    )
    return jax.shard_map(
        per_device, mesh=mesh, in_specs=in_specs, out_specs=P(whole, "chan"), check_vma=False
    )
```

```python
import functools

import jax
import jax.numpy as jnp
from jax import lax
from jax.experimental import pallas as pl
from jax.experimental.pallas import tpu as pltpu
from jax.sharding import Mesh, PartitionSpec as P

NEAR = 16
STEP = 8
F32 = jnp.float32
HBM = pl.BlockSpec(memory_space=pl.ANY)
ROOMY = pltpu.CompilerParams(vmem_limit_bytes=24 * 2**20)


def in_vmem(array):
    return pltpu.with_memory_space_constraint(array, pltpu.VMEM)


def in_hbm(array):
    return pltpu.with_memory_space_constraint(array, pltpu.HBM)


def lanes_of(shape):
    return lax.broadcasted_iota(jnp.int32, shape, 1)


def rows_of(shape):
    return lax.broadcasted_iota(jnp.int32, shape, 0)


def swap(tile):
    return pltpu.roll(tile, tile.shape[1] // 2, 1)


def twice(row):
    return jnp.concatenate([row, row], axis=1)


def folded(poles):
    half = poles.shape[0] // 2
    return jnp.concatenate([poles[:half], poles[half:]], axis=1)


def project_kernel(tok_hbm, w_hbm, out_ref, tok_ref, w_ref, acc_ref, sems):
    streams, depth, _ = w_ref.shape
    pieces = sems.shape[0]
    deep = depth // pieces
    parts = [pl.ds(i * deep, deep) for i in range(pieces)]
    copies = []
    for i, part in enumerate(parts):
        copies.append([pltpu.make_async_copy(tok_hbm.at[:, part], tok_ref.at[:, part], sems.at[i, streams])])
        for s in range(streams):
            copies[i].append(pltpu.make_async_copy(w_hbm.at[s, part], w_ref.at[s, part], sems.at[i, s]))
    for piece in copies:
        for copy in piece:
            copy.start()
    for i, part in enumerate(parts):
        for copy in copies[i]:
            copy.wait()
        for s in range(streams):
            term = jnp.dot(tok_ref[:, part], w_ref[s, part, :], preferred_element_type=F32)
            acc_ref[s] = term if i == 0 else acc_ref[s] + term
    rows = acc_ref.shape[1] // 2
    for s in range(streams):
        for pair in range(acc_ref.shape[2] // 128):
            early = acc_ref[s, :rows, 128 * pair : 128 * (pair + 1)]
            late = acc_ref[s, rows:, 128 * pair : 128 * (pair + 1)]
            left = lanes_of(early.shape) < 64
            out_ref[2 * pair, s] = jnp.where(left, early, swap(late))
            out_ref[2 * pair + 1, s] = jnp.where(left, swap(early), late)


def project(tokens, weight):
    rows, depth = tokens.shape
    streams, _, width = weight.shape
    chan = width // 64
    pieces = 4
    return pl.pallas_call(
        project_kernel,
        in_specs=[HBM, HBM],
        out_shape=pltpu.VMEM((chan, streams, rows // 2, 128), F32),
        scratch_shapes=[
            pltpu.VMEM(tokens.shape, tokens.dtype),
            pltpu.VMEM(weight.shape, weight.dtype),
            pltpu.VMEM((streams, rows, width), F32),
            pltpu.SemaphoreType.DMA((pieces, streams + 1)),
        ],
        compiler_params=ROOMY,
        name="project",
    )(in_hbm(tokens), in_hbm(weight))


def local_kernel(part_ref, short_ref, residue_ref, rates_ref, skip_ref, send_ref, keep_ref):
    count = part_ref.shape[0]
    rows, width = part_ref.shape[2:]
    right = lanes_of((1, width)) >= width // 2
    row = rows_of((rows, width))
    feats, edges = [], []
    for s in range(3):
        p = part_ref[0, s]
        for i in range(1, count):
            p = p + part_ref[i, s]
        tap = [twice(short_ref[k, s : s + 1, :]) for k in range(3)]
        before = jnp.where(right, swap(p[rows - 8 :]), 0.0)
        one = jnp.where(row < 1, before[7:8], pltpu.roll(p, 1, 0))
        two = pltpu.roll(p, 2, 0)
        two = jnp.where(row == 0, before[6:7], jnp.where(row == 1, before[7:8], two))
        feats.append(tap[0] * p + tap[1] * one + tap[2] * two)
        edges.append((tap[1] * p[rows - 1 :] + tap[2] * p[rows - 2 : rows - 1], tap[2] * p[rows - 1 :]))
    q, a, b = feats
    keep_ref[0:rows, :] = q
    x = jnp.where(jnp.logical_and(row < 2, jnp.logical_not(right)), 0.0, a * b)
    keep_ref[rows : 2 * rows, :] = x
    tile = [
        jnp.where(right, swap(b[0:1]), a[0:1]),
        jnp.where(right, swap(b[1:2]), a[1:2]),
        jnp.where(right, edges[2][0], swap(edges[1][0])),
        jnp.where(right, edges[2][1], swap(edges[1][1])),
        jnp.where(right, edges[0][1], swap(edges[0][0])),
    ]
    own = jnp.concatenate(tile + [jnp.zeros((3, width), F32)], axis=0)
    keep_ref[2 * rows : 2 * rows + 8, :] = own

    rates = twice(rates_ref[...])
    weight = twice(residue_ref[...]) * jnp.sqrt(2.0 * rates)
    poles = rates.shape[0]
    at = 2 * rows + 8 + poles
    keep_ref[at : at + poles, :] = rates
    keep_ref[at + poles : at + 2 * poles, :] = weight
    keep_ref[at + 2 * poles :, :] = jnp.broadcast_to(twice(skip_ref[...]), (8, width))
    step_pos = rows_of((STEP, width)).astype(F32)
    decay = jnp.exp(-float(STEP) * rates)
    half = []
    for r in range(poles):
        sums = x[:STEP]
        for k in range(1, rows // STEP):
            sums = sums * decay[r : r + 1] + x[k * STEP : (k + 1) * STEP]
        into = jnp.exp(-rates[r : r + 1] * (STEP - 1.0 - step_pos))
        half.append(jnp.sum(into * sums, axis=0, keepdims=True))
    half = jnp.concatenate(half, axis=0)
    keep_ref[2 * rows + 8 : at, :] = half
    total = half + jnp.exp(-float(rows) * rates) * swap(half)
    h = poles // 2
    packed = jnp.where(right, total[h:], swap(total[:h]))
    for i in range(send_ref.shape[0]):
        send_ref[i, 0:8, :] = packed
        send_ref[i, 8:16, :] = own


def within_kernel(keep_ref, *outs):
    *kept_refs, y_ref = outs
    for ref in kept_refs:
        ref[...] = keep_ref[...]
    rows, width = y_ref.shape
    poles = (keep_ref.shape[0] - 2 * rows - 16) // 3
    at = 2 * rows + 8 + poles
    rates = keep_ref[at : at + poles, :]
    weight = keep_ref[at + poles : at + 2 * poles, :]
    inner = rows_of((STEP, width))
    step_pos = inner.astype(F32)
    impulse = [jnp.sum(weight * jnp.exp(-rates * float(u)), axis=0, keepdims=True) for u in range(STEP)]
    near = [jnp.where(inner >= u, impulse[u], 0.0) for u in range(STEP)]
    decay = jnp.exp(-float(STEP) * rates)
    into, outof, fade = [], [], []
    for r in range(poles):
        rate = rates[r : r + 1]
        into.append(jnp.exp(-rate * (STEP - 1.0 - step_pos)))
        outof.append(weight[r : r + 1] * jnp.exp(-rate * (step_pos + 1.0)))
        fade.append(decay[r : r + 1])
    state = [None] * poles
    for k in range(rows // STEP):
        xk = keep_ref[rows + k * STEP : rows + (k + 1) * STEP, :]
        yk = near[0] * xk
        for u in range(1, STEP):
            yk = yk + near[u] * pltpu.roll(xk, u, 0)
        for r in range(poles):
            gain = jnp.sum(into[r] * xk, axis=0, keepdims=True)
            if k > 0:
                yk = yk + outof[r] * state[r]
                gain = gain + fade[r] * state[r]
            state[r] = gain
        y_ref[k * STEP : (k + 1) * STEP, :] = yk


def within(keep, rows, both):
    outs = (pltpu.VMEM(keep.shape, F32),) * both + (pltpu.VMEM((rows, keep.shape[1]), F32),)
    return pl.pallas_call(within_kernel, out_shape=outs, compiler_params=ROOMY, name="within")(in_vmem(keep))


def local(parts, short_weight, residue, rates, skip):
    _, _, rows, width = parts.shape
    return pl.pallas_call(
        local_kernel,
        out_shape=(
            pltpu.VMEM((NEAR, 16, width), F32),
            pltpu.VMEM((2 * rows + 16 + 3 * rates.shape[0], width), F32),
        ),
        compiler_params=ROOMY,
        name="local",
    )(in_vmem(parts), in_vmem(short_weight), in_vmem(residue), in_vmem(rates), in_vmem(skip))


def gate_of(tile, before):
    a = tile[0:2]
    if before is not None:
        a = a + before[2:4]
    return a * swap(a)


def near_kernel(shard_rows, got_ref, rates_ref, send_ref, keep_ref):
    near = lax.axis_index("near")
    rates = folded(rates_ref[...])
    fade = jnp.exp(-float(shard_rows) * rates)
    first = jnp.exp(-(shard_rows - 1.0) * rates)
    second = jnp.exp(-(shard_rows - 2.0) * rates)
    total = got_ref[0, 0:8, :]
    prefix = jnp.where(near > 0, total, 0.0)
    before = jnp.zeros_like(total)
    for i in range(1, NEAR):
        edge = got_ref[i - 1, 8:16, :]
        gate = gate_of(got_ref[i, 8:16, :], edge)
        grown = total * fade + (got_ref[i, 0:8, :] + first * gate[0:1] + second * gate[1:2])
        before = jnp.where(near == i, edge, before)
        total = grown
        prefix = jnp.where(near > i, grown, prefix)
    keep_ref[0:8, :] = prefix
    keep_ref[8:16, :] = before
    keep_ref[16:24, :] = rates
    head = got_ref[0, 8:16, :]
    tail = got_ref[NEAR - 1, 8:16, :]
    ends = jnp.where(rows_of(head.shape) < 2, head, tail)
    send_ref[0:8, :] = total
    send_ref[8:16, :] = ends


def near_sums(got, rates, shard_rows):
    width = got.shape[2]
    return pl.pallas_call(
        functools.partial(near_kernel, shard_rows),
        out_shape=(pltpu.VMEM((16, width), F32), pltpu.VMEM((24, width), F32)),
        compiler_params=ROOMY,
        name="near_sums",
    )(in_vmem(got), in_vmem(rates))


def with_row(shard_rows, row, got, rates):
    gate = gate_of(row[8:16], got[8:16])
    start = jnp.exp(-(shard_rows - 1.0) * rates) * gate[0:1] + jnp.exp(-(shard_rows - 2.0) * rates) * gate[1:2]
    state = row[0:8] + jnp.exp(-float((NEAR - 1) * shard_rows) * rates) * start
    state = state + jnp.exp(-float(NEAR * shard_rows) * rates) * got[0:8]
    return jnp.concatenate([state, row[8:16]], axis=0)


def first_kernel(shard_rows, row_ref, near_ref, total_ref):
    total_ref[...] = with_row(shard_rows, row_ref[...], jnp.zeros(row_ref.shape, F32), near_ref[16:24, :])


def first_sum(shard_rows, row, near):
    return pl.pallas_call(
        functools.partial(first_kernel, shard_rows),
        out_shape=pltpu.VMEM(row.shape, F32),
        compiler_params=ROOMY,
        name="first_sum",
    )(in_vmem(row), in_vmem(near))


def hop_kernel(shard_rows, sums, sources, *refs):
    kept = (len(refs) - sources - sums - 1) // 2
    rows_before, work_refs, refs = refs[:sources], refs[sources : sources + kept], refs[sources + kept :]
    sum_refs, before_ref, work_outs = refs[:sums], refs[sums], refs[sums + 1 :]
    row_ref, near_ref = work_refs[:2]
    rates = near_ref[16:24, :]
    before = rows_before[0][...]
    if sources > 1:
        before = with_row(shard_rows, rows_before[1][...], before, rates)
    before_ref[...] = before
    if sums:
        total = with_row(shard_rows, row_ref[...], before, rates)
    for ref in sum_refs:
        ref[...] = total
    for ref, out in zip(work_refs, work_outs):
        out[...] = ref[...]


def hop(shard_rows, sums, sources, row, *rest):
    operands = [in_vmem(a) for a in (*sources, row, *rest)]
    outs = (row,) * (sums + 2) + rest
    return pl.pallas_call(
        functools.partial(hop_kernel, shard_rows, sums, len(sources)),
        out_shape=tuple(pltpu.VMEM(a.shape, F32) for a in outs),
        compiler_params=ROOMY,
        name="hop",
    )(*operands)


def finish_kernel(shard_rows, row_ref, got_ref, near_ref, keep_ref, y_ref, out_ref):
    near = lax.axis_index("near")
    rows, width = out_ref.shape[1] // 2, keep_ref.shape[1]
    poles = 2 * near_ref[16:24, :].shape[0]
    at = 2 * rows + 8 + poles
    rates = keep_ref[at : at + poles, :]
    weight = keep_ref[at + poles : at + 2 * poles, :]
    skip = keep_ref[at + 2 * poles : at + 2 * poles + 1, :]
    step_pos = rows_of((STEP, width)).astype(F32)
    decay = jnp.exp(-float(STEP) * rates)
    half_decay = jnp.exp(-float(rows) * rates)
    ahead = jnp.sum(weight * jnp.exp(rates), axis=0, keepdims=True)
    outof, fade = [], []
    for r in range(poles):
        outof.append(weight[r : r + 1] * jnp.exp(-rates[r : r + 1] * (step_pos + 1.0)))
        fade.append(jnp.broadcast_to(decay[r : r + 1], (STEP, width)))

    rates = near_ref[16:24, :]
    first = jnp.exp(-(shard_rows - 1.0) * rates)
    second = jnp.exp(-(shard_rows - 2.0) * rates)
    place = near.astype(F32) * float(shard_rows)
    place_fade = jnp.exp(-place * rates)
    beyond_fade = jnp.where(near > 0, jnp.exp(-jnp.maximum(place - shard_rows, 0.0) * rates), 0.0)
    ahead_one, ahead_two = jnp.exp(rates), jnp.exp(2.0 * rates)
    edge = got_ref[8:16, :]
    before = jnp.where(near == 0, edge, near_ref[8:16, :])
    gate = gate_of(row_ref[8:16, :], edge)
    opening = first * gate[0:1] + second * gate[1:2]
    carry = got_ref[0:8, :]
    state = near_ref[0:8, :] + place_fade * carry + beyond_fade * opening
    gate = gate_of(keep_ref[2 * rows : 2 * rows + 8, :], before)
    state = state + ahead_one * gate[0:1] + ahead_two * gate[1:2]

    left = lanes_of((1, width)) < width // 2
    other = swap(state)
    whole = jnp.concatenate([jnp.where(left, state, other), jnp.where(left, other, state)], axis=0)
    whole = jnp.where(left, whole, swap(keep_ref[2 * rows + 8 : 2 * rows + 8 + poles, :]) + half_decay * whole)
    states = [jnp.broadcast_to(whole[r : r + 1], (STEP, width)) * outof[r] for r in range(poles)]
    steps = []
    for k in range(rows // STEP):
        at = k * STEP
        qk = keep_ref[at : at + STEP, :]
        xk = keep_ref[rows + at : rows + at + STEP, :]
        yk = y_ref[at : at + STEP, :]
        if k == 0:
            inner = rows_of((STEP, width))
            top = jnp.logical_and(left, inner == 0)
            next_ = jnp.logical_and(left, inner == 1)
            xk = jnp.where(top, gate[0:1], jnp.where(next_, gate[1:2], xk))
            yk = yk - jnp.where(top, ahead * gate[1:2], 0.0)
            q_edge = before[4:5]
            qk = qk + jnp.where(top, q_edge, jnp.where(next_, swap(q_edge), 0.0))
        for r in range(poles):
            yk = yk + states[r]
            states[r] = states[r] * fade[r]
        steps.append(qk * (yk + skip * xk))
    mixed = jnp.concatenate(steps, axis=0).T
    out_ref[:, :rows] = mixed[: width // 2].astype(out_ref.dtype)
    out_ref[:, rows:] = mixed[width // 2 :].astype(out_ref.dtype)


def finish(shard_rows, row, got, near, keep, y=None):
    width = keep.shape[1]
    if y is None:
        (y,) = within(keep, shard_rows // 2, False)
    return pl.pallas_call(
        functools.partial(finish_kernel, shard_rows),
        out_shape=jax.ShapeDtypeStruct((width // 2, shard_rows), jnp.bfloat16),
        compiler_params=ROOMY,
        name="finish",
    )(in_vmem(row), in_vmem(got), in_vmem(near), in_vmem(keep), in_vmem(y))


def moved_kernel(source_ref, target_ref):
    target_ref[...] = source_ref[...]


def moved(array):
    return pl.pallas_call(
        moved_kernel, out_shape=pltpu.VMEM(array.shape, F32), compiler_params=ROOMY, name="moved"
    )(in_vmem(array))


def nothing(*shapes):
    return pl.pallas_call(
        lambda *refs: None,
        out_shape=tuple(pltpu.VMEM(shape, F32) for shape in shapes),
        name="nothing",
    )()


def crossed(source, target):
    return [(source * NEAR + i, target * NEAR + (i ^ 1)) for i in range(NEAR)]


def per_device(tokens, in_weight, short_weight, residue, rates, skip):
    shard_rows = tokens.shape[0]
    residue, rates, skip = residue.T, rates.T, skip[None, :]
    weight = in_weight.transpose(1, 0, 2)
    far, far_count = lax.axis_index("far"), lax.axis_size("far")

    def row_of_shards(full):
        parts = lax.all_to_all(project(tokens, weight), "chan", 0, 0, tiled=True)
        send, keep = local(parts, short_weight, residue, rates, skip)
        row, near = near_sums(lax.all_to_all(send, "near", 0, 0, tiled=True), rates, shard_rows)
        if not full:
            return row, near, keep
        row, keep = lax.optimization_barrier((row, keep))
        return row, near, *within(keep, shard_rows // 2, True)

    shapes = [a.shape for a in jax.eval_shape(lambda: row_of_shards(True))]

    def work_of(mine, full=True):
        return lax.cond(mine, lambda: row_of_shards(full), lambda: nothing(*shapes[: 3 + full]))

    none = jnp.zeros(shapes[0], F32)
    chained = jnp.logical_and(far > 0, far % 2 == 0)
    row, near, keep = work_of(jnp.logical_not(chained), False)
    total = first_sum(shard_rows, row, near)
    again = total
    after = none
    results = [None]

    def hand_on(after, total, k):
        here = jnp.logical_or(far == k, far == k + 1)
        return lax.cond(here, lambda: moved(lax.ppermute(total, "far", [(k, k + 1)])), lambda: moved(after))

    for k in range(2, far_count, 2):

        sums = 2 if k + 2 < far_count else 1
        full = k > 2

        def even_row(k=k, total=total, sums=sums, full=full):
            sources = [lax.ppermute(total, ("far", "near"), crossed(k - 2, k)), lax.ppermute(row, "far", [(k - 1, k)])]
            return hop(shard_rows, sums, sources, *work_of(far == k, full))

        here = jnp.logical_and(far <= k, far >= k - 2)
        out = lax.cond(here, even_row, lambda sums=sums, full=full: nothing(*shapes[:1] * (sums + 1), *shapes[: 3 + full]))
        results.append((out[sums + 1], out[sums], *out[sums + 2 :]))
        again, *out = lax.optimization_barrier((again, *out))
        if k == 2:
            keep, again = lax.optimization_barrier((keep, again))
            kept = lax.cond(
                chained,
                lambda: nothing(shapes[2], shapes[3]),
                lambda: within(keep, shard_rows // 2, True),
            )
            again, *kept = lax.optimization_barrier((again, *kept))
        after = hand_on(after, again, k - 2)
        total, again = out[0], out[sums - 1]
    after = hand_on(after, again, far_count - 2)
    results[0] = (row, jnp.where(far == 0, none, after), near, *kept)
    branches = [lambda r=r: finish(shard_rows, *r) for r in results]
    return lax.switch(jnp.where(chained, far // 2, 0), branches).T


def solution(mesh):
    seq, chan = mesh.devices.shape
    mesh = Mesh(mesh.devices.reshape(seq // NEAR, NEAR, chan), ("far", "near", "chan"))
    whole = ("far", "near")
    in_specs = (
        P(whole, "chan"),
        P("chan", None, None),
        P(None, None, "chan"),
        P("chan", None),
        P("chan", None),
        P("chan"),
    )
    return jax.shard_map(
        per_device, mesh=mesh, in_specs=in_specs, out_specs=P(whole, "chan"), check_vma=False
    )
```

```python
import functools

import jax
import jax.numpy as jnp
from jax import lax
from jax.experimental import pallas as pl
from jax.experimental.pallas import tpu as pltpu
from jax.sharding import Mesh, PartitionSpec as P

NEAR = 16
STEP = 8
F32 = jnp.float32
HBM = pl.BlockSpec(memory_space=pl.ANY)
ROOMY = pltpu.CompilerParams(vmem_limit_bytes=24 * 2**20)


def in_vmem(array):
    return pltpu.with_memory_space_constraint(array, pltpu.VMEM)


def in_hbm(array):
    return pltpu.with_memory_space_constraint(array, pltpu.HBM)


def lanes_of(shape):
    return lax.broadcasted_iota(jnp.int32, shape, 1)


def rows_of(shape):
    return lax.broadcasted_iota(jnp.int32, shape, 0)


def swap(tile):
    return pltpu.roll(tile, tile.shape[1] // 2, 1)


def twice(row):
    return jnp.concatenate([row, row], axis=1)


def folded(poles):
    half = poles.shape[0] // 2
    return jnp.concatenate([poles[:half], poles[half:]], axis=1)


def project_kernel(tok_hbm, w_hbm, out_ref, tok_ref, w_ref, acc_ref, sems):
    streams, depth, _ = w_ref.shape
    pieces = sems.shape[0]
    deep = depth // pieces
    parts = [pl.ds(i * deep, deep) for i in range(pieces)]
    copies = []
    for i, part in enumerate(parts):
        copies.append([pltpu.make_async_copy(tok_hbm.at[:, part], tok_ref.at[:, part], sems.at[i, streams])])
        for s in range(streams):
            copies[i].append(pltpu.make_async_copy(w_hbm.at[s, part], w_ref.at[s, part], sems.at[i, s]))
    for piece in copies:
        for copy in piece:
            copy.start()
    for i, part in enumerate(parts):
        for copy in copies[i]:
            copy.wait()
        for s in range(streams):
            term = jnp.dot(tok_ref[:, part], w_ref[s, part, :], preferred_element_type=F32)
            acc_ref[s] = term if i == 0 else acc_ref[s] + term
    rows = acc_ref.shape[1] // 2
    for s in range(streams):
        for pair in range(acc_ref.shape[2] // 128):
            early = acc_ref[s, :rows, 128 * pair : 128 * (pair + 1)]
            late = acc_ref[s, rows:, 128 * pair : 128 * (pair + 1)]
            left = lanes_of(early.shape) < 64
            out_ref[2 * pair, s] = jnp.where(left, early, swap(late))
            out_ref[2 * pair + 1, s] = jnp.where(left, swap(early), late)


def project(tokens, weight):
    rows, depth = tokens.shape
    streams, _, width = weight.shape
    chan = width // 64
    pieces = 4
    return pl.pallas_call(
        project_kernel,
        in_specs=[HBM, HBM],
        out_shape=pltpu.VMEM((chan, streams, rows // 2, 128), F32),
        scratch_shapes=[
            pltpu.VMEM(tokens.shape, tokens.dtype),
            pltpu.VMEM(weight.shape, weight.dtype),
            pltpu.VMEM((streams, rows, width), F32),
            pltpu.SemaphoreType.DMA((pieces, streams + 1)),
        ],
        compiler_params=ROOMY,
        name="project",
    )(in_hbm(tokens), in_hbm(weight))


def local_kernel(part_ref, short_ref, residue_ref, rates_ref, skip_ref, send_ref, keep_ref):
    count = part_ref.shape[0]
    rows, width = part_ref.shape[2:]
    right = lanes_of((1, width)) >= width // 2
    row = rows_of((rows, width))
    feats, edges = [], []
    for s in range(3):
        p = part_ref[0, s]
        for i in range(1, count):
            p = p + part_ref[i, s]
        tap = [twice(short_ref[k, s : s + 1, :]) for k in range(3)]
        before = jnp.where(right, swap(p[rows - 8 :]), 0.0)
        one = jnp.where(row < 1, before[7:8], pltpu.roll(p, 1, 0))
        two = pltpu.roll(p, 2, 0)
        two = jnp.where(row == 0, before[6:7], jnp.where(row == 1, before[7:8], two))
        feats.append(tap[0] * p + tap[1] * one + tap[2] * two)
        edges.append((tap[1] * p[rows - 1 :] + tap[2] * p[rows - 2 : rows - 1], tap[2] * p[rows - 1 :]))
    q, a, b = feats
    keep_ref[0:rows, :] = q
    x = jnp.where(jnp.logical_and(row < 2, jnp.logical_not(right)), 0.0, a * b)
    keep_ref[rows : 2 * rows, :] = x
    tile = [
        jnp.where(right, swap(b[0:1]), a[0:1]),
        jnp.where(right, swap(b[1:2]), a[1:2]),
        jnp.where(right, edges[2][0], swap(edges[1][0])),
        jnp.where(right, edges[2][1], swap(edges[1][1])),
        jnp.where(right, edges[0][1], swap(edges[0][0])),
    ]
    own = jnp.concatenate(tile + [jnp.zeros((3, width), F32)], axis=0)
    keep_ref[2 * rows : 2 * rows + 8, :] = own

    rates = twice(rates_ref[...])
    weight = twice(residue_ref[...]) * jnp.sqrt(2.0 * rates)
    poles = rates.shape[0]
    at = 2 * rows + 8 + poles
    keep_ref[at : at + poles, :] = rates
    keep_ref[at + poles : at + 2 * poles, :] = weight
    keep_ref[at + 2 * poles :, :] = jnp.broadcast_to(twice(skip_ref[...]), (8, width))
    step_pos = rows_of((STEP, width)).astype(F32)
    decay = jnp.exp(-float(STEP) * rates)
    half = []
    for r in range(poles):
        sums = x[:STEP]
        for k in range(1, rows // STEP):
            sums = sums * decay[r : r + 1] + x[k * STEP : (k + 1) * STEP]
        into = jnp.exp(-rates[r : r + 1] * (STEP - 1.0 - step_pos))
        half.append(jnp.sum(into * sums, axis=0, keepdims=True))
    half = jnp.concatenate(half, axis=0)
    keep_ref[2 * rows + 8 : at, :] = half
    total = half + jnp.exp(-float(rows) * rates) * swap(half)
    h = poles // 2
    packed = jnp.where(right, total[h:], swap(total[:h]))
    for i in range(send_ref.shape[0]):
        send_ref[i, 0:8, :] = packed
        send_ref[i, 8:16, :] = own


def within_kernel(keep_ref, *outs):
    *kept_refs, y_ref = outs
    for ref in kept_refs:
        ref[...] = keep_ref[...]
    rows, width = y_ref.shape
    poles = (keep_ref.shape[0] - 2 * rows - 16) // 3
    at = 2 * rows + 8 + poles
    rates = keep_ref[at : at + poles, :]
    weight = keep_ref[at + poles : at + 2 * poles, :]
    inner = rows_of((STEP, width))
    step_pos = inner.astype(F32)
    impulse = [jnp.sum(weight * jnp.exp(-rates * float(u)), axis=0, keepdims=True) for u in range(STEP)]
    near = [jnp.where(inner >= u, impulse[u], 0.0) for u in range(STEP)]
    decay = jnp.exp(-float(STEP) * rates)
    into, outof, fade = [], [], []
    for r in range(poles):
        rate = rates[r : r + 1]
        into.append(jnp.exp(-rate * (STEP - 1.0 - step_pos)))
        outof.append(weight[r : r + 1] * jnp.exp(-rate * (step_pos + 1.0)))
        fade.append(decay[r : r + 1])
    state = [None] * poles
    for k in range(rows // STEP):
        xk = keep_ref[rows + k * STEP : rows + (k + 1) * STEP, :]
        yk = near[0] * xk
        for u in range(1, STEP):
            yk = yk + near[u] * pltpu.roll(xk, u, 0)
        for r in range(poles):
            gain = jnp.sum(into[r] * xk, axis=0, keepdims=True)
            if k > 0:
                yk = yk + outof[r] * state[r]
                gain = gain + fade[r] * state[r]
            state[r] = gain
        y_ref[k * STEP : (k + 1) * STEP, :] = yk


def within(keep, rows, both):
    outs = (pltpu.VMEM(keep.shape, F32),) * both + (pltpu.VMEM((rows, keep.shape[1]), F32),)
    return pl.pallas_call(within_kernel, out_shape=outs, compiler_params=ROOMY, name="within")(in_vmem(keep))


def local(parts, short_weight, residue, rates, skip):
    _, _, rows, width = parts.shape
    return pl.pallas_call(
        local_kernel,
        out_shape=(
            pltpu.VMEM((NEAR, 16, width), F32),
            pltpu.VMEM((2 * rows + 16 + 3 * rates.shape[0], width), F32),
        ),
        compiler_params=ROOMY,
        name="local",
    )(in_vmem(parts), in_vmem(short_weight), in_vmem(residue), in_vmem(rates), in_vmem(skip))


def gate_of(tile, before):
    a = tile[0:2]
    if before is not None:
        a = a + before[2:4]
    return a * swap(a)


def near_kernel(shard_rows, got_ref, rates_ref, send_ref, keep_ref):
    near = lax.axis_index("near")
    rates = folded(rates_ref[...])
    fade = jnp.exp(-float(shard_rows) * rates)
    first = jnp.exp(-(shard_rows - 1.0) * rates)
    second = jnp.exp(-(shard_rows - 2.0) * rates)
    total = got_ref[0, 0:8, :]
    prefix = jnp.where(near > 0, total, 0.0)
    before = jnp.zeros_like(total)
    for i in range(1, NEAR):
        edge = got_ref[i - 1, 8:16, :]
        gate = gate_of(got_ref[i, 8:16, :], edge)
        grown = total * fade + (got_ref[i, 0:8, :] + first * gate[0:1] + second * gate[1:2])
        before = jnp.where(near == i, edge, before)
        total = grown
        prefix = jnp.where(near > i, grown, prefix)
    keep_ref[0:8, :] = prefix
    keep_ref[8:16, :] = before
    keep_ref[16:24, :] = rates
    head = got_ref[0, 8:16, :]
    tail = got_ref[NEAR - 1, 8:16, :]
    ends = jnp.where(rows_of(head.shape) < 2, head, tail)
    send_ref[0:8, :] = total
    send_ref[8:16, :] = ends


def near_sums(got, rates, shard_rows):
    width = got.shape[2]
    return pl.pallas_call(
        functools.partial(near_kernel, shard_rows),
        out_shape=(pltpu.VMEM((16, width), F32), pltpu.VMEM((24, width), F32)),
        compiler_params=ROOMY,
        name="near_sums",
    )(in_vmem(got), in_vmem(rates))


def with_row(shard_rows, row, got, rates):
    gate = gate_of(row[8:16], got[8:16])
    start = jnp.exp(-(shard_rows - 1.0) * rates) * gate[0:1] + jnp.exp(-(shard_rows - 2.0) * rates) * gate[1:2]
    state = row[0:8] + jnp.exp(-float((NEAR - 1) * shard_rows) * rates) * start
    state = state + jnp.exp(-float(NEAR * shard_rows) * rates) * got[0:8]
    return jnp.concatenate([state, row[8:16]], axis=0)


def first_kernel(shard_rows, row_ref, near_ref, total_ref):
    total_ref[...] = with_row(shard_rows, row_ref[...], jnp.zeros(row_ref.shape, F32), near_ref[16:24, :])


def first_sum(shard_rows, row, near):
    return pl.pallas_call(
        functools.partial(first_kernel, shard_rows),
        out_shape=pltpu.VMEM(row.shape, F32),
        compiler_params=ROOMY,
        name="first_sum",
    )(in_vmem(row), in_vmem(near))


def hop_kernel(shard_rows, sums, sources, *refs):
    kept = (len(refs) - sources - sums - 1) // 2
    rows_before, work_refs, refs = refs[:sources], refs[sources : sources + kept], refs[sources + kept :]
    sum_refs, before_ref, work_outs = refs[:sums], refs[sums], refs[sums + 1 :]
    row_ref, near_ref = work_refs[:2]
    rates = near_ref[16:24, :]
    before = rows_before[0][...]
    if sources > 1:
        before = with_row(shard_rows, rows_before[1][...], before, rates)
    before_ref[...] = before
    if sums:
        total = with_row(shard_rows, row_ref[...], before, rates)
    for ref in sum_refs:
        ref[...] = total
    for ref, out in zip(work_refs, work_outs):
        out[...] = ref[...]


def hop(shard_rows, sums, sources, row, *rest):
    operands = [in_vmem(a) for a in (*sources, row, *rest)]
    outs = (row,) * (sums + 2) + rest
    return pl.pallas_call(
        functools.partial(hop_kernel, shard_rows, sums, len(sources)),
        out_shape=tuple(pltpu.VMEM(a.shape, F32) for a in outs),
        compiler_params=ROOMY,
        name="hop",
    )(*operands)


def finish_kernel(shard_rows, row_ref, got_ref, near_ref, keep_ref, y_ref, out_ref):
    near = lax.axis_index("near")
    rows, width = out_ref.shape[1] // 2, keep_ref.shape[1]
    poles = 2 * near_ref[16:24, :].shape[0]
    at = 2 * rows + 8 + poles
    rates = keep_ref[at : at + poles, :]
    weight = keep_ref[at + poles : at + 2 * poles, :]
    skip = keep_ref[at + 2 * poles : at + 2 * poles + 1, :]
    step_pos = rows_of((STEP, width)).astype(F32)
    decay = jnp.exp(-float(STEP) * rates)
    half_decay = jnp.exp(-float(rows) * rates)
    ahead = jnp.sum(weight * jnp.exp(rates), axis=0, keepdims=True)
    outof, fade = [], []
    for r in range(poles):
        outof.append(weight[r : r + 1] * jnp.exp(-rates[r : r + 1] * (step_pos + 1.0)))
        fade.append(jnp.broadcast_to(decay[r : r + 1], (STEP, width)))

    rates = near_ref[16:24, :]
    first = jnp.exp(-(shard_rows - 1.0) * rates)
    second = jnp.exp(-(shard_rows - 2.0) * rates)
    place = near.astype(F32) * float(shard_rows)
    place_fade = jnp.exp(-place * rates)
    beyond_fade = jnp.where(near > 0, jnp.exp(-jnp.maximum(place - shard_rows, 0.0) * rates), 0.0)
    ahead_one, ahead_two = jnp.exp(rates), jnp.exp(2.0 * rates)
    edge = got_ref[8:16, :]
    before = jnp.where(near == 0, edge, near_ref[8:16, :])
    gate = gate_of(row_ref[8:16, :], edge)
    opening = first * gate[0:1] + second * gate[1:2]
    carry = got_ref[0:8, :]
    state = near_ref[0:8, :] + place_fade * carry + beyond_fade * opening
    gate = gate_of(keep_ref[2 * rows : 2 * rows + 8, :], before)
    state = state + ahead_one * gate[0:1] + ahead_two * gate[1:2]

    left = lanes_of((1, width)) < width // 2
    other = swap(state)
    whole = jnp.concatenate([jnp.where(left, state, other), jnp.where(left, other, state)], axis=0)
    whole = jnp.where(left, whole, swap(keep_ref[2 * rows + 8 : 2 * rows + 8 + poles, :]) + half_decay * whole)
    states = [jnp.broadcast_to(whole[r : r + 1], (STEP, width)) * outof[r] for r in range(poles)]
    steps = []
    for k in range(rows // STEP):
        at = k * STEP
        qk = keep_ref[at : at + STEP, :]
        xk = keep_ref[rows + at : rows + at + STEP, :]
        yk = y_ref[at : at + STEP, :]
        if k == 0:
            inner = rows_of((STEP, width))
            top = jnp.logical_and(left, inner == 0)
            next_ = jnp.logical_and(left, inner == 1)
            xk = jnp.where(top, gate[0:1], jnp.where(next_, gate[1:2], xk))
            yk = yk - jnp.where(top, ahead * gate[1:2], 0.0)
            q_edge = before[4:5]
            qk = qk + jnp.where(top, q_edge, jnp.where(next_, swap(q_edge), 0.0))
        for r in range(poles):
            yk = yk + states[r]
            states[r] = states[r] * fade[r]
        steps.append(qk * (yk + skip * xk))
    mixed = jnp.concatenate(steps, axis=0).T
    out_ref[:, :rows] = mixed[: width // 2].astype(out_ref.dtype)
    out_ref[:, rows:] = mixed[width // 2 :].astype(out_ref.dtype)


def finish(shard_rows, row, got, near, keep, y=None):
    width = keep.shape[1]
    if y is None:
        (y,) = within(keep, shard_rows // 2, False)
    return pl.pallas_call(
        functools.partial(finish_kernel, shard_rows),
        out_shape=jax.ShapeDtypeStruct((width // 2, shard_rows), jnp.bfloat16),
        compiler_params=ROOMY,
        name="finish",
    )(in_vmem(row), in_vmem(got), in_vmem(near), in_vmem(keep), in_vmem(y))


def nothing(*shapes):
    return pl.pallas_call(
        lambda *refs: None,
        out_shape=tuple(pltpu.VMEM(shape, F32) for shape in shapes),
        name="nothing",
    )()


def crossed(source, target):
    return [(source * NEAR + i, target * NEAR + (i ^ 1)) for i in range(NEAR)]


def per_device(tokens, in_weight, short_weight, residue, rates, skip):
    shard_rows = tokens.shape[0]
    residue, rates, skip = residue.T, rates.T, skip[None, :]
    weight = in_weight.transpose(1, 0, 2)
    far, far_count = lax.axis_index("far"), lax.axis_size("far")

    def row_of_shards(full):
        parts = lax.all_to_all(project(tokens, weight), "chan", 0, 0, tiled=True)
        send, keep = local(parts, short_weight, residue, rates, skip)
        row, near = near_sums(lax.all_to_all(send, "near", 0, 0, tiled=True), rates, shard_rows)
        if not full:
            return row, near, keep
        row, keep = lax.optimization_barrier((row, keep))
        return row, near, *within(keep, shard_rows // 2, True)

    shapes = [a.shape for a in jax.eval_shape(lambda: row_of_shards(True))]

    def work_of(mine, full=True):
        return lax.cond(mine, lambda: row_of_shards(full), lambda: nothing(*shapes[: 3 + full]))

    none = jnp.zeros(shapes[0], F32)
    even = far % 2 == 0
    row, near, keep = work_of(even, False)
    total = first_sum(shard_rows, row, near)
    after = none
    results = [None]
    for k in range(1, far_count, 2):
        sums = int(k + 1 < far_count)
        full = k != 3

        two = jnp.where(far == k - 1, row, total)

        def odd_row(k=k, total=total, two=two, sums=sums, full=full):
            block = jnp.where(far == max(k - 2, 0), total, none)
            sources = [lax.ppermute(block, ("far", "near"), crossed(max(k - 2, 0), k))]
            extra = []
            if k > 1:
                steps = crossed(k - 2, k - 1) + crossed(k - 1, k)
                extra = [lax.ppermute(two, ("far", "near"), steps)]
                sources += extra
            return hop(shard_rows, sums, sources, *work_of(far == k, full), *extra)

        here = jnp.logical_and(far <= k, far >= k - 2)
        outs = shapes[:1] * (sums + 1) + shapes[: 3 + full] + shapes[:1] * (k > 1)
        out = lax.cond(here, odd_row, lambda outs=outs: nothing(*outs))
        results.append((out[sums + 1], out[sums], *out[sums + 2 : sums + 4 + full]))
        if k > 1:
            after = jnp.where(far == k - 1, out[-1], after)
        if k == 3:
            keep, *out = lax.optimization_barrier((keep, *out))
            kept = lax.cond(
                even, lambda: within(keep, shard_rows // 2, True), lambda: nothing(shapes[2], shapes[3])
            )
            *out, kept0, kept1 = lax.optimization_barrier((*out, *kept))
            kept = (kept0, kept1)
        total = out[0]
    results[0] = (row, after, near, *kept)
    branches = [lambda r=r: finish(shard_rows, *r) for r in results]
    return lax.switch(jnp.where(even, 0, (far + 1) // 2), branches).T


def solution(mesh):
    seq, chan = mesh.devices.shape
    mesh = Mesh(mesh.devices.reshape(seq // NEAR, NEAR, chan), ("far", "near", "chan"))
    whole = ("far", "near")
    in_specs = (
        P(whole, "chan"),
        P("chan", None, None),
        P(None, None, "chan"),
        P("chan", None),
        P("chan", None),
        P("chan"),
    )
    return jax.shard_map(
        per_device, mesh=mesh, in_specs=in_specs, out_specs=P(whole, "chan"), check_vma=False
    )
```

```python
import functools

import jax
import jax.numpy as jnp
from jax import lax
from jax.experimental import pallas as pl
from jax.experimental.pallas import tpu as pltpu
from jax.sharding import Mesh, PartitionSpec as P

NEAR = 16
STEP = 8
F32 = jnp.float32
HBM = pl.BlockSpec(memory_space=pl.ANY)
ROOMY = pltpu.CompilerParams(vmem_limit_bytes=24 * 2**20)


def in_vmem(array):
    return pltpu.with_memory_space_constraint(array, pltpu.VMEM)


def in_hbm(array):
    return pltpu.with_memory_space_constraint(array, pltpu.HBM)


def lanes_of(shape):
    return lax.broadcasted_iota(jnp.int32, shape, 1)


def rows_of(shape):
    return lax.broadcasted_iota(jnp.int32, shape, 0)


def swap(tile):
    return pltpu.roll(tile, tile.shape[1] // 2, 1)


def twice(row):
    return jnp.concatenate([row, row], axis=1)


def folded(poles):
    half = poles.shape[0] // 2
    return jnp.concatenate([poles[:half], poles[half:]], axis=1)


def project_kernel(tok_hbm, w_hbm, out_ref, tok_ref, w_ref, acc_ref, sems):
    streams, depth, _ = w_ref.shape
    pieces = sems.shape[0]
    deep = depth // pieces
    parts = [pl.ds(i * deep, deep) for i in range(pieces)]
    copies = []
    for i, part in enumerate(parts):
        copies.append([pltpu.make_async_copy(tok_hbm.at[:, part], tok_ref.at[:, part], sems.at[i, streams])])
        for s in range(streams):
            copies[i].append(pltpu.make_async_copy(w_hbm.at[s, part], w_ref.at[s, part], sems.at[i, s]))
    for piece in copies:
        for copy in piece:
            copy.start()
    for i, part in enumerate(parts):
        for copy in copies[i]:
            copy.wait()
        for s in range(streams):
            term = jnp.dot(tok_ref[:, part], w_ref[s, part, :], preferred_element_type=F32)
            acc_ref[s] = term if i == 0 else acc_ref[s] + term
    rows = acc_ref.shape[1] // 2
    for s in range(streams):
        for pair in range(acc_ref.shape[2] // 128):
            early = acc_ref[s, :rows, 128 * pair : 128 * (pair + 1)]
            late = acc_ref[s, rows:, 128 * pair : 128 * (pair + 1)]
            left = lanes_of(early.shape) < 64
            out_ref[2 * pair, s] = jnp.where(left, early, swap(late))
            out_ref[2 * pair + 1, s] = jnp.where(left, swap(early), late)


def project(tokens, weight):
    rows, depth = tokens.shape
    streams, _, width = weight.shape
    chan = width // 64
    pieces = 4
    return pl.pallas_call(
        project_kernel,
        in_specs=[HBM, HBM],
        out_shape=pltpu.VMEM((chan, streams, rows // 2, 128), F32),
        scratch_shapes=[
            pltpu.VMEM(tokens.shape, tokens.dtype),
            pltpu.VMEM(weight.shape, weight.dtype),
            pltpu.VMEM((streams, rows, width), F32),
            pltpu.SemaphoreType.DMA((pieces, streams + 1)),
        ],
        compiler_params=ROOMY,
        name="project",
    )(in_hbm(tokens), in_hbm(weight))


def local_kernel(part_ref, short_ref, residue_ref, rates_ref, skip_ref, send_ref, keep_ref):
    count = part_ref.shape[0]
    rows, width = part_ref.shape[2:]
    right = lanes_of((1, width)) >= width // 2
    row = rows_of((rows, width))
    feats, edges = [], []
    for s in range(3):
        p = part_ref[0, s]
        for i in range(1, count):
            p = p + part_ref[i, s]
        tap = [twice(short_ref[k, s : s + 1, :]) for k in range(3)]
        before = jnp.where(right, swap(p[rows - 8 :]), 0.0)
        one = jnp.where(row < 1, before[7:8], pltpu.roll(p, 1, 0))
        two = pltpu.roll(p, 2, 0)
        two = jnp.where(row == 0, before[6:7], jnp.where(row == 1, before[7:8], two))
        feats.append(tap[0] * p + tap[1] * one + tap[2] * two)
        edges.append((tap[1] * p[rows - 1 :] + tap[2] * p[rows - 2 : rows - 1], tap[2] * p[rows - 1 :]))
    q, a, b = feats
    keep_ref[0:rows, :] = q
    x = jnp.where(jnp.logical_and(row < 2, jnp.logical_not(right)), 0.0, a * b)
    keep_ref[rows : 2 * rows, :] = x
    tile = [
        jnp.where(right, swap(b[0:1]), a[0:1]),
        jnp.where(right, swap(b[1:2]), a[1:2]),
        jnp.where(right, edges[2][0], swap(edges[1][0])),
        jnp.where(right, edges[2][1], swap(edges[1][1])),
        jnp.where(right, edges[0][1], swap(edges[0][0])),
    ]
    own = jnp.concatenate(tile + [jnp.zeros((3, width), F32)], axis=0)
    keep_ref[2 * rows : 2 * rows + 8, :] = own

    rates = twice(rates_ref[...])
    weight = twice(residue_ref[...]) * jnp.sqrt(2.0 * rates)
    poles = rates.shape[0]
    at = 2 * rows + 8 + poles
    keep_ref[at : at + poles, :] = rates
    keep_ref[at + poles : at + 2 * poles, :] = weight
    keep_ref[at + 2 * poles :, :] = jnp.broadcast_to(twice(skip_ref[...]), (8, width))
    step_pos = rows_of((STEP, width)).astype(F32)
    decay = jnp.exp(-float(STEP) * rates)
    half = []
    for r in range(poles):
        sums = x[:STEP]
        for k in range(1, rows // STEP):
            sums = sums * decay[r : r + 1] + x[k * STEP : (k + 1) * STEP]
        into = jnp.exp(-rates[r : r + 1] * (STEP - 1.0 - step_pos))
        half.append(jnp.sum(into * sums, axis=0, keepdims=True))
    half = jnp.concatenate(half, axis=0)
    keep_ref[2 * rows + 8 : at, :] = half
    total = half + jnp.exp(-float(rows) * rates) * swap(half)
    h = poles // 2
    packed = jnp.where(right, total[h:], swap(total[:h]))
    block = jnp.concatenate([packed, own[0:6]], axis=0)
    for j in range(send_ref.shape[1]):
        piece = block[2 * j : 2 * j + 2]
        for i in range(send_ref.shape[0]):
            send_ref[i, j] = piece


def within_kernel(keep_ref, *outs):
    *kept_refs, y_ref = outs
    for ref in kept_refs:
        ref[...] = keep_ref[...]
    rows, width = y_ref.shape
    poles = (keep_ref.shape[0] - 2 * rows - 16) // 3
    at = 2 * rows + 8 + poles
    rates = keep_ref[at : at + poles, :]
    weight = keep_ref[at + poles : at + 2 * poles, :]
    inner = rows_of((STEP, width))
    step_pos = inner.astype(F32)
    impulse = [jnp.sum(weight * jnp.exp(-rates * float(u)), axis=0, keepdims=True) for u in range(STEP)]
    near = [jnp.where(inner >= u, impulse[u], 0.0) for u in range(STEP)]
    decay = jnp.exp(-float(STEP) * rates)
    into, outof, fade = [], [], []
    for r in range(poles):
        rate = rates[r : r + 1]
        into.append(jnp.exp(-rate * (STEP - 1.0 - step_pos)))
        outof.append(weight[r : r + 1] * jnp.exp(-rate * (step_pos + 1.0)))
        fade.append(decay[r : r + 1])
    state = [None] * poles
    for k in range(rows // STEP):
        xk = keep_ref[rows + k * STEP : rows + (k + 1) * STEP, :]
        yk = near[0] * xk
        for u in range(1, STEP):
            yk = yk + near[u] * pltpu.roll(xk, u, 0)
        for r in range(poles):
            gain = jnp.sum(into[r] * xk, axis=0, keepdims=True)
            if k > 0:
                yk = yk + outof[r] * state[r]
                gain = gain + fade[r] * state[r]
            state[r] = gain
        y_ref[k * STEP : (k + 1) * STEP, :] = yk


def within(keep, rows, both):
    outs = (pltpu.VMEM(keep.shape, F32),) * both + (pltpu.VMEM((rows, keep.shape[1]), F32),)
    return pl.pallas_call(within_kernel, out_shape=outs, compiler_params=ROOMY, name="within")(in_vmem(keep))


def local(parts, short_weight, residue, rates, skip):
    _, _, rows, width = parts.shape
    return pl.pallas_call(
        local_kernel,
        out_shape=(
            pltpu.VMEM((NEAR, 7, 2, width), F32),
            pltpu.VMEM((2 * rows + 16 + 3 * rates.shape[0], width), F32),
        ),
        compiler_params=ROOMY,
        name="local",
    )(in_vmem(parts), in_vmem(short_weight), in_vmem(residue), in_vmem(rates), in_vmem(skip))


def gate_of(tile, before):
    a = tile[0:2]
    if before is not None:
        a = a + before[2:4]
    return a * swap(a)


def near_kernel(shard_rows, got_ref, rates_ref, send_ref, keep_ref):
    near = lax.axis_index("near")
    rates = folded(rates_ref[...])
    fade = jnp.exp(-float(shard_rows) * rates)
    first = jnp.exp(-(shard_rows - 1.0) * rates)
    second = jnp.exp(-(shard_rows - 2.0) * rates)
    blank = jnp.zeros((2, got_ref.shape[3]), F32)

    def state_of(i):
        return jnp.concatenate([got_ref[i, j] for j in range(4)], axis=0)

    def tile_of(i):
        return jnp.concatenate([got_ref[i, j] for j in range(4, 7)] + [blank], axis=0)

    total = state_of(0)
    head = edge = tile_of(0)
    prefix = jnp.where(near > 0, total, 0.0)
    before = jnp.zeros_like(total)
    for i in range(1, NEAR):
        tile = tile_of(i)
        gate = gate_of(tile, edge)
        grown = total * fade + (state_of(i) + first * gate[0:1] + second * gate[1:2])
        before = jnp.where(near == i, edge, before)
        total = grown
        prefix = jnp.where(near > i, grown, prefix)
        edge = tile
    keep_ref[0:8, :] = prefix
    keep_ref[8:16, :] = before
    keep_ref[16:24, :] = rates
    ends = jnp.where(rows_of(head.shape) < 2, head, edge)
    send_ref[0:8, :] = total
    send_ref[8:16, :] = ends


def near_sums(got, rates, shard_rows):
    width = got.shape[-1]
    return pl.pallas_call(
        functools.partial(near_kernel, shard_rows),
        out_shape=(pltpu.VMEM((16, width), F32), pltpu.VMEM((24, width), F32)),
        compiler_params=ROOMY,
        name="near_sums",
    )(in_vmem(got), in_vmem(rates))


def with_row(shard_rows, row, got, rates):
    gate = gate_of(row[8:16], got[8:16])
    start = jnp.exp(-(shard_rows - 1.0) * rates) * gate[0:1] + jnp.exp(-(shard_rows - 2.0) * rates) * gate[1:2]
    state = row[0:8] + jnp.exp(-float((NEAR - 1) * shard_rows) * rates) * start
    state = state + jnp.exp(-float(NEAR * shard_rows) * rates) * got[0:8]
    return jnp.concatenate([state, row[8:16]], axis=0)


def first_kernel(shard_rows, row_ref, near_ref, total_ref):
    total_ref[...] = with_row(shard_rows, row_ref[...], jnp.zeros(row_ref.shape, F32), near_ref[16:24, :])


def first_sum(shard_rows, row, near):
    return pl.pallas_call(
        functools.partial(first_kernel, shard_rows),
        out_shape=pltpu.VMEM(row.shape, F32),
        compiler_params=ROOMY,
        name="first_sum",
    )(in_vmem(row), in_vmem(near))


def hop_kernel(shard_rows, sums, sources, *refs):
    kept = (len(refs) - sources - sums - 1) // 2
    rows_before, work_refs, refs = refs[:sources], refs[sources : sources + kept], refs[sources + kept :]
    sum_refs, before_ref, work_outs = refs[:sums], refs[sums], refs[sums + 1 :]
    row_ref, near_ref = work_refs[:2]
    rates = near_ref[16:24, :]
    before = rows_before[0][...]
    if sources > 1:
        before = with_row(shard_rows, rows_before[1][...], before, rates)
    before_ref[...] = before
    if sums:
        total = with_row(shard_rows, row_ref[...], before, rates)
    for ref in sum_refs:
        ref[...] = total
    for ref, out in zip(work_refs, work_outs):
        out[...] = ref[...]


def hop(shard_rows, sums, sources, row, *rest):
    operands = [in_vmem(a) for a in (*sources, row, *rest)]
    outs = (row,) * (sums + 2) + rest
    return pl.pallas_call(
        functools.partial(hop_kernel, shard_rows, sums, len(sources)),
        out_shape=tuple(pltpu.VMEM(a.shape, F32) for a in outs),
        compiler_params=ROOMY,
        name="hop",
    )(*operands)


def finish_kernel(shard_rows, row_ref, got_ref, near_ref, keep_ref, y_ref, out_ref):
    near = lax.axis_index("near")
    rows, width = out_ref.shape[1] // 2, keep_ref.shape[1]
    poles = 2 * near_ref[16:24, :].shape[0]
    at = 2 * rows + 8 + poles
    rates = keep_ref[at : at + poles, :]
    weight = keep_ref[at + poles : at + 2 * poles, :]
    skip = keep_ref[at + 2 * poles : at + 2 * poles + 1, :]
    step_pos = rows_of((STEP, width)).astype(F32)
    decay = jnp.exp(-float(STEP) * rates)
    half_decay = jnp.exp(-float(rows) * rates)
    ahead = jnp.sum(weight * jnp.exp(rates), axis=0, keepdims=True)
    outof, fade = [], []
    for r in range(poles):
        outof.append(weight[r : r + 1] * jnp.exp(-rates[r : r + 1] * (step_pos + 1.0)))
        fade.append(jnp.broadcast_to(decay[r : r + 1], (STEP, width)))

    rates = near_ref[16:24, :]
    first = jnp.exp(-(shard_rows - 1.0) * rates)
    second = jnp.exp(-(shard_rows - 2.0) * rates)
    place = near.astype(F32) * float(shard_rows)
    place_fade = jnp.exp(-place * rates)
    beyond_fade = jnp.where(near > 0, jnp.exp(-jnp.maximum(place - shard_rows, 0.0) * rates), 0.0)
    ahead_one, ahead_two = jnp.exp(rates), jnp.exp(2.0 * rates)
    edge = got_ref[8:16, :]
    before = jnp.where(near == 0, edge, near_ref[8:16, :])
    gate = gate_of(row_ref[8:16, :], edge)
    opening = first * gate[0:1] + second * gate[1:2]
    carry = got_ref[0:8, :]
    state = near_ref[0:8, :] + place_fade * carry + beyond_fade * opening
    gate = gate_of(keep_ref[2 * rows : 2 * rows + 8, :], before)
    state = state + ahead_one * gate[0:1] + ahead_two * gate[1:2]

    left = lanes_of((1, width)) < width // 2
    other = swap(state)
    whole = jnp.concatenate([jnp.where(left, state, other), jnp.where(left, other, state)], axis=0)
    whole = jnp.where(left, whole, swap(keep_ref[2 * rows + 8 : 2 * rows + 8 + poles, :]) + half_decay * whole)
    states = [jnp.broadcast_to(whole[r : r + 1], (STEP, width)) * outof[r] for r in range(poles)]
    steps = []
    for k in range(rows // STEP):
        at = k * STEP
        qk = keep_ref[at : at + STEP, :]
        xk = keep_ref[rows + at : rows + at + STEP, :]
        yk = y_ref[at : at + STEP, :]
        if k == 0:
            inner = rows_of((STEP, width))
            top = jnp.logical_and(left, inner == 0)
            next_ = jnp.logical_and(left, inner == 1)
            xk = jnp.where(top, gate[0:1], jnp.where(next_, gate[1:2], xk))
            yk = yk - jnp.where(top, ahead * gate[1:2], 0.0)
            q_edge = before[4:5]
            qk = qk + jnp.where(top, q_edge, jnp.where(next_, swap(q_edge), 0.0))
        for r in range(poles):
            yk = yk + states[r]
            states[r] = states[r] * fade[r]
        steps.append(qk * (yk + skip * xk))
    mixed = jnp.concatenate(steps, axis=0).T
    out_ref[:, :rows] = mixed[: width // 2].astype(out_ref.dtype)
    out_ref[:, rows:] = mixed[width // 2 :].astype(out_ref.dtype)


def finish(shard_rows, row, got, near, keep, y=None):
    width = keep.shape[1]
    if y is None:
        (y,) = within(keep, shard_rows // 2, False)
    return pl.pallas_call(
        functools.partial(finish_kernel, shard_rows),
        out_shape=jax.ShapeDtypeStruct((width // 2, shard_rows), jnp.bfloat16),
        compiler_params=ROOMY,
        name="finish",
    )(in_vmem(row), in_vmem(got), in_vmem(near), in_vmem(keep), in_vmem(y))


def nothing(*shapes):
    return pl.pallas_call(
        lambda *refs: None,
        out_shape=tuple(pltpu.VMEM(shape, F32) for shape in shapes),
        name="nothing",
    )()


def crossed(source, target):
    return [(source * NEAR + i, target * NEAR + (i ^ 1)) for i in range(NEAR)]


def per_device(tokens, in_weight, short_weight, residue, rates, skip):
    shard_rows = tokens.shape[0]
    residue, rates, skip = residue.T, rates.T, skip[None, :]
    weight = in_weight.transpose(1, 0, 2)
    far, far_count = lax.axis_index("far"), lax.axis_size("far")

    def row_of_shards(full):
        parts = lax.all_to_all(project(tokens, weight), "chan", 0, 0, tiled=True)
        send, keep = local(parts, short_weight, residue, rates, skip)
        row, near = near_sums(lax.all_to_all(send, "near", 0, 0, tiled=True), rates, shard_rows)
        if not full:
            return row, near, keep
        row, keep = lax.optimization_barrier((row, keep))
        return row, near, *within(keep, shard_rows // 2, True)

    shapes = [a.shape for a in jax.eval_shape(lambda: row_of_shards(True))]

    def work_of(mine, full=True):
        return lax.cond(mine, lambda: row_of_shards(full), lambda: nothing(*shapes[: 3 + full]))

    none = jnp.zeros(shapes[0], F32)
    even = far % 2 == 0
    row, near, keep = work_of(even, False)
    total = first_sum(shard_rows, row, near)
    after = none
    results = [None]
    for k in range(1, far_count, 2):
        sums = int(k + 1 < far_count)
        full = k != 3

        two = jnp.where(far == k - 1, row, total)

        def odd_row(k=k, total=total, two=two, sums=sums, full=full):
            block = jnp.where(far == max(k - 2, 0), total, none)
            sources = [lax.ppermute(block, ("far", "near"), crossed(max(k - 2, 0), k))]
            extra = []
            if k > 1:
                steps = crossed(k - 2, k - 1) + crossed(k - 1, k)
                extra = [lax.ppermute(two, ("far", "near"), steps)]
                sources += extra
            return hop(shard_rows, sums, sources, *work_of(far == k, full), *extra)

        here = jnp.logical_and(far <= k, far >= k - 2)
        outs = shapes[:1] * (sums + 1) + shapes[: 3 + full] + shapes[:1] * (k > 1)
        out = lax.cond(here, odd_row, lambda outs=outs: nothing(*outs))
        results.append((out[sums + 1], out[sums], *out[sums + 2 : sums + 4 + full]))
        if k > 1:
            after = jnp.where(far == k - 1, out[-1], after)
        if k == 3:
            keep, *out = lax.optimization_barrier((keep, *out))
            kept = lax.cond(
                even, lambda: within(keep, shard_rows // 2, True), lambda: nothing(shapes[2], shapes[3])
            )
            *out, kept0, kept1 = lax.optimization_barrier((*out, *kept))
            kept = (kept0, kept1)
        total = out[0]
    results[0] = (row, after, near, *kept)
    branches = [lambda r=r: finish(shard_rows, *r) for r in results]
    return lax.switch(jnp.where(even, 0, (far + 1) // 2), branches).T


def solution(mesh):
    seq, chan = mesh.devices.shape
    mesh = Mesh(mesh.devices.reshape(seq // NEAR, NEAR, chan), ("far", "near", "chan"))
    whole = ("far", "near")
    in_specs = (
        P(whole, "chan"),
        P("chan", None, None),
        P(None, None, "chan"),
        P("chan", None),
        P("chan", None),
        P("chan"),
    )
    return jax.shard_map(
        per_device, mesh=mesh, in_specs=in_specs, out_specs=P(whole, "chan"), check_vma=False
    )
```

```python
import functools

import jax
import jax.numpy as jnp
from jax import lax
from jax.experimental import pallas as pl
from jax.experimental.pallas import tpu as pltpu
from jax.sharding import Mesh, PartitionSpec as P

NEAR = 16
STEP = 8
F32 = jnp.float32
HBM = pl.BlockSpec(memory_space=pl.ANY)
ROOMY = pltpu.CompilerParams(vmem_limit_bytes=24 * 2**20)


def in_vmem(array):
    return pltpu.with_memory_space_constraint(array, pltpu.VMEM)


def in_hbm(array):
    return pltpu.with_memory_space_constraint(array, pltpu.HBM)


def lanes_of(shape):
    return lax.broadcasted_iota(jnp.int32, shape, 1)


def rows_of(shape):
    return lax.broadcasted_iota(jnp.int32, shape, 0)


def swap(tile):
    return pltpu.roll(tile, tile.shape[1] // 2, 1)


def twice(row):
    return jnp.concatenate([row, row], axis=1)


def folded(poles):
    half = poles.shape[0] // 2
    return jnp.concatenate([poles[:half], poles[half:]], axis=1)


def project_kernel(tok_hbm, w_hbm, out_ref, tok_ref, w_ref, acc_ref, sems):
    streams, depth, _ = w_ref.shape
    pieces = sems.shape[0]
    deep = depth // pieces
    parts = [pl.ds(i * deep, deep) for i in range(pieces)]
    copies = []
    for i, part in enumerate(parts):
        copies.append([pltpu.make_async_copy(tok_hbm.at[:, part], tok_ref.at[:, part], sems.at[i, streams])])
        for s in range(streams):
            copies[i].append(pltpu.make_async_copy(w_hbm.at[s, part], w_ref.at[s, part], sems.at[i, s]))
    for piece in copies:
        for copy in piece:
            copy.start()
    for i, part in enumerate(parts):
        for copy in copies[i]:
            copy.wait()
        for s in range(streams):
            term = jnp.dot(tok_ref[:, part], w_ref[s, part, :], preferred_element_type=F32)
            acc_ref[s] = term if i == 0 else acc_ref[s] + term
    rows = acc_ref.shape[1] // 2
    for s in range(streams):
        for pair in range(acc_ref.shape[2] // 128):
            early = acc_ref[s, :rows, 128 * pair : 128 * (pair + 1)]
            late = acc_ref[s, rows:, 128 * pair : 128 * (pair + 1)]
            left = lanes_of(early.shape) < 64
            out_ref[2 * pair, s] = jnp.where(left, early, swap(late))
            out_ref[2 * pair + 1, s] = jnp.where(left, swap(early), late)


def project(tokens, weight):
    rows, depth = tokens.shape
    streams, _, width = weight.shape
    chan = width // 64
    pieces = 4
    return pl.pallas_call(
        project_kernel,
        in_specs=[HBM, HBM],
        out_shape=pltpu.VMEM((chan, streams, rows // 2, 128), F32),
        scratch_shapes=[
            pltpu.VMEM(tokens.shape, tokens.dtype),
            pltpu.VMEM(weight.shape, weight.dtype),
            pltpu.VMEM((streams, rows, width), F32),
            pltpu.SemaphoreType.DMA((pieces, streams + 1)),
        ],
        compiler_params=ROOMY,
        name="project",
    )(in_hbm(tokens), in_hbm(weight))


def local_kernel(part_ref, short_ref, residue_ref, rates_ref, skip_ref, send_ref, keep_ref):
    count = part_ref.shape[0]
    rows, width = part_ref.shape[2:]
    right = lanes_of((1, width)) >= width // 2
    row = rows_of((rows, width))
    feats, edges = [], []
    for s in range(3):
        p = part_ref[0, s]
        for i in range(1, count):
            p = p + part_ref[i, s]
        tap = [twice(short_ref[k, s : s + 1, :]) for k in range(3)]
        before = jnp.where(right, swap(p[rows - 8 :]), 0.0)
        one = jnp.where(row < 1, before[7:8], pltpu.roll(p, 1, 0))
        two = pltpu.roll(p, 2, 0)
        two = jnp.where(row == 0, before[6:7], jnp.where(row == 1, before[7:8], two))
        feats.append(tap[0] * p + tap[1] * one + tap[2] * two)
        edges.append((tap[1] * p[rows - 1 :] + tap[2] * p[rows - 2 : rows - 1], tap[2] * p[rows - 1 :]))
    q, a, b = feats
    keep_ref[0:rows, :] = q
    x = jnp.where(jnp.logical_and(row < 2, jnp.logical_not(right)), 0.0, a * b)
    keep_ref[rows : 2 * rows, :] = x
    tile = [
        jnp.where(right, swap(b[0:1]), a[0:1]),
        jnp.where(right, swap(b[1:2]), a[1:2]),
        jnp.where(right, edges[2][0], swap(edges[1][0])),
        jnp.where(right, edges[2][1], swap(edges[1][1])),
        jnp.where(right, edges[0][1], swap(edges[0][0])),
    ]
    own = jnp.concatenate(tile + [jnp.zeros((3, width), F32)], axis=0)
    keep_ref[2 * rows : 2 * rows + 8, :] = own

    rates = twice(rates_ref[...])
    weight = twice(residue_ref[...]) * jnp.sqrt(2.0 * rates)
    poles = rates.shape[0]
    at = 2 * rows + 8 + poles
    keep_ref[at : at + poles, :] = rates
    keep_ref[at + poles : at + 2 * poles, :] = weight
    keep_ref[at + 2 * poles :, :] = jnp.broadcast_to(twice(skip_ref[...]), (8, width))
    step_pos = rows_of((STEP, width)).astype(F32)
    decay = jnp.exp(-float(STEP) * rates)
    half = []
    for r in range(poles):
        sums = x[:STEP]
        for k in range(1, rows // STEP):
            sums = sums * decay[r : r + 1] + x[k * STEP : (k + 1) * STEP]
        into = jnp.exp(-rates[r : r + 1] * (STEP - 1.0 - step_pos))
        half.append(jnp.sum(into * sums, axis=0, keepdims=True))
    half = jnp.concatenate(half, axis=0)
    keep_ref[2 * rows + 8 : at, :] = half
    total = half + jnp.exp(-float(rows) * rates) * swap(half)
    h = poles // 2
    packed = jnp.where(right, total[h:], swap(total[:h]))
    for i in range(send_ref.shape[0]):
        send_ref[i, 0:8, :] = packed
        send_ref[i, 8:16, :] = own


def within_kernel(keep_ref, *outs):
    *kept_refs, y_ref = outs
    for ref in kept_refs:
        ref[...] = keep_ref[...]
    rows, width = y_ref.shape
    poles = (keep_ref.shape[0] - 2 * rows - 16) // 3
    at = 2 * rows + 8 + poles
    rates = keep_ref[at : at + poles, :]
    weight = keep_ref[at + poles : at + 2 * poles, :]
    inner = rows_of((STEP, width))
    step_pos = inner.astype(F32)
    impulse = [jnp.sum(weight * jnp.exp(-rates * float(u)), axis=0, keepdims=True) for u in range(STEP)]
    near = [jnp.where(inner >= u, impulse[u], 0.0) for u in range(STEP)]
    decay = jnp.exp(-float(STEP) * rates)
    into, outof, fade = [], [], []
    for r in range(poles):
        rate = rates[r : r + 1]
        into.append(jnp.exp(-rate * (STEP - 1.0 - step_pos)))
        outof.append(weight[r : r + 1] * jnp.exp(-rate * (step_pos + 1.0)))
        fade.append(decay[r : r + 1])
    state = [None] * poles
    for k in range(rows // STEP):
        xk = keep_ref[rows + k * STEP : rows + (k + 1) * STEP, :]
        yk = near[0] * xk
        for u in range(1, STEP):
            yk = yk + near[u] * pltpu.roll(xk, u, 0)
        for r in range(poles):
            gain = jnp.sum(into[r] * xk, axis=0, keepdims=True)
            if k > 0:
                yk = yk + outof[r] * state[r]
                gain = gain + fade[r] * state[r]
            state[r] = gain
        y_ref[k * STEP : (k + 1) * STEP, :] = yk


def within(keep, rows, both):
    outs = (pltpu.VMEM(keep.shape, F32),) * both + (pltpu.VMEM((rows, keep.shape[1]), F32),)
    return pl.pallas_call(within_kernel, out_shape=outs, compiler_params=ROOMY, name="within")(in_vmem(keep))


def local(parts, short_weight, residue, rates, skip):
    _, _, rows, width = parts.shape
    return pl.pallas_call(
        local_kernel,
        out_shape=(
            pltpu.VMEM((NEAR, 16, width), F32),
            pltpu.VMEM((2 * rows + 16 + 3 * rates.shape[0], width), F32),
        ),
        compiler_params=ROOMY,
        name="local",
    )(in_vmem(parts), in_vmem(short_weight), in_vmem(residue), in_vmem(rates), in_vmem(skip))


def gate_of(tile, before):
    a = tile[0:2]
    if before is not None:
        a = a + before[2:4]
    return a * swap(a)


def near_kernel(shard_rows, got_ref, rates_ref, send_ref, keep_ref):
    near = lax.axis_index("near")
    rates = folded(rates_ref[...])
    fade = jnp.exp(-float(shard_rows) * rates)
    first = jnp.exp(-(shard_rows - 1.0) * rates)
    second = jnp.exp(-(shard_rows - 2.0) * rates)
    total = got_ref[0, 0:8, :]
    prefix = jnp.where(near > 0, total, 0.0)
    before = jnp.zeros_like(total)
    for i in range(1, NEAR):
        edge = got_ref[i - 1, 8:16, :]
        gate = gate_of(got_ref[i, 8:16, :], edge)
        grown = total * fade + (got_ref[i, 0:8, :] + first * gate[0:1] + second * gate[1:2])
        before = jnp.where(near == i, edge, before)
        total = grown
        prefix = jnp.where(near > i, grown, prefix)
    keep_ref[0:8, :] = prefix
    keep_ref[8:16, :] = before
    keep_ref[16:24, :] = rates
    head = got_ref[0, 8:16, :]
    tail = got_ref[NEAR - 1, 8:16, :]
    ends = jnp.where(rows_of(head.shape) < 2, head, tail)
    send_ref[0:8, :] = total
    send_ref[8:16, :] = ends


def near_sums(got, rates, shard_rows):
    width = got.shape[2]
    return pl.pallas_call(
        functools.partial(near_kernel, shard_rows),
        out_shape=(pltpu.VMEM((16, width), F32), pltpu.VMEM((24, width), F32)),
        compiler_params=ROOMY,
        name="near_sums",
    )(in_vmem(got), in_vmem(rates))


def with_row(shard_rows, row, got, rates):
    gate = gate_of(row[8:16], got[8:16])
    start = jnp.exp(-(shard_rows - 1.0) * rates) * gate[0:1] + jnp.exp(-(shard_rows - 2.0) * rates) * gate[1:2]
    state = row[0:8] + jnp.exp(-float((NEAR - 1) * shard_rows) * rates) * start
    state = state + jnp.exp(-float(NEAR * shard_rows) * rates) * got[0:8]
    return jnp.concatenate([state, row[8:16]], axis=0)


def first_kernel(shard_rows, row_ref, near_ref, total_ref):
    total_ref[...] = with_row(shard_rows, row_ref[...], jnp.zeros(row_ref.shape, F32), near_ref[16:24, :])


def first_sum(shard_rows, row, near):
    return pl.pallas_call(
        functools.partial(first_kernel, shard_rows),
        out_shape=pltpu.VMEM(row.shape, F32),
        compiler_params=ROOMY,
        name="first_sum",
    )(in_vmem(row), in_vmem(near))


def hop_kernel(shard_rows, sums, sources, *refs):
    kept = (len(refs) - sources - sums - 1) // 2
    rows_before, work_refs, refs = refs[:sources], refs[sources : sources + kept], refs[sources + kept :]
    sum_refs, before_ref, work_outs = refs[:sums], refs[sums], refs[sums + 1 :]
    row_ref, near_ref = work_refs[:2]
    rates = near_ref[16:24, :]
    before = rows_before[0][...]
    if sources > 1:
        before = with_row(shard_rows, rows_before[1][...], before, rates)
    before_ref[...] = before
    if sums:
        total = with_row(shard_rows, row_ref[...], before, rates)
    for ref in sum_refs:
        ref[...] = total
    for ref, out in zip(work_refs, work_outs):
        out[...] = ref[...]


def hop(shard_rows, sums, sources, row, *rest):
    operands = [in_vmem(a) for a in (*sources, row, *rest)]
    outs = (row,) * (sums + 2) + rest
    return pl.pallas_call(
        functools.partial(hop_kernel, shard_rows, sums, len(sources)),
        out_shape=tuple(pltpu.VMEM(a.shape, F32) for a in outs),
        compiler_params=ROOMY,
        name="hop",
    )(*operands)


def finish_kernel(shard_rows, row_ref, got_ref, near_ref, keep_ref, y_ref, out_ref):
    near = lax.axis_index("near")
    rows, width = out_ref.shape[1] // 2, keep_ref.shape[1]
    poles = 2 * near_ref[16:24, :].shape[0]
    at = 2 * rows + 8 + poles
    rates = keep_ref[at : at + poles, :]
    weight = keep_ref[at + poles : at + 2 * poles, :]
    skip = keep_ref[at + 2 * poles : at + 2 * poles + 1, :]
    step_pos = rows_of((STEP, width)).astype(F32)
    decay = jnp.exp(-float(STEP) * rates)
    half_decay = jnp.exp(-float(rows) * rates)
    ahead = jnp.sum(weight * jnp.exp(rates), axis=0, keepdims=True)
    outof, fade = [], []
    for r in range(poles):
        outof.append(weight[r : r + 1] * jnp.exp(-rates[r : r + 1] * (step_pos + 1.0)))
        fade.append(jnp.broadcast_to(decay[r : r + 1], (STEP, width)))

    rates = near_ref[16:24, :]
    first = jnp.exp(-(shard_rows - 1.0) * rates)
    second = jnp.exp(-(shard_rows - 2.0) * rates)
    place = near.astype(F32) * float(shard_rows)
    place_fade = jnp.exp(-place * rates)
    beyond_fade = jnp.where(near > 0, jnp.exp(-jnp.maximum(place - shard_rows, 0.0) * rates), 0.0)
    ahead_one, ahead_two = jnp.exp(rates), jnp.exp(2.0 * rates)
    edge = got_ref[8:16, :]
    before = jnp.where(near == 0, edge, near_ref[8:16, :])
    gate = gate_of(row_ref[8:16, :], edge)
    opening = first * gate[0:1] + second * gate[1:2]
    carry = got_ref[0:8, :]
    state = near_ref[0:8, :] + place_fade * carry + beyond_fade * opening
    gate = gate_of(keep_ref[2 * rows : 2 * rows + 8, :], before)
    state = state + ahead_one * gate[0:1] + ahead_two * gate[1:2]

    left = lanes_of((1, width)) < width // 2
    other = swap(state)
    whole = jnp.concatenate([jnp.where(left, state, other), jnp.where(left, other, state)], axis=0)
    whole = jnp.where(left, whole, swap(keep_ref[2 * rows + 8 : 2 * rows + 8 + poles, :]) + half_decay * whole)
    states = [jnp.broadcast_to(whole[r : r + 1], (STEP, width)) * outof[r] for r in range(poles)]
    steps = []
    for k in range(rows // STEP):
        at = k * STEP
        qk = keep_ref[at : at + STEP, :]
        xk = keep_ref[rows + at : rows + at + STEP, :]
        yk = y_ref[at : at + STEP, :]
        if k == 0:
            inner = rows_of((STEP, width))
            top = jnp.logical_and(left, inner == 0)
            next_ = jnp.logical_and(left, inner == 1)
            xk = jnp.where(top, gate[0:1], jnp.where(next_, gate[1:2], xk))
            yk = yk - jnp.where(top, ahead * gate[1:2], 0.0)
            q_edge = before[4:5]
            qk = qk + jnp.where(top, q_edge, jnp.where(next_, swap(q_edge), 0.0))
        for r in range(poles):
            yk = yk + states[r]
            states[r] = states[r] * fade[r]
        steps.append(qk * (yk + skip * xk))
    mixed = jnp.concatenate(steps, axis=0).T
    out_ref[:, :rows] = mixed[: width // 2].astype(out_ref.dtype)
    out_ref[:, rows:] = mixed[width // 2 :].astype(out_ref.dtype)


def finish(shard_rows, row, got, near, keep, y=None):
    width = keep.shape[1]
    if y is None:
        (y,) = within(keep, shard_rows // 2, False)
    return pl.pallas_call(
        functools.partial(finish_kernel, shard_rows),
        out_shape=jax.ShapeDtypeStruct((width // 2, shard_rows), jnp.bfloat16),
        compiler_params=ROOMY,
        name="finish",
    )(in_vmem(row), in_vmem(got), in_vmem(near), in_vmem(keep), in_vmem(y))


def nothing(*shapes):
    return pl.pallas_call(
        lambda *refs: None,
        out_shape=tuple(pltpu.VMEM(shape, F32) for shape in shapes),
        name="nothing",
    )()


def crossed(source, target):
    return [(source * NEAR + i, target * NEAR + (i ^ 1)) for i in range(NEAR)]


def per_device(tokens, in_weight, short_weight, residue, rates, skip):
    shard_rows = tokens.shape[0]
    residue, rates, skip = residue.T, rates.T, skip[None, :]
    weight = in_weight.transpose(1, 0, 2)
    far, far_count = lax.axis_index("far"), lax.axis_size("far")

    def row_of_shards(full):
        parts = lax.all_to_all(project(tokens, weight), "chan", 0, 0, tiled=True)
        send, keep = local(parts, short_weight, residue, rates, skip)
        row, near = near_sums(lax.all_to_all(send, "near", 0, 0, tiled=True), rates, shard_rows)
        if not full:
            return row, near, keep
        row, keep = lax.optimization_barrier((row, keep))
        return row, near, *within(keep, shard_rows // 2, True)

    shapes = [a.shape for a in jax.eval_shape(lambda: row_of_shards(True))]

    def work_of(mine, full=True):
        return lax.cond(mine, lambda: row_of_shards(full), lambda: nothing(*shapes[: 3 + full]))

    none = jnp.zeros(shapes[0], F32)
    even = far % 2 == 0
    row, near, keep = work_of(even, False)
    total = first_sum(shard_rows, row, near)
    after = none
    results = [None]
    for k in range(1, far_count, 2):
        sums = int(k + 1 < far_count)
        full = k > 3

        two = jnp.where(far == k - 1, row, total)

        def odd_row(k=k, total=total, two=two, sums=sums, full=full):
            block = jnp.where(far == max(k - 2, 0), total, none)
            sources = [lax.ppermute(block, ("far", "near"), crossed(max(k - 2, 0), k))]
            extra = []
            if k > 1:
                steps = crossed(k - 2, k - 1) + crossed(k - 1, k)
                extra = [lax.ppermute(two, ("far", "near"), steps)]
                sources += extra
            return hop(shard_rows, sums, sources, *work_of(far == k, full), *extra)

        here = jnp.logical_and(far <= k, far >= k - 2)
        outs = shapes[:1] * (sums + 1) + shapes[: 3 + full] + shapes[:1] * (k > 1)
        out = lax.cond(here, odd_row, lambda outs=outs: nothing(*outs))
        results.append((out[sums + 1], out[sums], *out[sums + 2 : sums + 4 + full]))
        if k > 1:
            after = jnp.where(far == k - 1, out[-1], after)
        if k == 3:
            keep, *out = lax.optimization_barrier((keep, *out))
            kept = lax.cond(
                even, lambda: within(keep, shard_rows // 2, True), lambda: nothing(shapes[2], shapes[3])
            )
            *out, kept0, kept1 = lax.optimization_barrier((*out, *kept))
            kept = (kept0, kept1)
        total = out[0]
    results[0] = (row, after, near, *kept)
    branches = [lambda r=r: finish(shard_rows, *r) for r in results]
    return lax.switch(jnp.where(even, 0, (far + 1) // 2), branches).T


def solution(mesh):
    seq, chan = mesh.devices.shape
    mesh = Mesh(mesh.devices.reshape(seq // NEAR, NEAR, chan), ("far", "near", "chan"))
    whole = ("far", "near")
    in_specs = (
        P(whole, "chan"),
        P("chan", None, None),
        P(None, None, "chan"),
        P("chan", None),
        P("chan", None),
        P("chan"),
    )
    return jax.shard_map(
        per_device, mesh=mesh, in_specs=in_specs, out_specs=P(whole, "chan"), check_vma=False
    )
```

```python
import functools

import jax
import jax.numpy as jnp
from jax import lax
from jax.experimental import pallas as pl
from jax.experimental.pallas import tpu as pltpu
from jax.sharding import Mesh, PartitionSpec as P

NEAR = 16
STEP = 8
F32 = jnp.float32
HBM = pl.BlockSpec(memory_space=pl.ANY)
ROOMY = pltpu.CompilerParams(vmem_limit_bytes=24 * 2**20)


def in_vmem(array):
    return pltpu.with_memory_space_constraint(array, pltpu.VMEM)


def in_hbm(array):
    return pltpu.with_memory_space_constraint(array, pltpu.HBM)


def lanes_of(shape):
    return lax.broadcasted_iota(jnp.int32, shape, 1)


def rows_of(shape):
    return lax.broadcasted_iota(jnp.int32, shape, 0)


def swap(tile):
    return pltpu.roll(tile, tile.shape[1] // 2, 1)


def twice(row):
    return jnp.concatenate([row, row], axis=1)


def folded(poles):
    half = poles.shape[0] // 2
    return jnp.concatenate([poles[:half], poles[half:]], axis=1)


def project_kernel(tok_hbm, w_hbm, out_ref, tok_ref, w_ref, acc_ref, sems):
    streams, depth, _ = w_ref.shape
    pieces = sems.shape[0]
    deep = depth // pieces
    parts = [pl.ds(i * deep, deep) for i in range(pieces)]
    copies = []
    for i, part in enumerate(parts):
        copies.append([pltpu.make_async_copy(tok_hbm.at[:, part], tok_ref.at[:, part], sems.at[i, streams])])
        for s in range(streams):
            copies[i].append(pltpu.make_async_copy(w_hbm.at[s, part], w_ref.at[s, part], sems.at[i, s]))
    for piece in copies:
        for copy in piece:
            copy.start()
    for i, part in enumerate(parts):
        for copy in copies[i]:
            copy.wait()
        for s in range(streams):
            term = jnp.dot(tok_ref[:, part], w_ref[s, part, :], preferred_element_type=F32)
            acc_ref[s] = term if i == 0 else acc_ref[s] + term
    rows = acc_ref.shape[1] // 2
    for s in range(streams):
        for pair in range(acc_ref.shape[2] // 128):
            early = acc_ref[s, :rows, 128 * pair : 128 * (pair + 1)]
            late = acc_ref[s, rows:, 128 * pair : 128 * (pair + 1)]
            left = lanes_of(early.shape) < 64
            out_ref[2 * pair, s] = jnp.where(left, early, swap(late))
            out_ref[2 * pair + 1, s] = jnp.where(left, swap(early), late)


def project(tokens, weight):
    rows, depth = tokens.shape
    streams, _, width = weight.shape
    chan = width // 64
    pieces = 4
    return pl.pallas_call(
        project_kernel,
        in_specs=[HBM, HBM],
        out_shape=pltpu.VMEM((chan, streams, rows // 2, 128), F32),
        scratch_shapes=[
            pltpu.VMEM(tokens.shape, tokens.dtype),
            pltpu.VMEM(weight.shape, weight.dtype),
            pltpu.VMEM((streams, rows, width), F32),
            pltpu.SemaphoreType.DMA((pieces, streams + 1)),
        ],
        compiler_params=ROOMY,
        name="project",
    )(in_hbm(tokens), in_hbm(weight))


def local_kernel(part_ref, short_ref, residue_ref, rates_ref, skip_ref, send_ref, keep_ref):
    count = part_ref.shape[0]
    rows, width = part_ref.shape[2:]
    right = lanes_of((1, width)) >= width // 2
    row = rows_of((rows, width))
    feats, edges = [], []
    for s in range(3):
        p = part_ref[0, s]
        for i in range(1, count):
            p = p + part_ref[i, s]
        tap = [twice(short_ref[k, s : s + 1, :]) for k in range(3)]
        before = jnp.where(right, swap(p[rows - 8 :]), 0.0)
        one = jnp.where(row < 1, before[7:8], pltpu.roll(p, 1, 0))
        two = pltpu.roll(p, 2, 0)
        two = jnp.where(row == 0, before[6:7], jnp.where(row == 1, before[7:8], two))
        feats.append(tap[0] * p + tap[1] * one + tap[2] * two)
        edges.append((tap[1] * p[rows - 1 :] + tap[2] * p[rows - 2 : rows - 1], tap[2] * p[rows - 1 :]))
    q, a, b = feats
    keep_ref[0:rows, :] = q
    x = jnp.where(jnp.logical_and(row < 2, jnp.logical_not(right)), 0.0, a * b)
    keep_ref[rows : 2 * rows, :] = x
    tile = [
        jnp.where(right, swap(b[0:1]), a[0:1]),
        jnp.where(right, swap(b[1:2]), a[1:2]),
        jnp.where(right, edges[2][0], swap(edges[1][0])),
        jnp.where(right, edges[2][1], swap(edges[1][1])),
        jnp.where(right, edges[0][1], swap(edges[0][0])),
    ]
    own = jnp.concatenate(tile + [jnp.zeros((3, width), F32)], axis=0)
    keep_ref[2 * rows : 2 * rows + 8, :] = own

    rates = twice(rates_ref[...])
    weight = twice(residue_ref[...]) * jnp.sqrt(2.0 * rates)
    poles = rates.shape[0]
    at = 2 * rows + 8 + poles
    keep_ref[at : at + poles, :] = rates
    keep_ref[at + poles : at + 2 * poles, :] = weight
    keep_ref[at + 2 * poles :, :] = jnp.broadcast_to(twice(skip_ref[...]), (8, width))
    step_pos = rows_of((STEP, width)).astype(F32)
    decay = jnp.exp(-float(STEP) * rates)
    half = []
    for r in range(poles):
        sums = x[:STEP]
        for k in range(1, rows // STEP):
            sums = sums * decay[r : r + 1] + x[k * STEP : (k + 1) * STEP]
        into = jnp.exp(-rates[r : r + 1] * (STEP - 1.0 - step_pos))
        half.append(jnp.sum(into * sums, axis=0, keepdims=True))
    half = jnp.concatenate(half, axis=0)
    keep_ref[2 * rows + 8 : at, :] = half
    total = half + jnp.exp(-float(rows) * rates) * swap(half)
    h = poles // 2
    packed = jnp.where(right, total[h:], swap(total[:h]))
    for i in range(send_ref.shape[0]):
        send_ref[i, 0:8, :] = packed
        send_ref[i, 8:16, :] = own


def within_kernel(keep_ref, *outs):
    *kept_refs, y_ref = outs
    for ref in kept_refs:
        ref[...] = keep_ref[...]
    rows, width = y_ref.shape
    poles = (keep_ref.shape[0] - 2 * rows - 16) // 3
    at = 2 * rows + 8 + poles
    rates = keep_ref[at : at + poles, :]
    weight = keep_ref[at + poles : at + 2 * poles, :]
    inner = rows_of((STEP, width))
    step_pos = inner.astype(F32)
    impulse = [jnp.sum(weight * jnp.exp(-rates * float(u)), axis=0, keepdims=True) for u in range(STEP)]
    near = [jnp.where(inner >= u, impulse[u], 0.0) for u in range(STEP)]
    decay = jnp.exp(-float(STEP) * rates)
    into, outof, fade = [], [], []
    for r in range(poles):
        rate = rates[r : r + 1]
        into.append(jnp.exp(-rate * (STEP - 1.0 - step_pos)))
        outof.append(weight[r : r + 1] * jnp.exp(-rate * (step_pos + 1.0)))
        fade.append(decay[r : r + 1])
    state = [None] * poles
    for k in range(rows // STEP):
        xk = keep_ref[rows + k * STEP : rows + (k + 1) * STEP, :]
        yk = near[0] * xk
        for u in range(1, STEP):
            yk = yk + near[u] * pltpu.roll(xk, u, 0)
        for r in range(poles):
            gain = jnp.sum(into[r] * xk, axis=0, keepdims=True)
            if k > 0:
                yk = yk + outof[r] * state[r]
                gain = gain + fade[r] * state[r]
            state[r] = gain
        y_ref[k * STEP : (k + 1) * STEP, :] = yk


def within(keep, rows, both):
    outs = (pltpu.VMEM(keep.shape, F32),) * both + (pltpu.VMEM((rows, keep.shape[1]), F32),)
    return pl.pallas_call(within_kernel, out_shape=outs, compiler_params=ROOMY, name="within")(in_vmem(keep))


def local(parts, short_weight, residue, rates, skip):
    _, _, rows, width = parts.shape
    return pl.pallas_call(
        local_kernel,
        out_shape=(
            pltpu.VMEM((NEAR, 16, width), F32),
            pltpu.VMEM((2 * rows + 16 + 3 * rates.shape[0], width), F32),
        ),
        compiler_params=ROOMY,
        name="local",
    )(in_vmem(parts), in_vmem(short_weight), in_vmem(residue), in_vmem(rates), in_vmem(skip))


def gate_of(tile, before):
    a = tile[0:2]
    if before is not None:
        a = a + before[2:4]
    return a * swap(a)


def near_kernel(shard_rows, got_ref, rates_ref, send_ref, keep_ref):
    near = lax.axis_index("near")
    rates = folded(rates_ref[...])
    fade = jnp.exp(-float(shard_rows) * rates)
    first = jnp.exp(-(shard_rows - 1.0) * rates)
    second = jnp.exp(-(shard_rows - 2.0) * rates)
    total = got_ref[0, 0:8, :]
    prefix = jnp.where(near > 0, total, 0.0)
    before = jnp.zeros_like(total)
    for i in range(1, NEAR):
        edge = got_ref[i - 1, 8:16, :]
        gate = gate_of(got_ref[i, 8:16, :], edge)
        grown = total * fade + (got_ref[i, 0:8, :] + first * gate[0:1] + second * gate[1:2])
        before = jnp.where(near == i, edge, before)
        total = grown
        prefix = jnp.where(near > i, grown, prefix)
    keep_ref[0:8, :] = prefix
    keep_ref[8:16, :] = before
    keep_ref[16:24, :] = rates
    head = got_ref[0, 8:16, :]
    tail = got_ref[NEAR - 1, 8:16, :]
    ends = jnp.where(rows_of(head.shape) < 2, head, tail)
    send_ref[0:8, :] = total
    send_ref[8:16, :] = ends


def near_sums(got, rates, shard_rows):
    width = got.shape[2]
    return pl.pallas_call(
        functools.partial(near_kernel, shard_rows),
        out_shape=(pltpu.VMEM((16, width), F32), pltpu.VMEM((24, width), F32)),
        compiler_params=ROOMY,
        name="near_sums",
    )(in_vmem(got), in_vmem(rates))


def with_row(shard_rows, row, got, rates):
    gate = gate_of(row[8:16], got[8:16])
    start = jnp.exp(-(shard_rows - 1.0) * rates) * gate[0:1] + jnp.exp(-(shard_rows - 2.0) * rates) * gate[1:2]
    state = row[0:8] + jnp.exp(-float((NEAR - 1) * shard_rows) * rates) * start
    state = state + jnp.exp(-float(NEAR * shard_rows) * rates) * got[0:8]
    return jnp.concatenate([state, row[8:16]], axis=0)


def first_kernel(shard_rows, row_ref, near_ref, total_ref):
    total_ref[...] = with_row(shard_rows, row_ref[...], jnp.zeros(row_ref.shape, F32), near_ref[16:24, :])


def first_sum(shard_rows, row, near):
    return pl.pallas_call(
        functools.partial(first_kernel, shard_rows),
        out_shape=pltpu.VMEM(row.shape, F32),
        compiler_params=ROOMY,
        name="first_sum",
    )(in_vmem(row), in_vmem(near))


def hop_kernel(shard_rows, sums, sources, *refs):
    kept = (len(refs) - sources - sums - 1) // 2
    rows_before, work_refs, refs = refs[:sources], refs[sources : sources + kept], refs[sources + kept :]
    sum_refs, before_ref, work_outs = refs[:sums], refs[sums], refs[sums + 1 :]
    row_ref, near_ref = work_refs[:2]
    rates = near_ref[16:24, :]
    before = rows_before[0][...]
    if sources > 1:
        before = with_row(shard_rows, rows_before[1][...], before, rates)
    before_ref[...] = before
    if sums:
        total = with_row(shard_rows, row_ref[...], before, rates)
    for ref in sum_refs:
        ref[...] = total
    for ref, out in zip(work_refs, work_outs):
        out[...] = ref[...]


def hop(shard_rows, sums, sources, row, *rest):
    operands = [in_vmem(a) for a in (*sources, row, *rest)]
    outs = (row,) * (sums + 2) + rest
    return pl.pallas_call(
        functools.partial(hop_kernel, shard_rows, sums, len(sources)),
        out_shape=tuple(pltpu.VMEM(a.shape, F32) for a in outs),
        compiler_params=ROOMY,
        name="hop",
    )(*operands)


def finish_kernel(shard_rows, row_ref, got_ref, near_ref, keep_ref, y_ref, out_ref):
    near = lax.axis_index("near")
    rows, width = out_ref.shape[1] // 2, keep_ref.shape[1]
    poles = 2 * near_ref[16:24, :].shape[0]
    at = 2 * rows + 8 + poles
    rates = keep_ref[at : at + poles, :]
    weight = keep_ref[at + poles : at + 2 * poles, :]
    skip = keep_ref[at + 2 * poles : at + 2 * poles + 1, :]
    step_pos = rows_of((STEP, width)).astype(F32)
    decay = jnp.exp(-float(STEP) * rates)
    half_decay = jnp.exp(-float(rows) * rates)
    ahead = jnp.sum(weight * jnp.exp(rates), axis=0, keepdims=True)
    outof, fade = [], []
    for r in range(poles):
        outof.append(weight[r : r + 1] * jnp.exp(-rates[r : r + 1] * (step_pos + 1.0)))
        fade.append(jnp.broadcast_to(decay[r : r + 1], (STEP, width)))

    rates = near_ref[16:24, :]
    first = jnp.exp(-(shard_rows - 1.0) * rates)
    second = jnp.exp(-(shard_rows - 2.0) * rates)
    place = near.astype(F32) * float(shard_rows)
    place_fade = jnp.exp(-place * rates)
    beyond_fade = jnp.where(near > 0, jnp.exp(-jnp.maximum(place - shard_rows, 0.0) * rates), 0.0)
    ahead_one, ahead_two = jnp.exp(rates), jnp.exp(2.0 * rates)
    edge = got_ref[8:16, :]
    before = jnp.where(near == 0, edge, near_ref[8:16, :])
    gate = gate_of(row_ref[8:16, :], edge)
    opening = first * gate[0:1] + second * gate[1:2]
    carry = got_ref[0:8, :]
    state = near_ref[0:8, :] + place_fade * carry + beyond_fade * opening
    gate = gate_of(keep_ref[2 * rows : 2 * rows + 8, :], before)
    state = state + ahead_one * gate[0:1] + ahead_two * gate[1:2]

    left = lanes_of((1, width)) < width // 2
    other = swap(state)
    whole = jnp.concatenate([jnp.where(left, state, other), jnp.where(left, other, state)], axis=0)
    whole = jnp.where(left, whole, swap(keep_ref[2 * rows + 8 : 2 * rows + 8 + poles, :]) + half_decay * whole)
    states = [jnp.broadcast_to(whole[r : r + 1], (STEP, width)) * outof[r] for r in range(poles)]
    steps = []
    for k in range(rows // STEP):
        at = k * STEP
        qk = keep_ref[at : at + STEP, :]
        xk = keep_ref[rows + at : rows + at + STEP, :]
        yk = y_ref[at : at + STEP, :]
        if k == 0:
            inner = rows_of((STEP, width))
            top = jnp.logical_and(left, inner == 0)
            next_ = jnp.logical_and(left, inner == 1)
            xk = jnp.where(top, gate[0:1], jnp.where(next_, gate[1:2], xk))
            yk = yk - jnp.where(top, ahead * gate[1:2], 0.0)
            q_edge = before[4:5]
            qk = qk + jnp.where(top, q_edge, jnp.where(next_, swap(q_edge), 0.0))
        for r in range(poles):
            yk = yk + states[r]
            states[r] = states[r] * fade[r]
        steps.append(qk * (yk + skip * xk))
    mixed = jnp.concatenate(steps, axis=0).T
    out_ref[:, :rows] = mixed[: width // 2].astype(out_ref.dtype)
    out_ref[:, rows:] = mixed[width // 2 :].astype(out_ref.dtype)


def finish(shard_rows, row, got, near, keep, y=None):
    width = keep.shape[1]
    if y is None:
        (y,) = within(keep, shard_rows // 2, False)
    return pl.pallas_call(
        functools.partial(finish_kernel, shard_rows),
        out_shape=jax.ShapeDtypeStruct((width // 2, shard_rows), jnp.bfloat16),
        compiler_params=ROOMY,
        name="finish",
    )(in_vmem(row), in_vmem(got), in_vmem(near), in_vmem(keep), in_vmem(y))


def nothing(*shapes):
    return pl.pallas_call(
        lambda *refs: None,
        out_shape=tuple(pltpu.VMEM(shape, F32) for shape in shapes),
        name="nothing",
    )()


def crossed(source, target):
    return [(source * NEAR + i, target * NEAR + (i ^ 1)) for i in range(NEAR)]


def per_device(tokens, in_weight, short_weight, residue, rates, skip):
    shard_rows = tokens.shape[0]
    residue, rates, skip = residue.T, rates.T, skip[None, :]
    weight = in_weight.transpose(1, 0, 2)
    far, far_count = lax.axis_index("far"), lax.axis_size("far")

    def row_of_shards(full):
        parts = lax.all_to_all(project(tokens, weight), "chan", 0, 0, tiled=True)
        send, keep = local(parts, short_weight, residue, rates, skip)
        row, near = near_sums(lax.all_to_all(send, "near", 0, 0, tiled=True), rates, shard_rows)
        if not full:
            return row, near, keep
        row, keep = lax.optimization_barrier((row, keep))
        return row, near, *within(keep, shard_rows // 2, True)

    shapes = [a.shape for a in jax.eval_shape(lambda: row_of_shards(True))]

    def work_of(mine, full=True):
        return lax.cond(mine, lambda: row_of_shards(full), lambda: nothing(*shapes[: 3 + full]))

    none = jnp.zeros(shapes[0], F32)
    even = far % 2 == 0
    row, near, keep = work_of(even, False)
    total = first_sum(shard_rows, row, near)
    after = none
    results = [None]
    for k in range(1, far_count, 2):
        sums = int(k + 1 < far_count)
        full = k > 3

        two = jnp.where(far == k - 1, row, total)

        def odd_row(k=k, total=total, two=two, sums=sums, full=full):
            block = jnp.where(far == max(k - 2, 0), total, none)
            sources = [lax.ppermute(block, ("far", "near"), crossed(max(k - 2, 0), k))]
            extra = []
            if k > 1:
                steps = crossed(k - 2, k - 1) + [((k - 1) * NEAR + i, k * NEAR + i) for i in range(NEAR)]
                extra = [lax.ppermute(two, ("far", "near"), steps)]
                sources += extra
            return hop(shard_rows, sums, sources, *work_of(far == k, full), *extra)

        here = jnp.logical_and(far <= k, far >= k - 2)
        outs = shapes[:1] * (sums + 1) + shapes[: 3 + full] + shapes[:1] * (k > 1)
        out = lax.cond(here, odd_row, lambda outs=outs: nothing(*outs))
        results.append((out[sums + 1], out[sums], *out[sums + 2 : sums + 4 + full]))
        if k > 1:
            after = jnp.where(far == k - 1, out[-1], after)
        if k == 3:
            keep, *out = lax.optimization_barrier((keep, *out))
            kept = lax.cond(
                even, lambda: within(keep, shard_rows // 2, True), lambda: nothing(shapes[2], shapes[3])
            )
            *out, kept0, kept1 = lax.optimization_barrier((*out, *kept))
            kept = (kept0, kept1)
        total = out[0]
    results[0] = (row, after, near, *kept)
    branches = [lambda r=r: finish(shard_rows, *r) for r in results]
    return lax.switch(jnp.where(even, 0, (far + 1) // 2), branches).T


def solution(mesh):
    seq, chan = mesh.devices.shape
    mesh = Mesh(mesh.devices.reshape(seq // NEAR, NEAR, chan), ("far", "near", "chan"))
    whole = ("far", "near")
    in_specs = (
        P(whole, "chan"),
        P("chan", None, None),
        P(None, None, "chan"),
        P("chan", None),
        P("chan", None),
        P("chan"),
    )
    return jax.shard_map(
        per_device, mesh=mesh, in_specs=in_specs, out_specs=P(whole, "chan"), check_vma=False
    )
```

```python
import functools

import jax
import jax.numpy as jnp
from jax import lax
from jax.experimental import pallas as pl
from jax.experimental.pallas import tpu as pltpu
from jax.sharding import Mesh, PartitionSpec as P

NEAR = 16
STEP = 8
F32 = jnp.float32
HBM = pl.BlockSpec(memory_space=pl.ANY)
ROOMY = pltpu.CompilerParams(vmem_limit_bytes=24 * 2**20)


def in_vmem(array):
    return pltpu.with_memory_space_constraint(array, pltpu.VMEM)


def in_hbm(array):
    return pltpu.with_memory_space_constraint(array, pltpu.HBM)


def lanes_of(shape):
    return lax.broadcasted_iota(jnp.int32, shape, 1)


def rows_of(shape):
    return lax.broadcasted_iota(jnp.int32, shape, 0)


def swap(tile):
    return pltpu.roll(tile, tile.shape[1] // 2, 1)


def twice(row):
    return jnp.concatenate([row, row], axis=1)


def folded(poles):
    half = poles.shape[0] // 2
    return jnp.concatenate([poles[:half], poles[half:]], axis=1)


def project_kernel(tok_hbm, w_hbm, out_ref, tok_ref, w_ref, acc_ref, sems):
    streams, depth, _ = w_ref.shape
    pieces = sems.shape[0]
    deep = depth // pieces
    parts = [pl.ds(i * deep, deep) for i in range(pieces)]
    copies = []
    for i, part in enumerate(parts):
        copies.append([pltpu.make_async_copy(tok_hbm.at[:, part], tok_ref.at[:, part], sems.at[i, streams])])
        for s in range(streams):
            copies[i].append(pltpu.make_async_copy(w_hbm.at[s, part], w_ref.at[s, part], sems.at[i, s]))
    for piece in copies:
        for copy in piece:
            copy.start()
    for i, part in enumerate(parts):
        for copy in copies[i]:
            copy.wait()
        for s in range(streams):
            term = jnp.dot(tok_ref[:, part], w_ref[s, part, :], preferred_element_type=F32)
            acc_ref[s] = term if i == 0 else acc_ref[s] + term
    rows = acc_ref.shape[1] // 2
    for s in range(streams):
        for pair in range(acc_ref.shape[2] // 128):
            early = acc_ref[s, :rows, 128 * pair : 128 * (pair + 1)]
            late = acc_ref[s, rows:, 128 * pair : 128 * (pair + 1)]
            left = lanes_of(early.shape) < 64
            out_ref[2 * pair, s] = jnp.where(left, early, swap(late))
            out_ref[2 * pair + 1, s] = jnp.where(left, swap(early), late)


def project(tokens, weight):
    rows, depth = tokens.shape
    streams, _, width = weight.shape
    chan = width // 64
    pieces = 4
    return pl.pallas_call(
        project_kernel,
        in_specs=[HBM, HBM],
        out_shape=pltpu.VMEM((chan, streams, rows // 2, 128), F32),
        scratch_shapes=[
            pltpu.VMEM(tokens.shape, tokens.dtype),
            pltpu.VMEM(weight.shape, weight.dtype),
            pltpu.VMEM((streams, rows, width), F32),
            pltpu.SemaphoreType.DMA((pieces, streams + 1)),
        ],
        compiler_params=ROOMY,
        name="project",
    )(in_hbm(tokens), in_hbm(weight))


def local_kernel(part_ref, short_ref, residue_ref, rates_ref, skip_ref, send_ref, keep_ref):
    count = part_ref.shape[0]
    rows, width = part_ref.shape[2:]
    right = lanes_of((1, width)) >= width // 2
    row = rows_of((rows, width))
    feats, edges = [], []
    for s in range(3):
        p = part_ref[0, s]
        for i in range(1, count):
            p = p + part_ref[i, s]
        tap = [twice(short_ref[k, s : s + 1, :]) for k in range(3)]
        before = jnp.where(right, swap(p[rows - 8 :]), 0.0)
        one = jnp.where(row < 1, before[7:8], pltpu.roll(p, 1, 0))
        two = pltpu.roll(p, 2, 0)
        two = jnp.where(row == 0, before[6:7], jnp.where(row == 1, before[7:8], two))
        feats.append(tap[0] * p + tap[1] * one + tap[2] * two)
        edges.append((tap[1] * p[rows - 1 :] + tap[2] * p[rows - 2 : rows - 1], tap[2] * p[rows - 1 :]))
    q, a, b = feats
    keep_ref[0:rows, :] = q
    x = jnp.where(jnp.logical_and(row < 2, jnp.logical_not(right)), 0.0, a * b)
    keep_ref[rows : 2 * rows, :] = x
    tile = [
        jnp.where(right, swap(b[0:1]), a[0:1]),
        jnp.where(right, swap(b[1:2]), a[1:2]),
        jnp.where(right, edges[2][0], swap(edges[1][0])),
        jnp.where(right, edges[2][1], swap(edges[1][1])),
        jnp.where(right, edges[0][1], swap(edges[0][0])),
    ]
    own = jnp.concatenate(tile + [jnp.zeros((3, width), F32)], axis=0)
    keep_ref[2 * rows : 2 * rows + 8, :] = own

    rates = twice(rates_ref[...])
    weight = twice(residue_ref[...]) * jnp.sqrt(2.0 * rates)
    poles = rates.shape[0]
    at = 2 * rows + 8 + poles
    keep_ref[at : at + poles, :] = rates
    keep_ref[at + poles : at + 2 * poles, :] = weight
    keep_ref[at + 2 * poles :, :] = jnp.broadcast_to(twice(skip_ref[...]), (8, width))
    step_pos = rows_of((STEP, width)).astype(F32)
    decay = jnp.exp(-float(STEP) * rates)
    half = []
    for r in range(poles):
        sums = x[:STEP]
        for k in range(1, rows // STEP):
            sums = sums * decay[r : r + 1] + x[k * STEP : (k + 1) * STEP]
        into = jnp.exp(-rates[r : r + 1] * (STEP - 1.0 - step_pos))
        half.append(jnp.sum(into * sums, axis=0, keepdims=True))
    half = jnp.concatenate(half, axis=0)
    keep_ref[2 * rows + 8 : at, :] = half
    total = half + jnp.exp(-float(rows) * rates) * swap(half)
    h = poles // 2
    packed = jnp.where(right, total[h:], swap(total[:h]))
    for i in range(send_ref.shape[0]):
        send_ref[i, 0:8, :] = packed
        send_ref[i, 8:16, :] = own


def within_kernel(keep_ref, *outs):
    *kept_refs, y_ref = outs
    for ref in kept_refs:
        ref[...] = keep_ref[...]
    rows, width = y_ref.shape
    poles = (keep_ref.shape[0] - 2 * rows - 16) // 3
    at = 2 * rows + 8 + poles
    rates = keep_ref[at : at + poles, :]
    weight = keep_ref[at + poles : at + 2 * poles, :]
    inner = rows_of((STEP, width))
    step_pos = inner.astype(F32)
    impulse = [jnp.sum(weight * jnp.exp(-rates * float(u)), axis=0, keepdims=True) for u in range(STEP)]
    near = [jnp.where(inner >= u, impulse[u], 0.0) for u in range(STEP)]
    decay = jnp.exp(-float(STEP) * rates)
    into, outof, fade = [], [], []
    for r in range(poles):
        rate = rates[r : r + 1]
        into.append(jnp.exp(-rate * (STEP - 1.0 - step_pos)))
        outof.append(weight[r : r + 1] * jnp.exp(-rate * (step_pos + 1.0)))
        fade.append(decay[r : r + 1])
    state = [None] * poles
    for k in range(rows // STEP):
        xk = keep_ref[rows + k * STEP : rows + (k + 1) * STEP, :]
        yk = near[0] * xk
        for u in range(1, STEP):
            yk = yk + near[u] * pltpu.roll(xk, u, 0)
        for r in range(poles):
            gain = jnp.sum(into[r] * xk, axis=0, keepdims=True)
            if k > 0:
                yk = yk + outof[r] * state[r]
                gain = gain + fade[r] * state[r]
            state[r] = gain
        y_ref[k * STEP : (k + 1) * STEP, :] = yk


def within(keep, rows, both):
    outs = (pltpu.VMEM(keep.shape, F32),) * both + (pltpu.VMEM((rows, keep.shape[1]), F32),)
    return pl.pallas_call(within_kernel, out_shape=outs, compiler_params=ROOMY, name="within")(in_vmem(keep))


def local(parts, short_weight, residue, rates, skip):
    _, _, rows, width = parts.shape
    return pl.pallas_call(
        local_kernel,
        out_shape=(
            pltpu.VMEM((NEAR, 16, width), F32),
            pltpu.VMEM((2 * rows + 16 + 3 * rates.shape[0], width), F32),
        ),
        compiler_params=ROOMY,
        name="local",
    )(in_vmem(parts), in_vmem(short_weight), in_vmem(residue), in_vmem(rates), in_vmem(skip))


def gate_of(tile, before):
    a = tile[0:2]
    if before is not None:
        a = a + before[2:4]
    return a * swap(a)


def near_kernel(shard_rows, got_ref, rates_ref, send_ref, keep_ref):
    near = lax.axis_index("near")
    rates = folded(rates_ref[...])
    fade = jnp.exp(-float(shard_rows) * rates)
    first = jnp.exp(-(shard_rows - 1.0) * rates)
    second = jnp.exp(-(shard_rows - 2.0) * rates)
    total = got_ref[0, 0:8, :]
    prefix = jnp.where(near > 0, total, 0.0)
    before = jnp.zeros_like(total)
    for i in range(1, NEAR):
        edge = got_ref[i - 1, 8:16, :]
        gate = gate_of(got_ref[i, 8:16, :], edge)
        grown = total * fade + (got_ref[i, 0:8, :] + first * gate[0:1] + second * gate[1:2])
        before = jnp.where(near == i, edge, before)
        total = grown
        prefix = jnp.where(near > i, grown, prefix)
    keep_ref[0:8, :] = prefix
    keep_ref[8:16, :] = before
    keep_ref[16:24, :] = rates
    head = got_ref[0, 8:16, :]
    tail = got_ref[NEAR - 1, 8:16, :]
    ends = jnp.where(rows_of(head.shape) < 2, head, tail)
    send_ref[0:8, :] = total
    send_ref[8:16, :] = ends


def near_sums(got, rates, shard_rows):
    width = got.shape[2]
    return pl.pallas_call(
        functools.partial(near_kernel, shard_rows),
        out_shape=(pltpu.VMEM((16, width), F32), pltpu.VMEM((24, width), F32)),
        compiler_params=ROOMY,
        name="near_sums",
    )(in_vmem(got), in_vmem(rates))


def with_row(shard_rows, row, got, rates):
    gate = gate_of(row[8:16], got[8:16])
    start = jnp.exp(-(shard_rows - 1.0) * rates) * gate[0:1] + jnp.exp(-(shard_rows - 2.0) * rates) * gate[1:2]
    state = row[0:8] + jnp.exp(-float((NEAR - 1) * shard_rows) * rates) * start
    state = state + jnp.exp(-float(NEAR * shard_rows) * rates) * got[0:8]
    return jnp.concatenate([state, row[8:16]], axis=0)


def first_kernel(shard_rows, row_ref, near_ref, total_ref):
    total_ref[...] = with_row(shard_rows, row_ref[...], jnp.zeros(row_ref.shape, F32), near_ref[16:24, :])


def first_sum(shard_rows, row, near):
    return pl.pallas_call(
        functools.partial(first_kernel, shard_rows),
        out_shape=pltpu.VMEM(row.shape, F32),
        compiler_params=ROOMY,
        name="first_sum",
    )(in_vmem(row), in_vmem(near))


def hop_kernel(shard_rows, sums, sources, *refs):
    kept = (len(refs) - sources - sums - 1) // 2
    rows_before, work_refs, refs = refs[:sources], refs[sources : sources + kept], refs[sources + kept :]
    sum_refs, before_ref, work_outs = refs[:sums], refs[sums], refs[sums + 1 :]
    row_ref, near_ref = work_refs[:2]
    rates = near_ref[16:24, :]
    before = rows_before[0][...]
    if sources > 1:
        before = with_row(shard_rows, rows_before[1][...], before, rates)
    before_ref[...] = before
    if sums:
        total = with_row(shard_rows, row_ref[...], before, rates)
    for ref in sum_refs:
        ref[...] = total
    for ref, out in zip(work_refs, work_outs):
        out[...] = ref[...]


def hop(shard_rows, sums, sources, row, *rest):
    operands = [in_vmem(a) for a in (*sources, row, *rest)]
    outs = (row,) * (sums + 2) + rest
    return pl.pallas_call(
        functools.partial(hop_kernel, shard_rows, sums, len(sources)),
        out_shape=tuple(pltpu.VMEM(a.shape, F32) for a in outs),
        compiler_params=ROOMY,
        name="hop",
    )(*operands)


def finish_kernel(shard_rows, row_ref, got_ref, near_ref, keep_ref, y_ref, out_ref):
    near = lax.axis_index("near")
    rows, width = out_ref.shape[1] // 2, keep_ref.shape[1]
    poles = 2 * near_ref[16:24, :].shape[0]
    at = 2 * rows + 8 + poles
    rates = keep_ref[at : at + poles, :]
    weight = keep_ref[at + poles : at + 2 * poles, :]
    skip = keep_ref[at + 2 * poles : at + 2 * poles + 1, :]
    step_pos = rows_of((STEP, width)).astype(F32)
    decay = jnp.exp(-float(STEP) * rates)
    half_decay = jnp.exp(-float(rows) * rates)
    ahead = jnp.sum(weight * jnp.exp(rates), axis=0, keepdims=True)
    outof, fade = [], []
    for r in range(poles):
        outof.append(weight[r : r + 1] * jnp.exp(-rates[r : r + 1] * (step_pos + 1.0)))
        fade.append(jnp.broadcast_to(decay[r : r + 1], (STEP, width)))

    rates = near_ref[16:24, :]
    first = jnp.exp(-(shard_rows - 1.0) * rates)
    second = jnp.exp(-(shard_rows - 2.0) * rates)
    place = near.astype(F32) * float(shard_rows)
    place_fade = jnp.exp(-place * rates)
    beyond_fade = jnp.where(near > 0, jnp.exp(-jnp.maximum(place - shard_rows, 0.0) * rates), 0.0)
    ahead_one, ahead_two = jnp.exp(rates), jnp.exp(2.0 * rates)
    edge = got_ref[8:16, :]
    before = jnp.where(near == 0, edge, near_ref[8:16, :])
    gate = gate_of(row_ref[8:16, :], edge)
    opening = first * gate[0:1] + second * gate[1:2]
    carry = got_ref[0:8, :]
    state = near_ref[0:8, :] + place_fade * carry + beyond_fade * opening
    gate = gate_of(keep_ref[2 * rows : 2 * rows + 8, :], before)
    state = state + ahead_one * gate[0:1] + ahead_two * gate[1:2]

    left = lanes_of((1, width)) < width // 2
    other = swap(state)
    whole = jnp.concatenate([jnp.where(left, state, other), jnp.where(left, other, state)], axis=0)
    whole = jnp.where(left, whole, swap(keep_ref[2 * rows + 8 : 2 * rows + 8 + poles, :]) + half_decay * whole)
    states = [jnp.broadcast_to(whole[r : r + 1], (STEP, width)) * outof[r] for r in range(poles)]
    steps = []
    for k in range(rows // STEP):
        at = k * STEP
        qk = keep_ref[at : at + STEP, :]
        xk = keep_ref[rows + at : rows + at + STEP, :]
        yk = y_ref[at : at + STEP, :]
        if k == 0:
            inner = rows_of((STEP, width))
            top = jnp.logical_and(left, inner == 0)
            next_ = jnp.logical_and(left, inner == 1)
            xk = jnp.where(top, gate[0:1], jnp.where(next_, gate[1:2], xk))
            yk = yk - jnp.where(top, ahead * gate[1:2], 0.0)
            q_edge = before[4:5]
            qk = qk + jnp.where(top, q_edge, jnp.where(next_, swap(q_edge), 0.0))
        for r in range(poles):
            yk = yk + states[r]
            states[r] = states[r] * fade[r]
        steps.append(qk * (yk + skip * xk))
    mixed = jnp.concatenate(steps, axis=0).T
    out_ref[:, :rows] = mixed[: width // 2].astype(out_ref.dtype)
    out_ref[:, rows:] = mixed[width // 2 :].astype(out_ref.dtype)


def finish(shard_rows, row, got, near, keep, y=None):
    width = keep.shape[1]
    if y is None:
        (y,) = within(keep, shard_rows // 2, False)
    return pl.pallas_call(
        functools.partial(finish_kernel, shard_rows),
        out_shape=jax.ShapeDtypeStruct((width // 2, shard_rows), jnp.bfloat16),
        compiler_params=ROOMY,
        name="finish",
    )(in_vmem(row), in_vmem(got), in_vmem(near), in_vmem(keep), in_vmem(y))


def nothing(*shapes):
    return pl.pallas_call(
        lambda *refs: None,
        out_shape=tuple(pltpu.VMEM(shape, F32) for shape in shapes),
        name="nothing",
    )()


def crossed(source, target):
    return [(source * NEAR + i, target * NEAR + (i ^ 1)) for i in range(NEAR)]


def per_device(tokens, in_weight, short_weight, residue, rates, skip):
    shard_rows = tokens.shape[0]
    residue, rates, skip = residue.T, rates.T, skip[None, :]
    weight = in_weight.transpose(1, 0, 2)
    far, far_count = lax.axis_index("far"), lax.axis_size("far")

    def row_of_shards(full):
        parts = lax.all_to_all(project(tokens, weight), "chan", 0, 0, tiled=True)
        send, keep = local(parts, short_weight, residue, rates, skip)
        row, near = near_sums(lax.all_to_all(send, "near", 0, 0, tiled=True), rates, shard_rows)
        if not full:
            return row, near, keep
        row, keep = lax.optimization_barrier((row, keep))
        return row, near, *within(keep, shard_rows // 2, True)

    shapes = [a.shape for a in jax.eval_shape(lambda: row_of_shards(True))]

    def work_of(mine, full=True):
        return lax.cond(mine, lambda: row_of_shards(full), lambda: nothing(*shapes[: 3 + full]))

    none = jnp.zeros(shapes[0], F32)
    even = far % 2 == 0
    row, near, keep = work_of(even, False)
    total = first_sum(shard_rows, row, near)
    after = none
    results = [None]
    for k in range(1, far_count, 2):
        sums = int(k + 1 < far_count)
        full = k != 3

        two = jnp.where(far == k - 1, row, total)

        def odd_row(k=k, total=total, two=two, sums=sums, full=full):
            final = k + 1 == far_count
            block = total if final else jnp.where(far == max(k - 2, 0), total, none)
            sources = [lax.ppermute(block, ("far", "near"), crossed(max(k - 2, 0), k))]
            extra = []
            if k > 1:
                steps = crossed(k - 2, k - 1) + crossed(k - 1, k)
                both = jnp.where(far == k - 1, row, total) if final else two
                extra = [lax.ppermute(both, ("far", "near"), steps)]
                sources += extra
            return hop(shard_rows, sums, sources, *work_of(far == k, full), *extra)

        here = jnp.logical_and(far <= k, far >= k - 2)
        outs = shapes[:1] * (sums + 1) + shapes[: 3 + full] + shapes[:1] * (k > 1)
        out = lax.cond(here, odd_row, lambda outs=outs: nothing(*outs))
        results.append((out[sums + 1], out[sums], *out[sums + 2 : sums + 4 + full]))
        if k > 1:
            after = jnp.where(far == k - 1, out[-1], after)
        if k == 3:
            keep, *out = lax.optimization_barrier((keep, *out))
            kept = lax.cond(
                even, lambda: within(keep, shard_rows // 2, True), lambda: nothing(shapes[2], shapes[3])
            )
            *out, kept0, kept1 = lax.optimization_barrier((*out, *kept))
            kept = (kept0, kept1)
        total = out[0]
    results[0] = (row, after, near, *kept)
    branches = [lambda r=r: finish(shard_rows, *r) for r in results]
    return lax.switch(jnp.where(even, 0, (far + 1) // 2), branches).T


def solution(mesh):
    seq, chan = mesh.devices.shape
    mesh = Mesh(mesh.devices.reshape(seq // NEAR, NEAR, chan), ("far", "near", "chan"))
    whole = ("far", "near")
    in_specs = (
        P(whole, "chan"),
        P("chan", None, None),
        P(None, None, "chan"),
        P("chan", None),
        P("chan", None),
        P("chan"),
    )
    return jax.shard_map(
        per_device, mesh=mesh, in_specs=in_specs, out_specs=P(whole, "chan"), check_vma=False
    )
```
